32 devices in a mesh: dp: 8 (over y, x, core), tensor: 4 (over z).
Axes of the slice: x: 2, y: 2, z: 4, core: 2. Of those that a mesh axis runs over, the one named last changes fastest.
Arguments:
- tokens_in: bfloat16 [16, 1536, 1280], P('dp', 'tensor'), may hold values from -6 to 6
- cotangent: bfloat16 [16, 1536, 1280], P('dp', 'tensor'), may hold values from -6 to 6
- picture_ids: int32 [16, 1536], P('dp', 'tensor'), may hold values from 0 to 3, as said below
- patch_positions: int32 [2, 16, 1536], P(None, 'dp', 'tensor'), may hold values from 0 to 511, as said below
- qkv_weight: float32 [1280, 3, 1280], P('dp', None, 'tensor'), may hold values from -0.15625 to 0.15625
- out_weight: float32 [1280, 1280], P('tensor', 'dp'), may hold values from -0.75 to 0.75
- up_projection_weight: float32 [1280, 4, 1280], P('dp', None, 'tensor'), may hold values from -0.15625 to 0.15625
- down_weight: float32 [4, 1280, 1280], P(None, 'tensor', 'dp'), may hold values from -0.078125 to 0.078125
- projection_bias_rows: float32 [7, 1280], P(None, 'tensor'), may hold values from -1.8 to 1.8
- norm_vectors: float32 [6, 1280], replicated
- qkv_first: float32 [1280, 3, 1280], P('dp', None, 'tensor'), may hold values from -104.40705 to 104.40705
- out_first: float32 [1280, 1280], P('tensor', 'dp'), may hold values from -20.850058 to 20.850058
- up_first: float32 [1280, 4, 1280], P('dp', None, 'tensor'), may hold values from -31.353468 to 31.353468
- down_first: float32 [4, 1280, 1280], P(None, 'tensor', 'dp'), may hold values from -52.203526 to 52.203526
- bias_first: float32 [7, 1280], P(None, 'tensor'), may hold values from -62.706936 to 62.706936
- vector_first: float32 [6, 1280], replicated, may hold values from -104.40705 to 104.40705
- qkv_second: float32 [1280, 3, 1280], P('dp', None, 'tensor'), may hold values from 1292.6976 to 5160.96
- out_second: float32 [1280, 1280], P('tensor', 'dp'), may hold values from 51.6096 to 206.4384
- up_second: float32 [1280, 4, 1280], P('dp', None, 'tensor'), may hold values from 115.5072 to 466.944
- down_second: float32 [4, 1280, 1280], P(None, 'tensor', 'dp'), may hold values from 324.4032 to 1292.6976
- bias_second: float32 [7, 1280], P(None, 'tensor'), may hold values from 466.944 to 1867.776
- vector_second: float32 [6, 1280], replicated, may hold values from 1292.6976 to 5160.96
Outputs:
- block_out: bfloat16 [16, 1536, 1280], P('dp', 'tensor')
- input_grad: float32 [16, 1536, 1280], P('dp', 'tensor')
- qkv_new: float32 [1280, 3, 1280], P('dp', None, 'tensor')
- qkv_first_new: float32 [1280, 3, 1280], P('dp', None, 'tensor')
- qkv_second_new: float32 [1280, 3, 1280], P('dp', None, 'tensor')
- out_new: float32 [1280, 1280], P('tensor', 'dp')
- out_first_new: float32 [1280, 1280], P('tensor', 'dp')
- out_second_new: float32 [1280, 1280], P('tensor', 'dp')
- up_new: float32 [1280, 4, 1280], P('dp', None, 'tensor')
- up_first_new: float32 [1280, 4, 1280], P('dp', None, 'tensor')
- up_second_new: float32 [1280, 4, 1280], P('dp', None, 'tensor')
- down_new: float32 [4, 1280, 1280], P(None, 'tensor', 'dp')
- down_first_new: float32 [4, 1280, 1280], P(None, 'tensor', 'dp')
- down_second_new: float32 [4, 1280, 1280], P(None, 'tensor', 'dp')
- bias_new: float32 [7, 1280], P(None, 'tensor')
- bias_first_new: float32 [7, 1280], P(None, 'tensor')
- bias_second_new: float32 [7, 1280], P(None, 'tensor')
- vector_new: float32 [6, 1280], replicated
- vector_first_new: float32 [6, 1280], replicated
- vector_second_new: float32 [6, 1280], replicated
The draws below stay inside these ranges and needn't reach their ends.
Inputs may be any that keep to these rules, and one draw needn't show every extreme that they name: `picture_ids`: each row holds three pictures numbered 1, 2, 3 one after another from its first slot, then padding numbered 0; picture 2 has exactly 1024 patches, pictures 1 and 3 at least 102. `patch_positions`: patch i of a picture of grid width w lies at row i // w and column i % w; each picture has its own width, from 2 to 33, and picture 2 of the first packed row has width 2; padding lies at 0, 0.
All inputs are finite; a program needn't handle non-finite values.
Results may differ from the reference program's by a relative error of at most 0.015.
Values may be sent and summed in bfloat16 or wider, within the bound.
No kernel may reach another device: no remote copies, remote signals or barrier semaphores. Data moves between devices by JAX's collectives and lax.ppermute only.
A program may use at most 256 MiB of HBM per device.

```python
import math
from functools import reduce
import jax
import jax.numpy as jnp
from jax import lax

D = 1280
HEAD = 80
FF = 5120
ROW = 1536
STEP = 10
ROWS = 16
TOKENS = 24576
N_TENSOR = 4


def picture_layout(key):
    first_key, third_key, width_key = jax.random.split(key, 3)
    first_len = jax.random.randint(first_key, (ROWS, 1), ROW // 12, ROW // 4)
    third_len = jax.random.randint(third_key, (ROWS, 1), ROW // 15, ROW // 3 - first_len + 1)
    widths = jax.random.randint(width_key, (ROWS, 4), 2, 2 + ROW // 48)
    widths = widths.at[0, 2].set(2)
    middle_end = first_len + 2 * ROW // 3
    third_end = middle_end + third_len
    places = jnp.arange(ROW, dtype=jnp.int32)[None, :]
    numbers = jnp.where(places < first_len, 1, jnp.where(places < middle_end, 2, jnp.where(places < third_end, 3, 0)))
    numbers = numbers.astype(jnp.int32)
    starts = jnp.where(numbers == 2, first_len, jnp.where(numbers == 3, middle_end, 0))
    chosen = jnp.take_along_axis(widths, numbers, axis=1)
    within = places - starts
    grid_row = jnp.where(numbers > 0, within // chosen, 0)
    grid_col = jnp.where(numbers > 0, within % chosen, 0)
    return (numbers, jnp.stack([grid_row, grid_col]).astype(jnp.int32))


def draw_picture_ids(key, part):
    return picture_layout(key)[0]


def draw_patch_positions(key, part):
    return picture_layout(key)[1]


def draw_norm_vectors(key, part):
    key = jax.random.fold_in(key, 7)
    gain_key, shift_key = jax.random.split(key)
    gain_rows = jax.random.uniform(gain_key, (6, D), jnp.float32, 0.5, 1.5)
    shifts = 0.3 * jax.random.normal(shift_key, (6, D), jnp.float32)
    row_index = jnp.arange(6)[:, None]
    is_gain = (row_index == 0) | (row_index == 2)
    return jnp.where(is_gain, gain_rows, shifts)


def block_levels(key, extent, pieces, least, top_value):
    level, own = 1.0, jax.random.fold_in(key, 6)
    for dim, parts in pieces:
        steps = jnp.exp(jax.random.uniform(jax.random.fold_in(own, dim), (parts,), jnp.float32, least / len(pieces), top_value / len(pieces)))
        level = level * jnp.repeat(steps, extent[dim] // parts).reshape([-1 if axis == dim else 1 for axis in range(len(extent))])
    return level


def noise(key, shape, scale, most, cuts=(), kind=jnp.bfloat16):
    values = scale * jax.random.normal(key, shape, jnp.float32)
    if cuts:
        values = values * block_levels(key, shape, cuts, -0.22, 0.18)
    return jnp.clip(values, -most, most).astype(kind)


def setup_inputs(seed: int = 0) -> dict:
    key_list = jax.random.split(jax.random.key(seed), 23)
    return {
        "tokens_in": noise(key_list[0], (ROWS, ROW, D), 1.0, 6.0, ((0, 8), (1, 4))),
        "cotangent": noise(key_list[1], (ROWS, ROW, D), 1.0, 6.0, ((0, 8), (1, 4))),
        "picture_ids": draw_picture_ids(jax.random.fold_in(key_list[22], 71), 0),
        "patch_positions": draw_patch_positions(jax.random.fold_in(key_list[22], 71), 0),
        "qkv_weight": noise(key_list[4], (D, 3, D), D ** -0.5, 0.15625, ((0, 8), (2, 4)), jnp.float32),
        "out_weight": noise(key_list[5], (D, D), (D // 20) ** -0.5, 0.75, ((0, 4), (1, 8)), jnp.float32),
        "up_projection_weight": noise(key_list[6], (D, FF // D, D), D ** -0.5, 0.15625, ((0, 8), (2, 4)), jnp.float32),
        "down_weight": noise(key_list[7], (FF // D, D, D), FF ** -0.5, 0.078125, ((1, 4), (2, 8)), jnp.float32),
        "projection_bias_rows": noise(key_list[8], (7, D), 0.3, 1.8, ((1, 4),), jnp.float32),
        "norm_vectors": draw_norm_vectors(jax.random.fold_in(key_list[22], 71), 0),
        "qkv_first": noise(key_list[10], (D, 3, D), (0.111 * TOKENS ** 0.5), 104.40705, ((0, 8), (2, 4)), jnp.float32),
        "out_first": noise(key_list[11], (D, D), (0.0222 * TOKENS ** 0.5), 20.850058, ((0, 4), (1, 8)), jnp.float32),
        "up_first": noise(key_list[12], (D, FF // D, D), (0.0333 * TOKENS ** 0.5), 31.353468, ((0, 8), (2, 4)), jnp.float32),
        "down_first": noise(key_list[13], (FF // D, D, D), (0.0555 * TOKENS ** 0.5), 52.203526, ((1, 4), (2, 8)), jnp.float32),
        "bias_first": noise(key_list[14], (7, D), (0.0666 * TOKENS ** 0.5), 62.706936, ((1, 4),), jnp.float32),
        "vector_first": noise(key_list[15], (6, D), (0.111 * TOKENS ** 0.5), 104.40705, (), jnp.float32),
        "qkv_second": jnp.clip(jnp.exp(math.log(5160.96) - 1.3843914 * jax.random.uniform(key_list[16], (D, 3, D), jnp.float32) ** block_levels(key_list[16], (D, 3, D), ((0, 8), (2, 4)), -0.2, 0.2)), 1292.6976, 5160.96),
        "out_second": jnp.clip(jnp.exp(math.log(206.4384) - 1.3862944 * jax.random.uniform(key_list[17], (D, D), jnp.float32) ** block_levels(key_list[17], (D, D), ((0, 4), (1, 8)), -0.2, 0.2)), 51.6096, 206.4384),
        "up_second": jnp.clip(jnp.exp(math.log(466.944) - 1.3968765 * jax.random.uniform(key_list[18], (D, FF // D, D), jnp.float32) ** block_levels(key_list[18], (D, FF // D, D), ((0, 8), (2, 4)), -0.2, 0.2)), 115.5072, 466.944),
        "down_second": jnp.clip(jnp.exp(math.log(1292.6976) - 1.3824993 * jax.random.uniform(key_list[19], (FF // D, D, D), jnp.float32) ** block_levels(key_list[19], (FF // D, D, D), ((1, 4), (2, 8)), -0.2, 0.2)), 324.4032, 1292.6976),
        "bias_second": jnp.clip(jnp.exp(math.log(1867.776) - 1.3862944 * jax.random.uniform(key_list[20], (7, D), jnp.float32) ** block_levels(key_list[20], (7, D), ((1, 4),), -0.2, 0.2)), 466.944, 1867.776),
        "vector_second": jnp.clip(jnp.exp(jax.random.uniform(key_list[21], (6, D), jnp.float32, math.log(1292.6976), math.log(5160.96))), 1292.6976, 5160.96),
    }


@jax.custom_vjp
def reduced_precision(v):
    return lax.optimization_barrier(v.astype(jnp.bfloat16)).astype(jnp.float32)

@jax.custom_vjp
def low_back(v):
    return v

def low_keep(v):
    return (reduced_precision(v), None)

def low_pass(kept, grad):
    return (grad,)

def back_keep(v):
    return (v, None)

def back_low(kept, grad):
    return (reduced_precision(grad),)
reduced_precision.defvjp(low_keep, low_pass)
low_back.defvjp(back_keep, back_low)
NORM_EPS = 1e-06
BETA_ONE = 0.9
BETA_TWO = 0.95
ADAM_EPS = 1e-08
MATRIX_RATE = 0.03
VECTOR_RATE = 0.2
MATRIX_DECAY = 0.1
GELU_SLOPE = 1.702

def layer_norm(source, gain_vec, offset_vec):
    centre = source - lax.optimization_barrier(jnp.mean(source, axis=-1, keepdims=True))
    spread = lax.rsqrt(lax.optimization_barrier(jnp.mean(centre * centre, axis=-1, keepdims=True)) + NORM_EPS)
    return centre * spread * gain_vec + offset_vec

def rotary_tables(positions):
    quarter = HEAD // 4
    powers = jnp.arange(quarter, dtype=jnp.float32) * (2.0 / (HEAD // 2))
    inverse = jnp.power(10000.0, -powers)
    angles = jnp.concatenate([positions[0].astype(jnp.float32)[:, None] * inverse, positions[1].astype(jnp.float32)[:, None] * inverse], axis=-1)
    angles = jnp.concatenate([angles, angles], axis=-1)
    return (jnp.cos(angles)[:, None, :], jnp.sin(angles)[:, None, :])

def turn(values, cosine, sine):
    half_size = values.shape[-1] // 2
    swapped = jnp.concatenate([-values[..., half_size:], values[..., :half_size]], axis=-1)
    return values * cosine + swapped * sine

def quick_gelu(values):
    return values * jax.nn.sigmoid(GELU_SLOPE * values)

def adam_step(weight, gradient, first, second, rate, decay):
    first_new = BETA_ONE * first + (1.0 - BETA_ONE) * gradient
    second_new = BETA_TWO * second + (1.0 - BETA_TWO) * gradient * gradient
    fix_one = 1.0 - BETA_ONE ** STEP
    fix_two = 1.0 - BETA_TWO ** STEP
    ratio = first_new / fix_one / (jnp.sqrt(second_new / fix_two) + ADAM_EPS)
    return (weight - rate * (ratio + decay * weight), first_new, second_new)

def block_row(row_in, picture_row, position_row, qkv_weight, out_weight, up_projection_weight, down_weight, projection_bias_rows, norm_vectors):
    highest_precision = lax.Precision.HIGHEST
    model_width = row_in.shape[-1]
    all_heads = model_width // HEAD
    slice_width = model_width // N_TENSOR
    first_in = reduced_precision(layer_norm(row_in, norm_vectors[0], norm_vectors[1]))
    mixed = jnp.einsum('td,dcf->tcf', first_in, reduced_precision(qkv_weight), precision=highest_precision) + projection_bias_rows[0:3][None]
    mixed = low_back(mixed)
    cosine, sine = rotary_tables(position_row)
    queries = reduced_precision(turn(mixed[:, 0].reshape(-1, all_heads, HEAD), cosine, sine))
    key_rows = reduced_precision(turn(mixed[:, 1].reshape(-1, all_heads, HEAD), cosine, sine))
    value_rows = reduced_precision(mixed[:, 2].reshape(-1, all_heads, HEAD))
    scores = low_back(jnp.einsum('qhe,khe->hqk', queries, key_rows, precision=highest_precision) * HEAD ** (-0.5))
    allowed = picture_row[:, None] == picture_row[None, :]
    scores = jnp.where(allowed[None], scores, -1e+30)
    largest = lax.optimization_barrier(jnp.max(scores, axis=-1, keepdims=True))
    raised = jnp.exp(scores - largest)
    chances = raised / lax.optimization_barrier(jnp.sum(raised, axis=-1, keepdims=True))
    attended = jnp.einsum('hqk,khe->qhe', reduced_precision(chances), value_rows, precision=highest_precision).reshape(-1, model_width)
    attended = reduced_precision(low_back(attended))
    out_low = reduced_precision(out_weight)
    pieces_one = []
    for group_index in range(N_TENSOR):
        lower_bound = group_index * slice_width
        upper_bound = lower_bound + slice_width
        pieces_one.append(reduced_precision(jnp.dot(attended[:, lower_bound:upper_bound], out_low[lower_bound:upper_bound], precision=highest_precision)))
    middle = row_in + low_back(reduce(jnp.add, pieces_one)) + norm_vectors[4]
    second_input = reduced_precision(layer_norm(middle, norm_vectors[2], norm_vectors[3]))
    hidden_units = jnp.einsum('sp,piv->siv', second_input, reduced_precision(up_projection_weight), precision=highest_precision) + projection_bias_rows[3:7][None]
    hidden_units = low_back(hidden_units)
    active_units = reduced_precision(quick_gelu(hidden_units))
    down_reduced = reduced_precision(down_weight)
    second_pieces = []
    for group_index in range(N_TENSOR):
        lower_bound = group_index * slice_width
        upper_bound = lower_bound + slice_width
        second_pieces.append(reduced_precision(jnp.einsum('ukx,kxq->uq', active_units[:, :, lower_bound:upper_bound], down_reduced[:, lower_bound:upper_bound], precision=highest_precision)))
    return middle + low_back(reduce(jnp.add, second_pieces)) + norm_vectors[5]

def reference(tokens_in, cotangent, picture_ids, patch_positions, qkv_weight, out_weight, up_projection_weight, down_weight, projection_bias_rows, norm_vectors, qkv_first, out_first, up_first, down_first, bias_first, vector_first, qkv_second, out_second, up_second, down_second, bias_second, vector_second):
    params = (qkv_weight, out_weight, up_projection_weight, down_weight, projection_bias_rows, norm_vectors)

    def one_row(totals, inputs):
        row_in, row_cot, picture_row, position_row = inputs

        def forward(source, *weights):
            return block_row(source, picture_row, position_row, *weights)
        result, pullback = jax.vjp(forward, row_in.astype(jnp.float32), *params)
        grads = pullback(row_cot.astype(jnp.float32))
        new_totals = tuple((left_one + right_one for left_one, right_one in zip(totals, grads[1:])))
        return (new_totals, (result.astype(jnp.bfloat16), grads[0]))
    zeros = tuple((jnp.zeros_like(weight) for weight in params))
    totals, outputs = lax.scan(one_row, zeros, (tokens_in, cotangent, picture_ids, jnp.moveaxis(patch_positions, 1, 0)))
    block_out, input_grad = outputs
    qkv_new, qkv_first_new, qkv_second_new = adam_step(qkv_weight, totals[0], qkv_first, qkv_second, MATRIX_RATE, MATRIX_DECAY)
    out_new, out_first_new, out_second_new = adam_step(out_weight, totals[1], out_first, out_second, MATRIX_RATE, MATRIX_DECAY)
    up_new, up_first_new, up_second_new = adam_step(up_projection_weight, totals[2], up_first, up_second, MATRIX_RATE, MATRIX_DECAY)
    down_new, down_first_new, down_second_new = adam_step(down_weight, totals[3], down_first, down_second, MATRIX_RATE, MATRIX_DECAY)
    bias_new, bias_first_new, bias_second_new = adam_step(projection_bias_rows, totals[4], bias_first, bias_second, VECTOR_RATE, 0.0)
    vector_new, vector_first_new, vector_second_new = adam_step(norm_vectors, totals[5], vector_first, vector_second, VECTOR_RATE, 0.0)
    return (block_out, input_grad, qkv_new, qkv_first_new, qkv_second_new, out_new, out_first_new, out_second_new, up_new, up_first_new, up_second_new, down_new, down_first_new, down_second_new, bias_new, bias_first_new, bias_second_new, vector_new, vector_first_new, vector_second_new)
```

```python
import functools

import jax
import jax.numpy as jnp
from jax import lax
from jax.experimental import pallas as pl
from jax.experimental.pallas import tpu as pltpu
from jax.sharding import Mesh, PartitionSpec as P

HEAD = 80
HALF = HEAD // 2
STEP = 10
MIDDLE = 1024

NORM_EPS = 1e-06
BETA_ONE = 0.9
BETA_TWO = 0.95
ADAM_EPS = 1e-08
MATRIX_RATE = 0.03
VECTOR_RATE = 0.2
MATRIX_DECAY = 0.1
GELU_SLOPE = 1.702
LOG2E = 1.4426950408889634
LN2 = 0.6931471805599453

BF = jnp.bfloat16
F32 = jnp.float32


def dot(left, right, left_dim, right_dim):
    return lax.dot_general(
        left, right, (((left_dim,), (right_dim,)), ((), ())), preferred_element_type=F32
    )


def normalise(source):
    centre = source - jnp.mean(source, axis=-1, keepdims=True)
    spread = lax.rsqrt(jnp.mean(centre * centre, axis=-1, keepdims=True) + NORM_EPS)
    return centre * spread, spread


def norm_back(gradient, gain_vec, normed, spread):
    scaled = gradient * gain_vec
    return spread * (
        scaled
        - jnp.mean(scaled, axis=-1, keepdims=True)
        - normed * jnp.mean(scaled * normed, axis=-1, keepdims=True)
    )


def adam_step(weight, gradient, first, second, rate, decay):
    first_new = BETA_ONE * first + (1.0 - BETA_ONE) * gradient
    second_new = BETA_TWO * second + (1.0 - BETA_TWO) * gradient * gradient
    fix_one = 1.0 - BETA_ONE**STEP
    fix_two = 1.0 - BETA_TWO**STEP
    ratio = first_new / fix_one / (jnp.sqrt(second_new / fix_two) + ADAM_EPS)
    return (weight - rate * (ratio + decay * weight), first_new, second_new)


NEAR = [(0, 1), (1, 0), (2, 3), (3, 2)]
MIDS = [(1, 2), (2, 1)]
OUTER = [(1, 0), (2, 3)]
INNER = [(0, 1), (3, 2)]


def after(value, *earlier):
    return lax.optimization_barrier((value, *earlier))[0]


def move(value, axis, pairs, *earlier):
    return lax.ppermute(after(value, *earlier) if earlier else value, axis, pairs)


def swap_core(value, *earlier):
    return move(value, "c", [(0, 1), (1, 0)], *earlier)


def swap_bit(value, bit, count, *earlier):
    return move(value, "g", [(i, i ^ (1 << bit)) for i in range(count)], *earlier)


class Gather:
    def __init__(self, block, order, g, count):
        self.rows, self.columns = block.shape
        self.order, self.g, self.count = list(order), g, count
        self.bits = len(self.order)
        self.current = block.reshape((1,) * self.bits + block.shape)

    def step(self, *earlier):
        if not self.order:
            return self.current
        bit = self.order.pop(0)
        other = swap_bit(self.current, bit, self.count, *earlier)
        axis = self.bits - 1 - bit
        upper = ((self.g >> bit) & 1) == 1
        mine = self.current
        self.current = jnp.concatenate(
            [jnp.where(upper, other, mine), jnp.where(upper, mine, other)], axis=axis
        )
        return other

    def finish(self, *earlier):
        last = self.step(*earlier)
        while self.order:
            last = self.step()
        return last

    def whole(self):
        return self.current.reshape(self.count * self.rows, self.columns)


def scatter_g(full, order, g, count, *earlier):
    bits = len(order)
    rows = full.shape[0] // count
    current = full.reshape((2,) * bits + (rows, full.shape[1]))
    for bit in order:
        axis = bits - 1 - bit
        mine = (g >> bit) & 1
        sent = lax.dynamic_slice_in_dim(current, 1 - mine, 1, axis).astype(BF)
        kept = lax.dynamic_slice_in_dim(current, mine, 1, axis)
        current = kept.astype(F32) + swap_bit(sent, bit, count, *earlier).astype(F32)
        earlier = ()
    return current.reshape(rows, full.shape[1])


def row_moves(step):
    moves = []
    for c in range(2):
        for z in range(4):
            place = z ^ step
            moves.append((c * 4 + z, (place >> 1) * 4 + 2 * c + (place & 1)))
    return moves


def rows_in(local, c, z, *earlier):
    _, size, width = local.shape
    part = size // 2
    pieces = []
    for step in range(4):
        place = z ^ step
        sent = lax.dynamic_slice(local, (place & 1, (place >> 1) * part, 0), (1, part, width))
        pieces.append(move(sent, ("c", "z"), row_moves(step), *earlier))
    own = jnp.concatenate(pieces, axis=0)
    both = jnp.stack([own, swap_core(own)])
    place = 2 * c + (z & 1)
    blocks = []
    for k in range(4):
        for h in range(2):
            which = h ^ c
            blocks.append(
                lax.dynamic_slice(both, (which, k ^ place ^ (2 * which), 0, 0), (1, 1, part, width)).reshape(
                    part, width
                )
            )
    return jnp.concatenate(blocks, axis=0)


def rows_out(turned, start, c, z, *earlier):
    rows, width = turned.shape
    part = rows // 8
    place = 2 * c + (z & 1)
    longer = jnp.concatenate([turned, turned[:part]], axis=0)
    pieces = []
    for step in range(4):
        k = place ^ step
        first = lax.rem(k * 2 * part + c * part - start + rows, rows)
        sent = lax.dynamic_slice(longer, (first, 0), (part, width))
        back = [(b, a) for a, b in row_moves(step)]
        pieces.append(move(sent, ("c", "z"), back, *earlier))
    stacked = jnp.stack(pieces)
    blocks = []
    for j in range(2):
        for h in range(2):
            blocks.append(
                lax.dynamic_slice(stacked, (z ^ (2 * h + j), 0, 0), (1, part, width)).reshape(part, width)
            )
    return jnp.concatenate(blocks, axis=0).reshape(2, 2 * part, width), pieces


def add_up(value, count):
    value = value + swap_core(value)
    for bit in range(count.bit_length() - 1):
        value = value + swap_bit(value, bit, count)
    for distance in (1, 2):
        value = value + lax.ppermute(value, "z", [(i, i ^ distance) for i in range(4)])
    return value


SEGMENTS = ((0, MIDDLE, False), (MIDDLE, None, True))


def attend_kernel(q_ref, k_ref, v_ref, cos_ref, sin_ref, mask_ref, qt_ref, kt_ref, vt_ref, ot_ref, lse_ref, *, block):
    cosine, sine = cos_ref[...], sin_ref[...]

    def turn(source, factor):
        first, second = source[:HALF], source[HALF:]
        return (
            jnp.concatenate([first * cosine - second * sine, second * cosine + first * sine], axis=0) * factor
        ).astype(BF)

    rows = q_ref.shape[1]
    qt = turn(q_ref[...], LOG2E * HEAD ** (-0.5))
    kt = turn(k_ref[...], 1.0)
    vt = v_ref[...].astype(BF)
    qt_ref[0] = qt
    kt_ref[0] = kt
    vt_ref[0] = vt
    for first, last, masked in ((0, MIDDLE, False), (MIDDLE, rows, True)):
        keys = kt[:, first:last]
        values = vt[:, first:last]
        for at in range(first, last, block):
            scores = dot(keys, qt[:, at : at + block], 0, 0)
            if masked:
                scores = scores + mask_ref[:, at - first : at - first + block]
            largest = jnp.max(scores, axis=0, keepdims=True)
            raised = jnp.exp2(scores - largest)
            total = jnp.sum(raised, axis=0, keepdims=True)
            mixed = dot(values, raised.astype(BF), 1, 0)
            ot_ref[:, at : at + block] = (mixed / total).astype(BF)
            lse_ref[0, :, at : at + block] = largest + jnp.log2(total)


def attend_back_kernel(qt_ref, kt_ref, vt_ref, ot_ref, dot_ref, lse_ref, cos_ref, sin_ref, mask_ref, dq_ref, dk_ref, dv_ref, *, block):
    cosine, sine = cos_ref[...], sin_ref[...]

    def turn_back(grad, factor):
        first, second = grad[:HALF] * factor, grad[HALF:] * factor
        return jnp.concatenate([first * cosine + second * sine, second * cosine - first * sine], axis=0).astype(BF)

    rows = cos_ref.shape[1]
    qt, kt, vt, dot_ = qt_ref[0], kt_ref[0], vt_ref[0], dot_ref[...]
    delta = jnp.sum(dot_.astype(F32) * ot_ref[...].astype(F32), axis=0, keepdims=True)
    lse = lse_ref[0]
    queries = qt.astype(F32).T.astype(BF)
    grads = dot_.astype(F32).T.astype(BF)
    dq_parts, dk_parts, dv_parts = [], [], []
    for first, last, masked in ((0, MIDDLE, False), (MIDDLE, rows, True)):
        keys = kt[:, first:last]
        values = vt[:, first:last]
        dk = dv = None
        for at in range(first, last, block):
            sl = slice(at, at + block)
            scores = dot(keys, qt[:, sl], 0, 0)
            if masked:
                scores = scores + mask_ref[:, at - first : at - first + block]
            chances = jnp.exp2(scores - lse[:, sl])
            grad_chances = dot(values, dot_[:, sl], 0, 0)
            grad_scores = (chances * (grad_chances - delta[:, sl])).astype(BF)
            dv_part = dot(chances.astype(BF), grads[sl], 1, 0)
            dk_part = dot(grad_scores, queries[sl], 1, 0)
            dv = dv_part if dv is None else dv + dv_part
            dk = dk_part if dk is None else dk + dk_part
            dq_parts.append(dot(keys, grad_scores, 1, 0))
        dk_parts.append(dk.T)
        dv_parts.append(dv.T)
    dq_ref[0] = turn_back(jnp.concatenate(dq_parts, axis=1), HEAD ** (-0.5))
    dk_ref[0] = turn_back(jnp.concatenate(dk_parts, axis=1), LN2)
    dv_ref[0] = jnp.concatenate(dv_parts, axis=1).astype(BF)


def attend(mixed, cosine, sine, mask):
    rows = mixed.shape[1]
    heads = 4
    once = lambda shape: pl.BlockSpec(shape, lambda h: (0, 0))
    part = lambda which: pl.BlockSpec((HEAD, rows), lambda h: ((h // 2) * 8 + 2 * which + h % 2, 0))
    each = pl.BlockSpec((1, HEAD, rows), lambda h: (h, 0, 0))
    return pl.pallas_call(
        functools.partial(attend_kernel, block=256),
        grid=(heads,),
        in_specs=[part(0), part(1), part(2), once(cosine.shape), once(sine.shape), once(mask.shape)],
        out_specs=[
            each,
            each,
            each,
            pl.BlockSpec((HEAD, rows), lambda h: (h, 0)),
            pl.BlockSpec((1, 1, rows), lambda h: (h, 0, 0)),
        ],
        out_shape=[jax.ShapeDtypeStruct((heads, HEAD, rows), BF)] * 3
        + [
            jax.ShapeDtypeStruct((heads * HEAD, rows), BF),
            jax.ShapeDtypeStruct((heads, 1, rows), F32),
        ],
        compiler_params=pltpu.CompilerParams(vmem_limit_bytes=40 * 2**20),
        cost_estimate=pl.CostEstimate(flops=heads * 4 * 1310720 * 256, bytes_accessed=16 * 2**20, transcendentals=heads * 1310720),
        name="attend",
    )(mixed, mixed, mixed, cosine, sine, mask)


def attend_back(saved, grad_mixed, cosine, sine, mask):
    qt, kt, vt, mixed, lse = saved
    heads, _, rows = qt.shape
    once = lambda shape: pl.BlockSpec(shape, lambda h: (0, 0))
    each = pl.BlockSpec((1, HEAD, rows), lambda h: (h, 0, 0))
    flat = pl.BlockSpec((HEAD, rows), lambda h: (h, 0))
    return pl.pallas_call(
        functools.partial(attend_back_kernel, block=256),
        grid=(heads,),
        in_specs=[
            each,
            each,
            each,
            flat,
            flat,
            pl.BlockSpec((1, 1, rows), lambda h: (h, 0, 0)),
            once(cosine.shape),
            once(sine.shape),
            once(mask.shape),
        ],
        out_specs=[each, each, each],
        out_shape=[jax.ShapeDtypeStruct((heads, HEAD, rows), BF)] * 3,
        compiler_params=pltpu.CompilerParams(vmem_limit_bytes=50 * 2**20),
        cost_estimate=pl.CostEstimate(flops=heads * 10 * 1310720 * 256, bytes_accessed=16 * 2**20, transcendentals=heads * 1310720),
        name="attend_back",
    )(qt, kt, vt, mixed, grad_mixed, lse, cosine, sine, mask)


def body(
    tokens_in,
    cotangent,
    picture_ids,
    patch_positions,
    qkv_weight,
    out_weight,
    up_projection_weight,
    down_weight,
    projection_bias_rows,
    norm_vectors,
    qkv_first,
    out_first,
    up_first,
    down_first,
    bias_first,
    vector_first,
    qkv_second,
    out_second,
    up_second,
    down_second,
    bias_second,
    vector_second,
):
    count = lax.axis_size("g")
    bits = count.bit_length() - 1
    g, c, z = lax.axis_index("g"), lax.axis_index("c"), lax.axis_index("z")
    is_mid = (z == 1) | (z == 2)
    low_core = c == 0
    d_local = qkv_weight.shape[0]
    width = tokens_in.shape[2]
    part_rows = tokens_in.shape[1]
    inner = 640
    forth, back = tuple(range(bits)), tuple(reversed(range(bits)))

    with jax.named_scope("small"):
        bias_half = jnp.where(
            low_core,
            jnp.concatenate([projection_bias_rows[0:3, :160].reshape(480), projection_bias_rows[3:5].reshape(640)]),
            jnp.concatenate([projection_bias_rows[0:3, 160:].reshape(480), projection_bias_rows[5:7].reshape(640)]),
        )
        counted = jnp.concatenate([picture_ids[None], patch_positions], axis=0).astype(F32)
        small = jnp.concatenate([bias_half, counted.reshape(3 * 2 * part_rows)])[None]
        relative = jnp.concatenate(
            [small] + [lax.ppermute(small, "z", [(i, i ^ d) for i in range(4)]) for d in (1, 2, 3)], axis=0
        )
        biases = relative[:, :1120]
        bias_near = biases[:2]
        bias_far = jnp.where(is_mid, biases[2:][::-1], biases[2:])
        counted = relative[:, 1120:].reshape(4, 3, 2, part_rows)
        counted = jnp.where((z & 1) == 0, counted[:, :, 0], counted[:, :, 1])
        counted = jnp.concatenate([lax.dynamic_slice_in_dim(counted, k ^ z, 1, 0) for k in range(4)], axis=0)
        counted = jnp.where((z >> 1) == c, counted, swap_core(counted))
        counted = jnp.moveaxis(counted, 1, 0).reshape(3, 4 * part_rows)

    with jax.named_scope("pack"):
        qkv_low = qkv_weight.astype(BF).reshape(d_local, 3, 2, 160)
        out_low = out_weight.astype(BF).T.reshape(d_local, 1, 2, 160)
        first_low = jnp.concatenate([qkv_low, out_low], axis=1)
        up_low = up_projection_weight.astype(BF)
        down_low = jnp.transpose(down_weight.astype(BF), (2, 0, 1))
        halves = [
            jnp.concatenate(
                [
                    first_low[:, :, h].reshape(d_local, inner),
                    up_low[:, 2 * h : 2 * h + 2].reshape(d_local, inner),
                    down_low[:, 2 * h : 2 * h + 2].reshape(d_local, inner),
                ],
                axis=1,
            )
            for h in range(2)
        ]
        keep = jnp.where(low_core, halves[0], halves[1])
        other = swap_core(jnp.where(low_core, halves[1], halves[0]))
        shard = jnp.concatenate([jnp.where(low_core, keep, other), jnp.where(low_core, other, keep)], axis=0)
        shard_q, shard_u, shard_d = [shard[:, i * inner : (i + 1) * inner] for i in range(3)]

    def near_z(own, *earlier):
        partner = move(own, "z", NEAR, *earlier)
        return jnp.concatenate([own, partner], axis=-1)

    def far_of(mid, end):
        return jnp.where(is_mid, mid, end)

    with jax.named_scope("rows_x"):
        source = rows_in(tokens_in, c, z)
    with jax.named_scope("gq"):
        near_q = near_z(shard_q)
        mid_q = move(near_q, "z", MIDS)
        qa = Gather(near_q, forth, g, count)
        qax = qa.step()
        end_q = move(mid_q, "z", OUTER)
    with jax.named_scope("gu"):
        near_u = near_z(shard_u, near_q)
        mid_u = move(near_u, "z", MIDS)
        ua = Gather(near_u, forth, g, count)
        uax = ua.step(near_q)
        end_u = move(mid_u, "z", OUTER, end_q)
    with jax.named_scope("gq"):
        qay = qa.finish()
        qb = Gather(far_of(mid_q, end_q), back, g, count)
        qby = qb.step(uax)
        qbx = qb.finish(uax)
    with jax.named_scope("gd"):
        near_d = near_z(shard_d, near_u)
        mid_d = move(near_d, "z", MIDS, mid_u)
        da = Gather(near_d, forth, g, count)
        dax = da.step(qax)
        end_d = move(mid_d, "z", OUTER, end_u)
    with jax.named_scope("gu"):
        uay = ua.finish(qay)
        ub = Gather(far_of(mid_u, end_u), back, g, count)
        uby = ub.step(qby)
        ubx = ub.finish(dax)
    with jax.named_scope("gd"):
        day = da.finish(uby)
        db = Gather(far_of(mid_d, end_d), back, g, count)
        dby = db.step(uay)
        dbx = db.finish(qbx)
    with jax.named_scope("rows_g"):
        grad_rows = rows_in(cotangent, c, z, end_u)

    first_wa, first_wb = qa.whole(), qb.whole()
    up_wa, up_wb = ua.whole(), ub.whole()
    down_wa, down_wb = da.whole(), db.whole()

    rows = source.shape[0]
    start = jnp.sum((counted[0] == 1).astype(jnp.int32))
    turned = lambda value: jnp.roll(value, -start, axis=0)
    counted = jnp.roll(counted, -start, axis=1)
    source = turned(source).astype(F32)
    grad_rows = turned(grad_rows)
    ids = counted[0, MIDDLE:]
    mask = jnp.where(ids[:, None] == ids[None, :], 0.0, -1e30).astype(F32)
    powers = jnp.arange(HEAD // 4, dtype=F32) * (2.0 / (HEAD // 2))
    inverse = jnp.power(10000.0, -powers)
    angles = jnp.concatenate([inverse[:, None] * counted[1][None], inverse[:, None] * counted[2][None]], axis=0)
    cosine, sine = jnp.cos(angles), jnp.sin(angles)

    hat_one, scale_one = normalise(source)
    a_one = (hat_one * norm_vectors[0] + norm_vectors[1]).astype(BF)

    def qkv_bias(pair):
        zero = jnp.zeros((160,), F32)
        return jnp.concatenate([pair[0, :480], zero, pair[1, :480], zero])

    saved = []
    for weight, bias, earlier in ((first_wa, bias_near, (dax, qby)), (first_wb, bias_far, (uby,))):
        mixed = dot(after(weight, *earlier), a_one, 0, 1) + qkv_bias(bias)[:, None]
        saved.append(attend(mixed, cosine, sine, mask))

    def out_part(weight):
        return jnp.concatenate([weight[:, 480:640], weight[:, 1120:1280]], axis=1)

    def qkv_part(weight):
        return jnp.concatenate([weight[:, :480], weight[:, 640:1120]], axis=1)

    out_wa, out_wb = out_part(first_wa), out_part(first_wb)
    branch = (dot(saved[0][3], out_wa, 0, 1) + dot(after(saved[1][3], grad_rows, uay), out_wb, 0, 1)).astype(BF)
    middle = source + (branch.astype(F32) + swap_core(branch).astype(F32)) + norm_vectors[4]
    hat_two, scale_two = normalise(middle)
    a_two = (hat_two * norm_vectors[2] + norm_vectors[3]).astype(BF)

    def up_bias(pair):
        return pair[:, 480:].reshape(1280)

    active, slopes = [], []
    for weight, bias, earlier in ((up_wa, bias_near, (dby,)), (up_wb, bias_far, (day,))):
        hidden = dot(a_two, after(weight, *earlier), 1, 0) + up_bias(bias)
        gate = jax.nn.sigmoid(GELU_SLOPE * hidden)
        active.append((hidden * gate).astype(BF))
        slopes.append((gate + GELU_SLOPE * hidden * gate * (1.0 - gate)).astype(BF))
    feed = (dot(active[0], down_wa, 1, 1) + dot(active[1], down_wb, 1, 1)).astype(BF)
    result = middle + (feed.astype(F32) + swap_core(feed).astype(F32)) + norm_vectors[5]
    with jax.named_scope("rows_out"):
        block_out, out_pieces = rows_out(result.astype(BF), start, c, z)

    def give(near, far, *earlier):
        far = scatter_g(far, forth, g, count, *earlier)
        near = scatter_g(near, back, g, count, *earlier)
        far = far + lax.ppermute(far.astype(BF), "z", INNER).astype(F32)
        near = near + lax.ppermute(far.astype(BF), "z", MIDS).astype(F32)
        own = near[:, :inner] + lax.ppermute(near[:, inner:].astype(BF), "z", NEAR).astype(F32)
        upper, lower = own[:d_local], own[d_local:]
        keep = jnp.where(low_core, upper, lower)
        other = swap_core(jnp.where(low_core, lower, upper).astype(BF)).astype(F32)
        return jnp.stack([jnp.where(low_core, keep, other), jnp.where(low_core, other, keep)], axis=1)

    with jax.named_scope("sd"):
        grad_down = give(*[dot(grad_rows, a, 0, 0).astype(BF) for a in active], day, dbx)
    grad_hidden = [
        (dot(grad_rows, w, 1, 0) * s.astype(F32)).astype(BF) for w, s in ((down_wa, slopes[0]), (down_wb, slopes[1]))
    ]
    bias_up = [jnp.sum(v, axis=0, dtype=F32) for v in grad_hidden]
    with jax.named_scope("su"):
        grad_up = give(*[dot(a_two, v, 0, 0).astype(BF) for v in grad_hidden])
    part = (dot(grad_hidden[0], up_wa, 1, 1) + dot(grad_hidden[1], up_wb, 1, 1)).astype(BF)
    grad_second = part.astype(F32) + swap_core(part).astype(F32)
    grad_out = grad_rows.astype(F32)
    grad_middle = grad_out + norm_back(grad_second, norm_vectors[2], hat_two, scale_two)
    grad_branch = grad_middle.astype(BF)
    grad_mixed, grad_outw = [None, None], [None, None]
    for i, weight, earlier in ((1, out_wb, ()), (0, out_wa, tuple(out_pieces))):
        grad_outw[i] = dot(grad_branch, saved[i][3], 0, 1).astype(BF)
        grad_att = dot(weight, grad_branch, 0, 1).astype(BF)
        if earlier:
            grad_att = after(grad_att, *earlier)
        dq, dk, dv = attend_back(saved[i], grad_att, cosine, sine, mask)
        joined = jnp.stack([v.reshape(2, 160, rows) for v in (dq, dk, dv)], axis=1)
        grad_mixed[i] = joined.reshape(960, rows)
    bias_qkv = [jnp.sum(v, axis=1, dtype=F32) for v in grad_mixed]
    part = (
        dot(grad_mixed[0], qkv_part(first_wa), 0, 1) + dot(grad_mixed[1], qkv_part(first_wb), 0, 1)
    ).astype(BF)
    grad_first_full = []
    for v, o in zip(grad_mixed, grad_outw):
        gq = dot(a_one, v, 0, 1).astype(BF)
        grad_first_full.append(jnp.concatenate([gq[:, :480], o[:, :160], gq[:, 480:], o[:, 160:]], axis=1))
    with jax.named_scope("sq"):
        grad_first = give(*grad_first_full)
    grad_norm = part.astype(F32) + swap_core(part).astype(F32)
    grad_source = grad_middle + norm_back(grad_norm, norm_vectors[0], hat_one, scale_one)
    with jax.named_scope("rows_dx"):
        input_grad, _ = rows_out(grad_source.astype(BF), start, c, z)
        input_grad = input_grad.astype(F32)

    def own_half(value):
        return jnp.where(low_core, value[: rows // 2], value[rows // 2 :])

    vector_grad = jnp.stack(
        [
            jnp.sum(own_half(v), axis=0)
            for v in (grad_norm * hat_one, grad_norm, grad_second * hat_two, grad_second, grad_middle, grad_out)
        ]
    )
    far_zero = jnp.where(z < 2, 2, 1)
    far_one = jnp.where(z < 2, 3, 0)
    placed = jnp.zeros((7, 4, 320), F32)
    for index, place in enumerate((z, z ^ 1, far_zero, far_one)):
        qkv_sum = bias_qkv[index // 2].reshape(2, 3, 1, 160)[index % 2]
        up_sum = bias_up[index // 2].reshape(2, 2, 1, 320)[index % 2]
        placed = lax.dynamic_update_slice(placed, qkv_sum, (0, place, c * 160))
        placed = lax.dynamic_update_slice(placed, up_sum, (3 + 2 * c, place, 0))
    with jax.named_scope("vectors"):
        summed = add_up(jnp.concatenate([placed.reshape(7, 4 * 320), vector_grad], axis=0), count)
    grad_bias = lax.dynamic_slice(summed, (0, z * 320), (7, 320))
    grad_vector = summed[7:]

    first_split = grad_first.reshape(d_local, 2, 4, 160)
    grad_qkv = jnp.moveaxis(first_split[:, :, :3], 1, 2).reshape(d_local, 3, 320)
    grad_o = first_split[:, :, 3].reshape(d_local, 320).T
    grad_up = grad_up.reshape(d_local, 4, 320)
    grad_down = jnp.transpose(grad_down.reshape(d_local, 4, 320), (1, 2, 0))
    outputs = [block_out, input_grad]
    for weight, grad, first, second, rate, decay in (
        (qkv_weight, grad_qkv, qkv_first, qkv_second, MATRIX_RATE, MATRIX_DECAY),
        (out_weight, grad_o, out_first, out_second, MATRIX_RATE, MATRIX_DECAY),
        (up_projection_weight, grad_up, up_first, up_second, MATRIX_RATE, MATRIX_DECAY),
        (down_weight, grad_down, down_first, down_second, MATRIX_RATE, MATRIX_DECAY),
        (projection_bias_rows, grad_bias, bias_first, bias_second, VECTOR_RATE, 0.0),
        (norm_vectors, grad_vector, vector_first, vector_second, VECTOR_RATE, 0.0),
    ):
        outputs.extend(adam_step(weight, grad, first, second, rate, decay))
    return tuple(outputs)


def solution(mesh):
    devices = mesh.devices.reshape(mesh.shape["dp"] // 2, 2, mesh.shape["tensor"])
    own_mesh = Mesh(devices, ("g", "c", "z"))
    rows = P(("g", "c"), "z", None)
    in_weights = (P(("g", "c"), None, "z"), P("z", ("g", "c")), P(("g", "c"), None, "z"), P(None, "z", ("g", "c")))
    vectors = (P(None, "z"), P())
    params = in_weights + vectors
    out_specs = [rows, rows]
    for spec in params:
        out_specs.extend([spec] * 3)
    return jax.shard_map(
        body,
        mesh=own_mesh,
        in_specs=(rows, rows, P(("g", "c"), "z"), P(None, ("g", "c"), "z")) + params * 3,
        out_specs=tuple(out_specs),
        check_vma=False,
    )
```

```python
import functools

import jax
import jax.numpy as jnp
from jax import lax
from jax.experimental import pallas as pl
from jax.experimental.pallas import tpu as pltpu
from jax.sharding import Mesh, PartitionSpec as P

HEAD = 80
HALF = HEAD // 2
STEP = 10
MIDDLE = 1024

NORM_EPS = 1e-06
BETA_ONE = 0.9
BETA_TWO = 0.95
ADAM_EPS = 1e-08
MATRIX_RATE = 0.03
VECTOR_RATE = 0.2
MATRIX_DECAY = 0.1
GELU_SLOPE = 1.702
LOG2E = 1.4426950408889634
LN2 = 0.6931471805599453

BF = jnp.bfloat16
F32 = jnp.float32


def dot(left, right, left_dim, right_dim):
    return lax.dot_general(
        left, right, (((left_dim,), (right_dim,)), ((), ())), preferred_element_type=F32
    )


def normalise(source):
    centre = source - jnp.mean(source, axis=-1, keepdims=True)
    spread = lax.rsqrt(jnp.mean(centre * centre, axis=-1, keepdims=True) + NORM_EPS)
    return centre * spread, spread


def norm_back(gradient, gain_vec, normed, spread):
    scaled = gradient * gain_vec
    return spread * (
        scaled
        - jnp.mean(scaled, axis=-1, keepdims=True)
        - normed * jnp.mean(scaled * normed, axis=-1, keepdims=True)
    )


def adam_step(weight, gradient, first, second, rate, decay):
    first_new = BETA_ONE * first + (1.0 - BETA_ONE) * gradient
    second_new = BETA_TWO * second + (1.0 - BETA_TWO) * gradient * gradient
    fix_one = 1.0 - BETA_ONE**STEP
    fix_two = 1.0 - BETA_TWO**STEP
    ratio = first_new / fix_one / (jnp.sqrt(second_new / fix_two) + ADAM_EPS)
    return (weight - rate * (ratio + decay * weight), first_new, second_new)


NEAR = [(0, 1), (1, 0), (2, 3), (3, 2)]
MIDS = [(1, 2), (2, 1)]
OUTER = [(1, 0), (2, 3)]
INNER = [(0, 1), (3, 2)]


def after(value, *earlier):
    return lax.optimization_barrier((value, *earlier))[0]


def move(value, axis, pairs, *earlier):
    return lax.ppermute(after(value, *earlier) if earlier else value, axis, pairs)


def swap_core(value, *earlier):
    return move(value, "c", [(0, 1), (1, 0)], *earlier)


def swap_bit(value, bit, count, *earlier):
    return move(value, "g", [(i, i ^ (1 << bit)) for i in range(count)], *earlier)


class Gather:
    def __init__(self, block, order, g, count):
        self.rows, self.columns = block.shape
        self.order, self.g, self.count = list(order), g, count
        self.bits = len(self.order)
        self.current = block.reshape((1,) * self.bits + block.shape)
        self.other = None

    def take(self, *earlier):
        if self.other is None:
            return
        other = after(self.other, *earlier) if earlier else self.other
        upper = ((self.g >> self.bit) & 1) == 1
        mine = self.current
        self.current = jnp.concatenate(
            [jnp.where(upper, other, mine), jnp.where(upper, mine, other)], axis=self.bits - 1 - self.bit
        )
        self.other = None

    def step(self, *earlier):
        self.take()
        if self.order:
            self.bit = self.order.pop(0)
            self.other = swap_bit(self.current, self.bit, self.count, *earlier)
            return self.other
        return self.current

    def finish(self, *earlier):
        last = self.step(*earlier)
        while self.order:
            last = self.step()
        return last

    def whole(self):
        self.take()
        return self.current.reshape(self.count * self.rows, self.columns)


class Scatter:
    def __init__(self, full, order, g, count):
        self.rows, self.columns = full.shape[0] // count, full.shape[1]
        self.order, self.g, self.count = list(order), g, count
        self.bits = len(self.order)
        self.terms = [full.reshape((2,) * self.bits + (self.rows, self.columns))]

    def sliced(self, place, axis):
        return [lax.dynamic_slice_in_dim(v, place, 1, axis) for v in self.terms]

    def total(self, terms):
        out = terms[0].astype(F32)
        for term in terms[1:]:
            out = out + term.astype(F32)
        return out

    def send(self, *earlier):
        bit = self.order.pop(0)
        axis = self.bits - 1 - bit
        mine = (self.g >> bit) & 1
        sent = self.total(self.sliced(1 - mine, axis)).astype(BF)
        self.kept = self.sliced(mine, axis)
        self.got = swap_bit(sent, bit, self.count, *earlier)
        return self.got

    def add(self, *earlier):
        self.terms = self.kept + [after(self.got, *earlier) if earlier else self.got]
        while len(self.order) > 1:
            self.send()
            self.terms = self.kept + [self.got]

    def whole(self):
        return self.total(self.terms).reshape(self.rows, self.columns)


def row_moves(step):
    moves = []
    for c in range(2):
        for z in range(4):
            moves.append((c * 4 + z, (z >> 1) * 4 + 2 * c + ((z & 1) ^ step)))
    return moves


class RowsIn:
    def __init__(self, local, z):
        self.local, self.odd = local, (z & 1) == 1
        self.pieces = []

    def send(self, *earlier):
        step = len(self.pieces)
        sent = jnp.where(self.odd, self.local[1 - step], self.local[step])
        self.sent = sent
        self.pieces.append(move(sent, ("c", "z"), row_moves(step), *earlier))
        return self.pieces[-1]

    def half(self, *earlier):
        first, second = [after(v, *earlier) if earlier else v for v in self.pieces]
        return jnp.concatenate(
            [jnp.where(self.odd, second, first), jnp.where(self.odd, first, second)], axis=0
        )


def rows_out(turned, start, c, z):
    rows, width = turned.shape
    part = rows // 4
    odd = z & 1
    longer = jnp.concatenate([turned, turned[:part]], axis=0)
    pieces = []
    for step in range(2):
        first = lax.rem((2 * c + (odd ^ step)) * part - start + rows, rows)
        sent = lax.dynamic_slice(longer, (first, 0), (part, width))
        pieces.append(lax.ppermute(sent, ("c", "z"), [(b, a) for a, b in row_moves(step)]))
    first, second = pieces
    return jnp.stack([jnp.where(odd == 1, second, first), jnp.where(odd == 1, first, second)]), pieces


def turn_rows(start, upper, lower, vectors=None):
    half, width = upper.shape
    rows = 2 * half
    block = 256
    more = block + 16

    def kernel(start_ref, up_ref, low_ref, *refs):
        wide = refs[-1]
        for at in range(0, half, block):
            wide[at : at + block] = up_ref[at : at + block].astype(F32)
            wide[half + at : half + at + block] = low_ref[at : at + block].astype(F32)
        wide[rows : rows + more] = up_ref[:more].astype(F32)

        @pl.loop(0, rows // block)
        def _(i):
            at = i * block
            first = lax.rem(at + start_ref[0], rows)
            low = lax.rem(first, 8)
            value = wide[pl.ds(pl.multiple_of(first - low, 8), more)]
            value = pltpu.roll(value, lax.rem(more - low, more), 0)[:block]
            into = pl.ds(pl.multiple_of(at, block), block)
            if vectors is None:
                refs[0][into] = value.astype(BF)
            else:
                refs[1][into] = value.astype(BF)
                refs[2][into] = first_norm_step(value, refs[0][...])[0].astype(BF)

    outs = 1 if vectors is None else 2
    extra = [] if vectors is None else [vectors]
    return pl.pallas_call(
        kernel,
        in_specs=[pl.BlockSpec(memory_space=pltpu.SMEM)]
        + [pl.BlockSpec(memory_space=pltpu.VMEM)] * (2 + len(extra)),
        out_specs=[pl.BlockSpec(memory_space=pltpu.VMEM)] * outs,
        out_shape=[jax.ShapeDtypeStruct((rows, width), BF)] * outs,
        scratch_shapes=[pltpu.VMEM((rows + more, width), F32)],
        compiler_params=pltpu.CompilerParams(vmem_limit_bytes=40 * 2**20),
        cost_estimate=FREE,
        name="turn_rows",
    )(start[None], upper, lower, *extra)


def add_up(value, count):
    value = value + swap_core(value)
    for bit in range(count.bit_length() - 1):
        value = value + swap_bit(value, bit, count)
    for distance in (1, 2):
        value = value + lax.ppermute(value, "z", [(i, i ^ distance) for i in range(4)])
    return value


SEGMENTS = ((0, MIDDLE, False), (MIDDLE, None, True))


def attend_kernel(q_ref, k_ref, v_ref, cos_ref, sin_ref, mask_ref, qt_ref, kt_ref, vt_ref, ot_ref, lse_ref, *, block):
    cosine, sine = cos_ref[...], sin_ref[...]

    def turn(source, factor):
        first, second = source[:HALF], source[HALF:]
        return (
            jnp.concatenate([first * cosine - second * sine, second * cosine + first * sine], axis=0) * factor
        ).astype(BF)

    rows = q_ref.shape[1]
    qt = turn(q_ref[...], LOG2E * HEAD ** (-0.5))
    kt = turn(k_ref[...], 1.0)
    vt = v_ref[...].astype(BF)
    qt_ref[0] = qt
    kt_ref[0] = kt
    vt_ref[0] = vt
    for first, last, masked in ((0, MIDDLE, False), (MIDDLE, rows, True)):
        keys = kt[:, first:last]
        values = vt[:, first:last]
        for at in range(first, last, block):
            scores = dot(keys, qt[:, at : at + block], 0, 0)
            if masked:
                scores = scores + mask_ref[:, at - first : at - first + block]
            largest = jnp.max(scores, axis=0, keepdims=True)
            raised = jnp.exp2(scores - largest)
            total = jnp.sum(raised, axis=0, keepdims=True)
            mixed = dot(values, raised.astype(BF), 1, 0)
            ot_ref[:, at : at + block] = (mixed / total).astype(BF)
            lse_ref[0, :, at : at + block] = largest + jnp.log2(total)


def attend_back_kernel(qt_ref, kt_ref, vt_ref, ot_ref, dot_ref, lse_ref, cos_ref, sin_ref, mask_ref, dq_ref, dk_ref, dv_ref, *, block):
    cosine, sine = cos_ref[...], sin_ref[...]

    def turn_back(grad, factor):
        first, second = grad[:HALF] * factor, grad[HALF:] * factor
        return jnp.concatenate([first * cosine + second * sine, second * cosine - first * sine], axis=0).astype(BF)

    rows = cos_ref.shape[1]
    qt, kt, vt, dot_ = qt_ref[0], kt_ref[0], vt_ref[0], dot_ref[...]
    delta = jnp.sum(dot_.astype(F32) * ot_ref[...].astype(F32), axis=0, keepdims=True)
    lse = lse_ref[0]
    queries = qt.astype(F32).T.astype(BF)
    grads = dot_.astype(F32).T.astype(BF)
    dq_parts, dk_parts, dv_parts = [], [], []
    for first, last, masked in ((0, MIDDLE, False), (MIDDLE, rows, True)):
        keys = kt[:, first:last]
        values = vt[:, first:last]
        dk = dv = None
        for at in range(first, last, block):
            sl = slice(at, at + block)
            scores = dot(keys, qt[:, sl], 0, 0)
            if masked:
                scores = scores + mask_ref[:, at - first : at - first + block]
            chances = jnp.exp2(scores - lse[:, sl])
            grad_chances = dot(values, dot_[:, sl], 0, 0)
            grad_scores = (chances * (grad_chances - delta[:, sl])).astype(BF)
            dv_part = dot(chances.astype(BF), grads[sl], 1, 0)
            dk_part = dot(grad_scores, queries[sl], 1, 0)
            dv = dv_part if dv is None else dv + dv_part
            dk = dk_part if dk is None else dk + dk_part
            dq_parts.append(dot(keys, grad_scores, 1, 0))
        dk_parts.append(dk.T)
        dv_parts.append(dv.T)
    dq_ref[0] = turn_back(jnp.concatenate(dq_parts, axis=1), HEAD ** (-0.5))
    dk_ref[0] = turn_back(jnp.concatenate(dk_parts, axis=1), LN2)
    dv_ref[0] = jnp.concatenate(dv_parts, axis=1).astype(BF)


def attend(mixed, cosine, sine, mask):
    rows = mixed.shape[1]
    heads = 4
    once = lambda shape: pl.BlockSpec(shape, lambda h: (0, 0))
    part = lambda which: pl.BlockSpec((HEAD, rows), lambda h: ((h // 2) * 8 + 2 * which + h % 2, 0))
    each = pl.BlockSpec((1, HEAD, rows), lambda h: (h, 0, 0))
    return pl.pallas_call(
        functools.partial(attend_kernel, block=256),
        grid=(heads,),
        in_specs=[part(0), part(1), part(2), once(cosine.shape), once(sine.shape), once(mask.shape)],
        out_specs=[
            each,
            each,
            each,
            pl.BlockSpec((HEAD, rows), lambda h: (h, 0)),
            pl.BlockSpec((1, 1, rows), lambda h: (h, 0, 0)),
        ],
        out_shape=[jax.ShapeDtypeStruct((heads, HEAD, rows), BF)] * 3
        + [
            jax.ShapeDtypeStruct((heads * HEAD, rows), BF),
            jax.ShapeDtypeStruct((heads, 1, rows), F32),
        ],
        compiler_params=pltpu.CompilerParams(vmem_limit_bytes=40 * 2**20),
        cost_estimate=FREE,
        name="attend",
    )(mixed, mixed, mixed, cosine, sine, mask)


def attend_back(saved, grad_mixed, cosine, sine, mask):
    qt, kt, vt, mixed, lse = saved
    heads, _, rows = qt.shape
    once = lambda shape: pl.BlockSpec(shape, lambda h: (0, 0))
    each = pl.BlockSpec((1, HEAD, rows), lambda h: (h, 0, 0))
    flat = pl.BlockSpec((HEAD, rows), lambda h: (h, 0))
    return pl.pallas_call(
        functools.partial(attend_back_kernel, block=256),
        grid=(heads,),
        in_specs=[
            each,
            each,
            each,
            flat,
            flat,
            pl.BlockSpec((1, 1, rows), lambda h: (h, 0, 0)),
            once(cosine.shape),
            once(sine.shape),
            once(mask.shape),
        ],
        out_specs=[each, each, each],
        out_shape=[jax.ShapeDtypeStruct((heads, HEAD, rows), BF)] * 3,
        compiler_params=pltpu.CompilerParams(vmem_limit_bytes=50 * 2**20),
        cost_estimate=FREE,
        name="attend_back",
    )(qt, kt, vt, mixed, grad_mixed, lse, cosine, sine, mask)


FREE = pl.CostEstimate(flops=0, bytes_accessed=0, transcendentals=0)
BLOCK = 256


def params(mib=48):
    return pltpu.CompilerParams(vmem_limit_bytes=mib * 2**20, dimension_semantics=("arbitrary",))


def whole(shape):
    return pl.BlockSpec(shape, lambda i: (0,) * len(shape))


def rows_of(width, block=BLOCK):
    return pl.BlockSpec((block, width), lambda i: (i, 0))


def columns_of(height, block=BLOCK):
    return pl.BlockSpec((height, block), lambda i: (0, i))


def product(name, pairs, outs, finish, extras=(), block=None):
    size = pairs[0][0].shape[1 - pairs[0][1]]
    block = block or (640 if size % 640 == 0 else 512 if size % 512 == 0 else BLOCK)
    in_specs, operands = [], []
    for left, left_dim, right, _ in pairs:
        in_specs.append(rows_of(left.shape[1], block) if left_dim == 1 else columns_of(left.shape[0], block))
        in_specs.append(whole(right.shape))
        operands.extend([left, right])
    for value in extras:
        in_specs.append(rows_of(value.shape[1], block) if value.shape[0] == size else whole(value.shape))
        operands.append(value)
    out_specs, out_shape = [], []
    for out in outs:
        if len(out) == 2:
            out_specs.append(rows_of(out[0], block))
            out_shape.append(jax.ShapeDtypeStruct((size, out[0]), out[1]))
        else:
            out_specs.append(whole((1, out[0])))
            out_shape.append(jax.ShapeDtypeStruct((1, out[0]), F32))

    def kernel(*refs):
        total = None
        for i, (_, left_dim, _, right_dim) in enumerate(pairs):
            term = dot(refs[2 * i][...], refs[2 * i + 1][...], left_dim, right_dim)
            total = term if total is None else total + term
        at = 2 * len(pairs)
        values = finish(total, *[r[...] for r in refs[at : at + len(extras)]])
        store(values, refs[at + len(extras) :], outs)

    return pl.pallas_call(
        kernel,
        grid=(size // block,),
        in_specs=in_specs,
        out_specs=out_specs,
        out_shape=out_shape,
        compiler_params=params(),
        cost_estimate=FREE,
        name=name,
    )(*operands)


def store(values, refs, outs):
    for value, ref, out in zip(values, refs, outs):
        if len(out) == 2:
            ref[...] = value.astype(out[1])
        else:
            summed = jnp.sum(value, axis=0, keepdims=True)

            @pl.when(pl.program_id(0) == 0)
            def _():
                ref[...] = summed

            @pl.when(pl.program_id(0) > 0)
            def _():
                ref[...] += summed


def by_rows(name, inputs, outs, step, block=256):
    size = inputs[0].shape[0]
    in_specs = [rows_of(v.shape[1], block) if v.shape[0] == size else whole(v.shape) for v in inputs]
    out_specs, out_shape = [], []
    for out in outs:
        if len(out) == 2:
            out_specs.append(rows_of(out[0], block))
            out_shape.append(jax.ShapeDtypeStruct((size, out[0]), out[1]))
        else:
            out_specs.append(whole((1, out[0])))
            out_shape.append(jax.ShapeDtypeStruct((1, out[0]), F32))

    def kernel(*refs):
        values = step(*[r[...] for r in refs[: len(inputs)]])
        store(values, refs[len(inputs) :], outs)

    return pl.pallas_call(
        kernel,
        grid=(size // block,),
        in_specs=in_specs,
        out_specs=out_specs,
        out_shape=out_shape,
        compiler_params=params(),
        cost_estimate=FREE,
        name=name,
    )(*inputs)


def first_norm_step(source, vectors):
    hat, _ = normalise(source.astype(F32))
    return (hat * vectors[0:1] + vectors[1:2],)


def second_norm_step(source, part, other, vectors):
    middle = source.astype(F32) + (part.astype(F32) + other.astype(F32)) + vectors[4:5]
    hat, _ = normalise(middle)
    return middle, hat * vectors[2:3] + vectors[3:4]


def second_back_step(part, other, middle, grad_out, vectors):
    grad = part.astype(F32) + other.astype(F32)
    hat, scale = normalise(middle.astype(F32))
    out = grad_out.astype(F32)
    grad_middle = out + norm_back(grad, vectors[2:3], hat, scale)
    return grad_middle, grad_middle, grad * hat, grad, grad_middle, out


def first_back_step(part, other, source, grad_middle, vectors):
    grad = part.astype(F32) + other.astype(F32)
    hat, scale = normalise(source.astype(F32))
    return grad_middle.astype(F32) + norm_back(grad, vectors[0:1], hat, scale), grad * hat, grad


def result_step(middle, part, other, vectors):
    return (middle.astype(F32) + (part.astype(F32) + other.astype(F32)) + vectors[5:6],)


def hidden_step(total, bias):
    hidden = total + bias
    gate = 1.0 / (1.0 + jnp.exp(-GELU_SLOPE * hidden))
    return hidden * gate, gate + GELU_SLOPE * hidden * gate * (1.0 - gate)


def hidden_back_step(total, slope):
    grad = (total * slope.astype(F32)).astype(BF)
    return grad, grad.astype(F32)


def feed_back(grad_rows, down, up, slopes):
    size, width = grad_rows.shape
    hidden = slopes[0].shape[1]

    def kernel(g_ref, da_ref, db_ref, ua_ref, ub_ref, sa_ref, sb_ref, ha_ref, hb_ref, part_ref, suma_ref, sumb_ref):
        total = None
        for d_ref, u_ref, s_ref, h_ref, sum_ref in (
            (da_ref, ua_ref, sa_ref, ha_ref, suma_ref),
            (db_ref, ub_ref, sb_ref, hb_ref, sumb_ref),
        ):
            grad = (dot(g_ref[...], d_ref[...], 1, 0) * s_ref[...].astype(F32)).astype(BF)
            h_ref[...] = grad
            store((grad.astype(F32),), (sum_ref,), ((hidden,),))
            term = dot(grad, u_ref[...], 1, 1)
            total = term if total is None else total + term
        part_ref[...] = total.astype(BF)

    weight = whole((width, hidden))
    return pl.pallas_call(
        kernel,
        grid=(size // 512,),
        in_specs=[rows_of(width, 512)] + [weight] * 4 + [rows_of(hidden, 512)] * 2,
        out_specs=[rows_of(hidden, 512)] * 2 + [rows_of(width, 512)] + [whole((1, hidden))] * 2,
        out_shape=[jax.ShapeDtypeStruct((size, hidden), BF)] * 2
        + [jax.ShapeDtypeStruct((size, width), BF)]
        + [jax.ShapeDtypeStruct((1, hidden), F32)] * 2,
        compiler_params=params(60),
        cost_estimate=FREE,
        name="feed_back",
    )(grad_rows, *down, *up, *slopes)


def second_norm_back(part, other, middle, grad_rows, vectors, outs):
    size, width = part.shape
    inner = outs[0].shape[1]

    def kernel(p_ref, o_ref, m_ref, g_ref, v_ref, wa_ref, wb_ref, branch_ref, da_ref, db_ref, *sums):
        _, grad_middle, *terms = second_back_step(p_ref[...], o_ref[...], m_ref[...], g_ref[...], v_ref[...])
        branch = grad_middle.astype(BF)
        branch_ref[...] = branch
        for w_ref, d_ref in ((wa_ref, da_ref), (wb_ref, db_ref)):
            d_ref[...] = dot(w_ref[...], branch, 0, 1).astype(BF)
        store(terms, sums, ((width,),) * 4)

    return pl.pallas_call(
        kernel,
        grid=(size // BLOCK,),
        in_specs=[rows_of(width)] * 4 + [whole(vectors.shape)] + [whole((width, inner))] * 2,
        out_specs=[rows_of(width)] + [columns_of(inner)] * 2 + [whole((1, width))] * 4,
        out_shape=[jax.ShapeDtypeStruct((size, width), BF)]
        + [jax.ShapeDtypeStruct((inner, size), BF)] * 2
        + [jax.ShapeDtypeStruct((1, width), F32)] * 4,
        compiler_params=params(),
        cost_estimate=FREE,
        name="norm_two_back",
    )(part, other, middle, grad_rows, vectors, *outs)


def first_grads(a_one, grad_branch, grad_mixed, mixed, inner):
    rows, width = a_one.shape

    def kernel(a_ref, g_ref, m_ref, o_ref, out_ref):
        for slot in range(2):
            at = slot * inner
            out_ref[:, at : at + 480] = dot(a_ref[...], m_ref[slot * 480 : (slot + 1) * 480], 0, 1).astype(BF)
            out_ref[:, at + 480 : at + 640] = dot(g_ref[...], o_ref[slot * 160 : (slot + 1) * 160], 0, 1).astype(BF)

    return pl.pallas_call(
        kernel,
        grid=(width // BLOCK,),
        in_specs=[columns_of(rows), columns_of(rows), whole(grad_mixed.shape), whole(mixed.shape)],
        out_specs=rows_of(2 * inner),
        out_shape=jax.ShapeDtypeStruct((width, 2 * inner), BF),
        compiler_params=params(),
        cost_estimate=FREE,
        name="first_grads",
    )(a_one, grad_branch, grad_mixed, mixed)


def pack(core, qkv, out, up, down, inner):
    rows = out.shape[0]

    def kernel(core_ref, qkv_ref, out_ref, up_ref, down_ref, keep_ref, give_ref):
        for ref, mine in ((keep_ref, core_ref[0]), (give_ref, 1 - core_ref[0])):
            low = mine == 0
            for i in range(3):
                value = qkv_ref[i]
                ref[:, i * 160 : (i + 1) * 160] = jnp.where(low, value[:, :160], value[:, 160:]).astype(BF)
            value = out_ref[...]
            ref[:, 480:640] = jnp.where(low, value[:, :160], value[:, 160:]).astype(BF)
            for j in range(2):
                ref[:, inner + j * 320 : inner + (j + 1) * 320] = jnp.where(
                    low, up_ref[:, j], up_ref[:, j + 2]
                ).astype(BF)
                ref[:, 2 * inner + j * 320 : 2 * inner + (j + 1) * 320] = jnp.where(
                    low, down_ref[j], down_ref[j + 2]
                ).astype(BF)

    return pl.pallas_call(
        kernel,
        in_specs=[pl.BlockSpec(memory_space=pltpu.SMEM)] + [pl.BlockSpec(memory_space=pltpu.VMEM)] * 4,
        out_specs=[pl.BlockSpec(memory_space=pltpu.VMEM)] * 2,
        out_shape=[jax.ShapeDtypeStruct((rows, 3 * inner), BF)] * 2,
        compiler_params=pltpu.CompilerParams(vmem_limit_bytes=40 * 2**20),
        cost_estimate=FREE,
        name="pack",
    )(core, qkv, out, up, down)


def body(
    tokens_in,
    cotangent,
    picture_ids,
    patch_positions,
    qkv_weight,
    out_weight,
    up_projection_weight,
    down_weight,
    projection_bias_rows,
    norm_vectors,
    qkv_first,
    out_first,
    up_first,
    down_first,
    bias_first,
    vector_first,
    qkv_second,
    out_second,
    up_second,
    down_second,
    bias_second,
    vector_second,
):
    count = lax.axis_size("g")
    bits = count.bit_length() - 1
    g, c, z = lax.axis_index("g"), lax.axis_index("c"), lax.axis_index("z")
    is_mid = (z == 1) | (z == 2)
    low_core = c == 0
    d_local = qkv_weight.shape[0]
    width = tokens_in.shape[2]
    part_rows = tokens_in.shape[1]
    inner = 640
    forth, back = tuple(range(bits)), tuple(reversed(range(bits)))

    with jax.named_scope("small"):
        bias_half = jnp.where(
            low_core,
            jnp.concatenate([projection_bias_rows[0:3, :160].reshape(480), projection_bias_rows[3:5].reshape(640)]),
            jnp.concatenate([projection_bias_rows[0:3, 160:].reshape(480), projection_bias_rows[5:7].reshape(640)]),
        )
        counted = jnp.concatenate([picture_ids[None], patch_positions], axis=0).astype(F32)
        small = jnp.concatenate([bias_half, counted.reshape(3 * 2 * part_rows)])[None]
        smalls = [lax.ppermute(small, "z", [(i, i ^ d) for i in range(4)]) for d in (1, 2, 3)]
        relative = jnp.concatenate([small] + smalls, axis=0)
        biases = relative[:, :1120]
        bias_near = biases[:2]
        bias_far = jnp.where(is_mid, biases[2:][::-1], biases[2:])
        counted = relative[:, 1120:].reshape(4, 3, 2, part_rows)
        counted = jnp.where((z & 1) == 0, counted[:, :, 0], counted[:, :, 1])
        counted = jnp.concatenate([lax.dynamic_slice_in_dim(counted, k ^ z, 1, 0) for k in range(4)], axis=0)
        counted = jnp.where((z >> 1) == c, counted, swap_core(counted))
        counted = jnp.moveaxis(counted, 1, 0).reshape(3, 4 * part_rows)

    rows_x, rows_g = RowsIn(tokens_in, z), RowsIn(cotangent, z)
    with jax.named_scope("rows_x"):
        r0, r1 = rows_x.send(), rows_x.send()

    with jax.named_scope("pack"):
        keep, give_away = pack(
            after(c[None].astype(jnp.int32), rows_x.sent),
            jnp.transpose(qkv_weight, (1, 0, 2)),
            out_weight.T,
            up_projection_weight,
            jnp.transpose(down_weight, (0, 2, 1)),
            inner,
        )
        other = swap_core(give_away)
        shard = jnp.concatenate([jnp.where(low_core, keep, other), jnp.where(low_core, other, keep)], axis=0)
        shard_q, shard_u, shard_d = [shard[:, i * inner : (i + 1) * inner] for i in range(3)]

    def pair(first, second):
        return jnp.concatenate([first, second], axis=-1)

    def along(value, distance, *earlier):
        return move(value, "z", [(i, i ^ distance) for i in range(4)], *earlier)

    def gather(block, order):
        return Gather(block, order, g, count)

    def far_of(two, three):
        return jnp.where(is_mid, pair(three, two), pair(two, three))

    def far_of(mid, end):
        return jnp.where(is_mid, mid, end)

    start = jnp.sum((counted[0] == 1).astype(jnp.int32))

    def halves_of(rows_half, *earlier):
        own = rows_half.half(*earlier)
        other = swap_core(own)
        return jnp.where(low_core, own, other), jnp.where(low_core, other, own)

    with jax.named_scope("near"):
        near_q = along(shard_q, 1)
        near_u = along(shard_u, 1)
        near_d = along(shard_d, 1, near_q)
    with jax.named_scope("far"):
        two_q = along(shard_q, 2, near_u)
        three_q = along(shard_q, 3, near_d)
    qa, ua, da = gather(pair(shard_q, near_q), forth), gather(pair(shard_u, near_u), back), gather(pair(shard_d, near_d), forth)
    with jax.named_scope("gx"):
        qax = qa.step()
        dax = da.step(qax)
    with jax.named_scope("gy"):
        uay = ua.step()
        qay = qa.finish(uay)
    with jax.named_scope("gx"):
        uax = ua.finish(dax)
    two_q, three_q = after(two_q, dax, qax, uay), after(three_q, dax, qax, uay)
    qb = gather(jnp.where(is_mid, pair(three_q, two_q), pair(two_q, three_q)), back)
    with jax.named_scope("rows_x"):
        source, a_one = turn_rows(start, *halves_of(rows_x, near_u), norm_vectors)
    qa.take(a_one)
    with jax.named_scope("far"):
        mid_u = move(pair(shard_u, near_u), "z", MIDS, two_q, three_q, dax, uay)
        end_u = move(mid_u, "z", OUTER, qay)
        mid_d = move(pair(shard_d, near_d), "z", MIDS, mid_u, qay)
    with jax.named_scope("gy"):
        qby = qb.step(qay)

    first_wa = qa.whole()

    rows = source.shape[0]
    counted = jnp.roll(counted, -start, axis=1)
    ids = counted[0, MIDDLE:]
    mask = jnp.where(ids[:, None] == ids[None, :], 0.0, -1e30).astype(F32)
    powers = jnp.arange(HEAD // 4, dtype=F32) * (2.0 / (HEAD // 2))
    inverse = jnp.power(10000.0, -powers)
    angles = jnp.concatenate([inverse[:, None] * counted[1][None], inverse[:, None] * counted[2][None]], axis=0)
    cosine, sine = jnp.cos(angles), jnp.sin(angles)

    def qkv_bias(pair):
        zero = jnp.zeros((160,), F32)
        return jnp.concatenate([pair[0, :480], zero, pair[1, :480], zero])

    mixed = dot(after(first_wa, mid_u), a_one, 0, 1) + qkv_bias(bias_near)[:, None]
    saved = [attend(mixed, cosine, sine, mask)]
    done = saved[0][3]
    qb.take(done)
    ua.take(done)
    with jax.named_scope("far"):
        end_d = move(mid_d, "z", OUTER, end_u, qby, done)
    with jax.named_scope("gx"):
        qbx = qb.finish(uax)
    with jax.named_scope("gy"):
        day = da.finish(qby)
    with jax.named_scope("rows_g"):
        rows_g.send(end_d, qby)
        rows_g.send(end_d, qby)
    ub, db = gather(far_of(mid_u, end_u), forth), gather(far_of(mid_d, end_d), back)
    with jax.named_scope("gx"):
        ubx = ub.step(qbx)
    with jax.named_scope("gy"):
        dby = db.step(day)
    first_wb = qb.whole()
    mixed = dot(after(first_wb, day), a_one, 0, 1) + qkv_bias(bias_far)[:, None]
    saved.append(attend(mixed, cosine, sine, mask))
    done = saved[1][3]
    ub.take(done)
    db.take(done)
    with jax.named_scope("gy"):
        uby = ub.finish(dby)
    with jax.named_scope("gx"):
        dbx = db.finish(ubx)
    with jax.named_scope("rows_g"):
        (grad_rows,) = turn_rows(start, *halves_of(rows_g, ubx, dby, done))

    def out_part(weight):
        return jnp.concatenate([weight[:, 480:640], weight[:, 1120:1280]], axis=1)

    def qkv_part(weight):
        return jnp.concatenate([weight[:, :480], weight[:, 640:1120]], axis=1)

    out_wa, out_wb = out_part(first_wa), out_part(first_wb)
    qkv_wa, qkv_wb = qkv_part(first_wa), qkv_part(first_wb)
    same = lambda total: (total,)
    (branch,) = product(
        "out_product",
        [(saved[0][3], 0, out_wa, 1), (saved[1][3], 0, out_wb, 1)],
        [(width, BF)],
        same,
    )
    middle, a_two = by_rows(
        "norm_two",
        [source, branch, swap_core(branch), norm_vectors],
        [(width, BF), (width, BF)],
        second_norm_step,
    )

    def feed_forward(weight, bias):
        return product(
            "up_product",
            [(a_two, 1, weight, 0)],
            [(2 * inner, BF), (2 * inner, BF)],
            hidden_step,
            [bias[:, 480:].reshape(1, 2 * inner)],
        )

    def down_grads(value):
        return product("down_grads", [(grad_rows, 0, value, 0)], [(2 * inner, BF)], same)[0]

    up_wa, down_wa = ua.whole(), da.whole()
    active_a, slope_a = feed_forward(up_wa, bias_near)
    grads_d_near = down_grads(active_a)
    ub.take(grads_d_near, qkv_wa, qkv_wb)
    db.take(grads_d_near)
    up_wb, down_wb = ub.whole(), db.whole()
    active_b, slope_b = feed_forward(up_wb, bias_far)
    grads_d_far = down_grads(active_b)
    active, slopes = (active_a, active_b), (slope_a, slope_b)

    def both_halves(own):
        upper, lower = own[:d_local], own[d_local:]
        keep = jnp.where(low_core, upper, lower)
        other = swap_core(jnp.where(low_core, lower, upper).astype(BF)).astype(F32)
        return jnp.stack([jnp.where(low_core, keep, other), jnp.where(low_core, other, keep)], axis=1)

    class SumZ:
        def __init__(self, near, far, *earlier):
            low_part, high_part = far[:, :inner].astype(BF), far[:, inner:].astype(BF)
            two, three = jnp.where(is_mid, high_part, low_part), jnp.where(is_mid, low_part, high_part)
            self.own = near[:, :inner]
            self.moved = [
                along(value, distance, *earlier)
                for distance, value in ((2, two), (3, three), (1, near[:, inner:].astype(BF)))
            ]

        def take(self, *earlier):
            for value in self.moved:
                self.own = self.own + (after(value, *earlier) if earlier else value).astype(F32)

        def whole(self, *earlier):
            return both_halves(after(self.own, *earlier) if earlier else self.own)

    grads_d = [grads_d_near, grads_d_far]
    with jax.named_scope("sd"):
        near_d, far_d = Scatter(grads_d[0], back, g, count), Scatter(grads_d[1], forth, g, count)
        one_d = [far_d.send(day, dbx), near_d.send(day, dbx)]
    *grad_hidden, part_u, sum_a, sum_b = feed_back(
        after(grad_rows, *grads_d), (down_wa, down_wb), (up_wa, up_wb), slopes
    )
    bias_up = [sum_a, sum_b]

    def up_grads(value, *earlier):
        return product("up_grads", [(after(a_two, *earlier), 0, value, 0)], [(2 * inner, BF)], same)[0]

    grads_u_far = up_grads(grad_hidden[1], part_u)
    with jax.named_scope("sd"):
        far_d.add(grads_u_far)
        near_d.add(grads_u_far)
        sent_d = [far_d.send(), near_d.send()]
    part_u_other = swap_core(part_u, *one_d, grads_u_far)
    (feed,) = product(
        "down_product",
        [(active[0], 1, down_wa, 1), (after(active[1], grads_u_far, *one_d), 1, down_wb, 1)],
        [(width, BF)],
        same,
    )
    feed_other = swap_core(feed)
    grads_u_near = up_grads(grad_hidden[0], feed)
    grad_branch, *grad_atts, sums_0, sums_1, sums_2, sums_3 = second_norm_back(
        part_u, part_u_other, after(middle, grads_u_near, feed_other), grad_rows, norm_vectors, (out_wa, out_wb)
    )
    sums_two = [sums_0, sums_1, sums_2, sums_3]
    with jax.named_scope("sd"):
        far_d.add(grad_branch)
        near_d.add(grad_branch)
    with jax.named_scope("su"):
        near_u, far_u = Scatter(grads_u_near, back, g, count), Scatter(grads_u_far, forth, g, count)
        one_u = [far_u.send(*sent_d, grad_branch), near_u.send(*sent_d, grad_branch)]

    def attention_back(i, *earlier):
        dq, dk, dv = attend_back(saved[i], after(grad_atts[i], *earlier), cosine, sine, mask)
        return jnp.stack([v.reshape(2, 160, rows) for v in (dq, dk, dv)], axis=1).reshape(960, rows)

    with jax.named_scope("sd"):
        line_d = SumZ(near_d.whole(), far_d.whole())
    mixed_far = attention_back(1, *sent_d)
    (result,) = by_rows(
        "result", [after(middle, mixed_far), feed, feed_other, norm_vectors], [(width, BF)], result_step
    )
    with jax.named_scope("sd"):
        line_d.take(result)
    with jax.named_scope("rows_out"):
        block_out, out_pieces = rows_out(after(result, *line_d.moved), start, c, z)
    grads_far = first_grads(a_one, after(grad_branch, result), mixed_far, saved[1][3], inner)
    with jax.named_scope("su"):
        far_u.add(grads_far)
        near_u.add(grads_far)
        sent_u = [far_u.send(), near_u.send()]
    mixed_near = attention_back(0, *one_u, grads_far)
    with jax.named_scope("su"):
        far_u.add(mixed_near)
        near_u.add(mixed_near)
        line_u = SumZ(near_u.whole(), far_u.whole())
    (part,) = product(
        "qkv_back",
        [(after(mixed_near, *sent_u), 0, qkv_wa, 1), (mixed_far, 0, qkv_wb, 1)],
        [(width, BF)],
        same,
    )
    part_other = swap_core(part, *out_pieces)
    grads_near = first_grads(a_one, after(grad_branch, part, *out_pieces), mixed_near, saved[0][3], inner)
    with jax.named_scope("sq"):
        near_q, far_q = Scatter(grads_near, back, g, count), Scatter(grads_far, forth, g, count)
        one_q = [far_q.send(grads_near), near_q.send(grads_near)]
    bias_qkv = [jnp.sum(v, axis=1, dtype=F32) for v in (mixed_near, mixed_far)]
    grad_source, *sums_one = by_rows(
        "norm_back",
        [part, part_other, after(source, grads_near), grad_branch, norm_vectors],
        [(width, BF), (width,), (width,)],
        first_back_step,
    )
    with jax.named_scope("su"):
        line_u.take(grad_source)
    with jax.named_scope("rows_dx"):
        input_grad, dx_pieces = rows_out(grad_source, start, c, z)
        input_grad = input_grad.astype(F32)
    with jax.named_scope("sq"):
        far_q.add(grad_source)
        near_q.add(grad_source)
        sent_q = [far_q.send(), near_q.send()]
        far_q.add(*dx_pieces)
        near_q.add(*dx_pieces)
        line_q = SumZ(near_q.whole(), far_q.whole())
        line_q.take()
        grad_first = line_q.whole()
    with jax.named_scope("sd"):
        grad_down = line_d.whole(*dx_pieces)
    with jax.named_scope("su"):
        grad_up = line_u.whole(*dx_pieces)

    vector_grad = 0.5 * jnp.concatenate(sums_one + sums_two, axis=0)
    bias_up = [after(v, *sent_q) for v in bias_up]
    far_zero = jnp.where(z < 2, 2, 1)
    far_one = jnp.where(z < 2, 3, 0)
    placed = jnp.zeros((7, 4, 320), F32)
    for index, place in enumerate((z, z ^ 1, far_zero, far_one)):
        qkv_sum = bias_qkv[index // 2].reshape(2, 3, 1, 160)[index % 2]
        up_sum = bias_up[index // 2].reshape(2, 2, 1, 320)[index % 2]
        placed = lax.dynamic_update_slice(placed, qkv_sum, (0, place, c * 160))
        placed = lax.dynamic_update_slice(placed, up_sum, (3 + 2 * c, place, 0))
    with jax.named_scope("vectors"):
        summed = add_up(
            after(jnp.concatenate([placed.reshape(7, 4 * 320), vector_grad], axis=0), *sent_q), count
        )
    grad_bias = lax.dynamic_slice(summed, (0, z * 320), (7, 320))
    grad_vector = summed[7:]

    first_split = grad_first.reshape(d_local, 2, 4, 160)
    grad_qkv = jnp.moveaxis(first_split[:, :, :3], 1, 2).reshape(d_local, 3, 320)
    grad_o = first_split[:, :, 3].reshape(d_local, 320).T
    grad_up = grad_up.reshape(d_local, 4, 320)
    grad_down = jnp.transpose(grad_down.reshape(d_local, 4, 320), (1, 2, 0))
    outputs = [block_out, input_grad]
    for weight, grad, first, second, rate, decay in (
        (qkv_weight, grad_qkv, qkv_first, qkv_second, MATRIX_RATE, MATRIX_DECAY),
        (out_weight, grad_o, out_first, out_second, MATRIX_RATE, MATRIX_DECAY),
        (up_projection_weight, grad_up, up_first, up_second, MATRIX_RATE, MATRIX_DECAY),
        (down_weight, grad_down, down_first, down_second, MATRIX_RATE, MATRIX_DECAY),
        (projection_bias_rows, grad_bias, bias_first, bias_second, VECTOR_RATE, 0.0),
        (norm_vectors, grad_vector, vector_first, vector_second, VECTOR_RATE, 0.0),
    ):
        outputs.extend(adam_step(weight, grad, first, second, rate, decay))
    return tuple(outputs)


def solution(mesh):
    devices = mesh.devices.reshape(mesh.shape["dp"] // 2, 2, mesh.shape["tensor"])
    own_mesh = Mesh(devices, ("g", "c", "z"))
    rows = P(("g", "c"), "z", None)
    in_weights = (P(("g", "c"), None, "z"), P("z", ("g", "c")), P(("g", "c"), None, "z"), P(None, "z", ("g", "c")))
    vectors = (P(None, "z"), P())
    params = in_weights + vectors
    out_specs = [rows, rows]
    for spec in params:
        out_specs.extend([spec] * 3)
    return jax.shard_map(
        body,
        mesh=own_mesh,
        in_specs=(rows, rows, P(("g", "c"), "z"), P(None, ("g", "c"), "z")) + params * 3,
        out_specs=tuple(out_specs),
        check_vma=False,
    )
```

```python
import functools

import jax
import jax.numpy as jnp
from jax import lax
from jax.experimental import pallas as pl
from jax.experimental.pallas import tpu as pltpu
from jax.sharding import Mesh, PartitionSpec as P

HEAD = 80
HALF = HEAD // 2
STEP = 10
MIDDLE = 1024

NORM_EPS = 1e-06
BETA_ONE = 0.9
BETA_TWO = 0.95
ADAM_EPS = 1e-08
MATRIX_RATE = 0.03
VECTOR_RATE = 0.2
MATRIX_DECAY = 0.1
GELU_SLOPE = 1.702
LOG2E = 1.4426950408889634
LN2 = 0.6931471805599453

BF = jnp.bfloat16
F32 = jnp.float32


def dot(left, right, left_dim, right_dim):
    return lax.dot_general(
        left, right, (((left_dim,), (right_dim,)), ((), ())), preferred_element_type=F32
    )


def normalise(source):
    centre = source - jnp.mean(source, axis=-1, keepdims=True)
    spread = lax.rsqrt(jnp.mean(centre * centre, axis=-1, keepdims=True) + NORM_EPS)
    return centre * spread, spread


def norm_back(gradient, gain_vec, normed, spread):
    scaled = gradient * gain_vec
    return spread * (
        scaled
        - jnp.mean(scaled, axis=-1, keepdims=True)
        - normed * jnp.mean(scaled * normed, axis=-1, keepdims=True)
    )


def adam_step(weight, gradient, first, second, rate, decay):
    first_new = BETA_ONE * first + (1.0 - BETA_ONE) * gradient
    second_new = BETA_TWO * second + (1.0 - BETA_TWO) * gradient * gradient
    fix_one = 1.0 - BETA_ONE**STEP
    fix_two = 1.0 - BETA_TWO**STEP
    ratio = first_new / fix_one / (jnp.sqrt(second_new / fix_two) + ADAM_EPS)
    return (weight - rate * (ratio + decay * weight), first_new, second_new)


def after(value, *earlier):
    return lax.optimization_barrier((value, *earlier))[0]


def move(value, axis, pairs, *earlier):
    return lax.ppermute(after(value, *earlier) if earlier else value, axis, pairs)


def swap_core(value, *earlier):
    return move(value, "c", [(0, 1), (1, 0)], *earlier)


def swap_bit(value, bit, count, *earlier):
    return move(value, "g", [(i, i ^ (1 << bit)) for i in range(count)], *earlier)


class Gather:
    def __init__(self, block, order, g, count):
        self.rows, self.columns = block.shape
        self.order, self.g, self.count = list(order), g, count
        self.bits = len(self.order)
        self.current = block.reshape((1,) * self.bits + block.shape)
        self.other = None

    def take(self, *earlier):
        if self.other is None:
            return
        other = after(self.other, *earlier) if earlier else self.other
        upper = ((self.g >> self.bit) & 1) == 1
        mine = self.current
        self.current = jnp.concatenate(
            [jnp.where(upper, other, mine), jnp.where(upper, mine, other)], axis=self.bits - 1 - self.bit
        )
        self.other = None

    def step(self, *earlier):
        self.take()
        if self.order:
            self.bit = self.order.pop(0)
            self.other = swap_bit(self.current, self.bit, self.count, *earlier)
            return self.other
        return self.current

    def finish(self, *earlier):
        last = self.step(*earlier)
        while self.order:
            last = self.step()
        return last

    def whole(self):
        self.take()
        return self.current.reshape(self.count * self.rows, self.columns)


class Scatter:
    def __init__(self, full, order, g, count):
        self.rows, self.columns = full.shape[0] // count, full.shape[1]
        self.order, self.g, self.count = list(order), g, count
        self.bits = len(self.order)
        self.terms = [full.reshape((2,) * self.bits + (self.rows, self.columns))]

    def sliced(self, place, axis):
        return [lax.dynamic_slice_in_dim(v, place, 1, axis) for v in self.terms]

    def total(self, terms):
        out = terms[0].astype(F32)
        for term in terms[1:]:
            out = out + term.astype(F32)
        return out

    def send(self, *earlier):
        bit = self.order.pop(0)
        axis = self.bits - 1 - bit
        mine = (self.g >> bit) & 1
        sent = self.total(self.sliced(1 - mine, axis)).astype(BF)
        self.kept = self.sliced(mine, axis)
        self.sent = sent
        self.got = swap_bit(sent, bit, self.count, *earlier)
        return self.got

    def add(self, *earlier):
        self.terms = self.kept + [after(self.got, *earlier) if earlier else self.got]
        while len(self.order) > 1:
            self.send()
            self.terms = self.kept + [self.got]

    def whole(self):
        return self.total(self.terms).reshape(self.rows, self.columns)


def row_moves(step):
    moves = []
    for c in range(2):
        for z in range(4):
            moves.append((c * 4 + z, (z >> 1) * 4 + 2 * c + ((z & 1) ^ step)))
    return [(a, b) for a, b in moves if a != b]


class RowsIn:
    def __init__(self, local, c, z):
        self.local, self.odd, self.stays = local, (z & 1) == 1, (z >> 1) == c
        self.pieces = []

    def send(self, *earlier):
        step = len(self.pieces)
        sent = jnp.where(self.odd, self.local[1 - step], self.local[step])
        self.sent = sent
        self.first = sent if step == 0 else self.first
        self.pieces.append(move(sent, ("c", "z"), row_moves(step), *earlier))
        return self.pieces[-1]

    def half(self, *earlier):
        first, second = [after(v, *earlier) if earlier else v for v in self.pieces]
        first = jnp.where(self.stays, self.first, first)
        return jnp.concatenate(
            [jnp.where(self.odd, second, first), jnp.where(self.odd, first, second)], axis=0
        )


def rows_out(turned, start, c, z, chained=False):
    rows, width = turned.shape
    part = rows // 4
    odd = z & 1
    longer = jnp.concatenate([turned, turned[:part]], axis=0)
    pieces, sents = [], []
    for step in range(2):
        first = lax.rem((2 * c + (odd ^ step)) * part - start + rows, rows)
        sent = lax.dynamic_slice(longer, (first, 0), (part, width))
        sents.append(sent)
        back = [(b, a) for a, b in row_moves(step)]
        pieces.append(move(sent, ("c", "z"), back, *(pieces if chained else [])))
    first, second = jnp.where((z >> 1) == c, sents[0], pieces[0]), pieces[1]
    return jnp.stack([jnp.where(odd == 1, second, first), jnp.where(odd == 1, first, second)]), pieces, sents


def turn_rows(start, upper, lower, vectors=None):
    half, width = upper.shape
    rows = 2 * half
    block = 256
    more = block + 16

    def kernel(start_ref, up_ref, low_ref, *refs):
        wide = refs[-1]
        for at in range(0, half, block):
            wide[at : at + block] = up_ref[at : at + block].astype(F32)
            wide[half + at : half + at + block] = low_ref[at : at + block].astype(F32)
        wide[rows : rows + more] = up_ref[:more].astype(F32)

        @pl.loop(0, rows // block)
        def _(i):
            at = i * block
            first = lax.rem(at + start_ref[0], rows)
            low = lax.rem(first, 8)
            value = wide[pl.ds(pl.multiple_of(first - low, 8), more)]
            value = pltpu.roll(value, lax.rem(more - low, more), 0)[:block]
            into = pl.ds(pl.multiple_of(at, block), block)
            if vectors is None:
                refs[0][into] = value.astype(BF)
            else:
                refs[1][into] = value.astype(BF)
                refs[2][into] = first_norm_step(value, refs[0][...])[0].astype(BF)

    outs = 1 if vectors is None else 2
    extra = [] if vectors is None else [vectors]
    return pl.pallas_call(
        kernel,
        in_specs=[pl.BlockSpec(memory_space=pltpu.SMEM)]
        + [pl.BlockSpec(memory_space=pltpu.VMEM)] * (2 + len(extra)),
        out_specs=[pl.BlockSpec(memory_space=pltpu.VMEM)] * outs,
        out_shape=[jax.ShapeDtypeStruct((rows, width), BF)] * outs,
        scratch_shapes=[pltpu.VMEM((rows + more, width), F32)],
        compiler_params=pltpu.CompilerParams(vmem_limit_bytes=40 * 2**20),
        cost_estimate=FREE,
        name="turn_rows",
    )(start[None], upper, lower, *extra)


def add_up(value, count, first, then):
    value = value + swap_core(value, *first)
    for bit in range(count.bit_length() - 1):
        value = value + swap_bit(value, bit, count)
    value = after(value, *then)
    for distance in (1, 2):
        value = value + lax.ppermute(value, "z", [(i, i ^ distance) for i in range(4)])
    return value


SEGMENTS = ((0, MIDDLE, False), (MIDDLE, None, True))


def attend_kernel(q_ref, k_ref, v_ref, cos_ref, sin_ref, mask_ref, qt_ref, kt_ref, vt_ref, ot_ref, lse_ref, *, block):
    cosine, sine = cos_ref[...], sin_ref[...]

    def turn(source, factor):
        first, second = source[:HALF], source[HALF:]
        return (
            jnp.concatenate([first * cosine - second * sine, second * cosine + first * sine], axis=0) * factor
        ).astype(BF)

    rows = q_ref.shape[1]
    qt = turn(q_ref[...], LOG2E * HEAD ** (-0.5))
    kt = turn(k_ref[...], 1.0)
    vt = v_ref[...].astype(BF)
    qt_ref[0] = qt
    kt_ref[0] = kt
    vt_ref[0] = vt
    for first, last, masked in ((0, MIDDLE, False), (MIDDLE, rows, True)):
        keys = kt[:, first:last]
        values = vt[:, first:last]
        for at in range(first, last, block):
            scores = dot(keys, qt[:, at : at + block], 0, 0)
            if masked:
                scores = scores + mask_ref[:, at - first : at - first + block]
            largest = jnp.max(scores, axis=0, keepdims=True)
            raised = jnp.exp2(scores - largest)
            total = jnp.sum(raised, axis=0, keepdims=True)
            mixed = dot(values, raised.astype(BF), 1, 0)
            ot_ref[:, at : at + block] = (mixed / total).astype(BF)
            lse_ref[0, :, at : at + block] = largest + jnp.log2(total)


def attend_back_kernel(qt_ref, kt_ref, vt_ref, ot_ref, dot_ref, lse_ref, cos_ref, sin_ref, mask_ref, dq_ref, dk_ref, dv_ref, *, block):
    cosine, sine = cos_ref[...], sin_ref[...]

    def turn_back(grad, factor):
        first, second = grad[:HALF] * factor, grad[HALF:] * factor
        return jnp.concatenate([first * cosine + second * sine, second * cosine - first * sine], axis=0).astype(BF)

    rows = cos_ref.shape[1]
    qt, kt, vt, dot_ = qt_ref[0], kt_ref[0], vt_ref[0], dot_ref[...]
    delta = jnp.sum(dot_.astype(F32) * ot_ref[...].astype(F32), axis=0, keepdims=True)
    lse = lse_ref[0]
    queries = qt.astype(F32).T.astype(BF)
    grads = dot_.astype(F32).T.astype(BF)
    dq_parts, dk_parts, dv_parts = [], [], []
    for first, last, masked in ((0, MIDDLE, False), (MIDDLE, rows, True)):
        keys = kt[:, first:last]
        values = vt[:, first:last]
        dk = dv = None
        for at in range(first, last, block):
            sl = slice(at, at + block)
            scores = dot(keys, qt[:, sl], 0, 0)
            if masked:
                scores = scores + mask_ref[:, at - first : at - first + block]
            chances = jnp.exp2(scores - lse[:, sl])
            grad_chances = dot(values, dot_[:, sl], 0, 0)
            grad_scores = (chances * (grad_chances - delta[:, sl])).astype(BF)
            dv_part = dot(chances.astype(BF), grads[sl], 1, 0)
            dk_part = dot(grad_scores, queries[sl], 1, 0)
            dv = dv_part if dv is None else dv + dv_part
            dk = dk_part if dk is None else dk + dk_part
            dq_parts.append(dot(keys, grad_scores, 1, 0))
        dk_parts.append(dk.T)
        dv_parts.append(dv.T)
    dq_ref[0] = turn_back(jnp.concatenate(dq_parts, axis=1), HEAD ** (-0.5))
    dk_ref[0] = turn_back(jnp.concatenate(dk_parts, axis=1), LN2)
    dv_ref[0] = jnp.concatenate(dv_parts, axis=1).astype(BF)


def attend(mixed, cosine, sine, mask):
    rows = mixed.shape[1]
    heads = 4
    once = lambda shape: pl.BlockSpec(shape, lambda h: (0, 0))
    part = lambda which: pl.BlockSpec((HEAD, rows), lambda h: ((h // 2) * 8 + 2 * which + h % 2, 0))
    each = pl.BlockSpec((1, HEAD, rows), lambda h: (h, 0, 0))
    return pl.pallas_call(
        functools.partial(attend_kernel, block=256),
        grid=(heads,),
        in_specs=[part(0), part(1), part(2), once(cosine.shape), once(sine.shape), once(mask.shape)],
        out_specs=[
            each,
            each,
            each,
            pl.BlockSpec((HEAD, rows), lambda h: (h, 0)),
            pl.BlockSpec((1, 1, rows), lambda h: (h, 0, 0)),
        ],
        out_shape=[jax.ShapeDtypeStruct((heads, HEAD, rows), BF)] * 3
        + [
            jax.ShapeDtypeStruct((heads * HEAD, rows), BF),
            jax.ShapeDtypeStruct((heads, 1, rows), F32),
        ],
        compiler_params=pltpu.CompilerParams(vmem_limit_bytes=40 * 2**20),
        cost_estimate=FREE,
        name="attend",
    )(mixed, mixed, mixed, cosine, sine, mask)


def attend_back(saved, grad_mixed, cosine, sine, mask):
    qt, kt, vt, mixed, lse = saved
    heads, _, rows = qt.shape
    once = lambda shape: pl.BlockSpec(shape, lambda h: (0, 0))
    each = pl.BlockSpec((1, HEAD, rows), lambda h: (h, 0, 0))
    flat = pl.BlockSpec((HEAD, rows), lambda h: (h, 0))
    return pl.pallas_call(
        functools.partial(attend_back_kernel, block=256),
        grid=(heads,),
        in_specs=[
            each,
            each,
            each,
            flat,
            flat,
            pl.BlockSpec((1, 1, rows), lambda h: (h, 0, 0)),
            once(cosine.shape),
            once(sine.shape),
            once(mask.shape),
        ],
        out_specs=[each, each, each],
        out_shape=[jax.ShapeDtypeStruct((heads, HEAD, rows), BF)] * 3,
        compiler_params=pltpu.CompilerParams(vmem_limit_bytes=50 * 2**20),
        cost_estimate=FREE,
        name="attend_back",
    )(qt, kt, vt, mixed, grad_mixed, lse, cosine, sine, mask)


FREE = pl.CostEstimate(flops=0, bytes_accessed=0, transcendentals=0)
BLOCK = 256


def params(mib=48):
    return pltpu.CompilerParams(vmem_limit_bytes=mib * 2**20, dimension_semantics=("arbitrary",))


def whole(shape):
    return pl.BlockSpec(shape, lambda i: (0,) * len(shape))


def rows_of(width, block=BLOCK):
    return pl.BlockSpec((block, width), lambda i: (i, 0))


def columns_of(height, block=BLOCK):
    return pl.BlockSpec((height, block), lambda i: (0, i))


def product(name, pairs, outs, finish, extras=(), block=None):
    size = pairs[0][0].shape[1 - pairs[0][1]]
    block = block or (640 if size % 640 == 0 else 512 if size % 512 == 0 else BLOCK)
    in_specs, operands = [], []
    for left, left_dim, right, _ in pairs:
        in_specs.append(rows_of(left.shape[1], block) if left_dim == 1 else columns_of(left.shape[0], block))
        in_specs.append(whole(right.shape))
        operands.extend([left, right])
    for value in extras:
        in_specs.append(rows_of(value.shape[1], block) if value.shape[0] == size else whole(value.shape))
        operands.append(value)
    out_specs, out_shape = [], []
    for out in outs:
        if len(out) == 2:
            out_specs.append(rows_of(out[0], block))
            out_shape.append(jax.ShapeDtypeStruct((size, out[0]), out[1]))
        else:
            out_specs.append(whole((1, out[0])))
            out_shape.append(jax.ShapeDtypeStruct((1, out[0]), F32))

    def kernel(*refs):
        total = None
        for i, (_, left_dim, _, right_dim) in enumerate(pairs):
            term = dot(refs[2 * i][...], refs[2 * i + 1][...], left_dim, right_dim)
            total = term if total is None else total + term
        at = 2 * len(pairs)
        values = finish(total, *[r[...] for r in refs[at : at + len(extras)]])
        store(values, refs[at + len(extras) :], outs)

    return pl.pallas_call(
        kernel,
        grid=(size // block,),
        in_specs=in_specs,
        out_specs=out_specs,
        out_shape=out_shape,
        compiler_params=params(),
        cost_estimate=FREE,
        name=name,
    )(*operands)


def store(values, refs, outs):
    for value, ref, out in zip(values, refs, outs):
        if len(out) == 2:
            ref[...] = value.astype(out[1])
        else:
            summed = jnp.sum(value, axis=0, keepdims=True)

            @pl.when(pl.program_id(0) == 0)
            def _():
                ref[...] = summed

            @pl.when(pl.program_id(0) > 0)
            def _():
                ref[...] += summed


def by_rows(name, inputs, outs, step, block=256):
    size = inputs[0].shape[0]
    in_specs = [rows_of(v.shape[1], block) if v.shape[0] == size else whole(v.shape) for v in inputs]
    out_specs, out_shape = [], []
    for out in outs:
        if len(out) == 2:
            out_specs.append(rows_of(out[0], block))
            out_shape.append(jax.ShapeDtypeStruct((size, out[0]), out[1]))
        else:
            out_specs.append(whole((1, out[0])))
            out_shape.append(jax.ShapeDtypeStruct((1, out[0]), F32))

    def kernel(*refs):
        values = step(*[r[...] for r in refs[: len(inputs)]])
        store(values, refs[len(inputs) :], outs)

    return pl.pallas_call(
        kernel,
        grid=(size // block,),
        in_specs=in_specs,
        out_specs=out_specs,
        out_shape=out_shape,
        compiler_params=params(),
        cost_estimate=FREE,
        name=name,
    )(*inputs)


def first_norm_step(source, vectors):
    hat, _ = normalise(source.astype(F32))
    return (hat * vectors[0:1] + vectors[1:2],)


def second_norm_step(source, part, other, vectors):
    middle = source.astype(F32) + (part.astype(F32) + other.astype(F32)) + vectors[4:5]
    hat, _ = normalise(middle)
    return middle, hat * vectors[2:3] + vectors[3:4]


def second_back_step(part, other, middle, grad_out, vectors):
    grad = part.astype(F32) + other.astype(F32)
    hat, scale = normalise(middle.astype(F32))
    out = grad_out.astype(F32)
    grad_middle = out + norm_back(grad, vectors[2:3], hat, scale)
    return grad_middle, grad_middle, grad * hat, grad, grad_middle, out


def first_back_step(part, other, source, grad_middle, vectors):
    grad = part.astype(F32) + other.astype(F32)
    hat, scale = normalise(source.astype(F32))
    return grad_middle.astype(F32) + norm_back(grad, vectors[0:1], hat, scale), grad * hat, grad


def result_step(middle, part, other, vectors):
    return (middle.astype(F32) + (part.astype(F32) + other.astype(F32)) + vectors[5:6],)


def hidden_step(total, bias):
    hidden = total + bias
    gate = 1.0 / (1.0 + jnp.exp(-GELU_SLOPE * hidden))
    return hidden * gate, gate + GELU_SLOPE * hidden * gate * (1.0 - gate)


def hidden_back_step(total, slope):
    grad = (total * slope.astype(F32)).astype(BF)
    return grad, grad.astype(F32)


def feed_back(grad_rows, down, up, slopes):
    size, width = grad_rows.shape
    hidden = slopes[0].shape[1]

    def kernel(g_ref, da_ref, db_ref, ua_ref, ub_ref, sa_ref, sb_ref, ha_ref, hb_ref, part_ref, suma_ref, sumb_ref):
        total = None
        for d_ref, u_ref, s_ref, h_ref, sum_ref in (
            (da_ref, ua_ref, sa_ref, ha_ref, suma_ref),
            (db_ref, ub_ref, sb_ref, hb_ref, sumb_ref),
        ):
            grad = (dot(g_ref[...], d_ref[...], 1, 0) * s_ref[...].astype(F32)).astype(BF)
            h_ref[...] = grad
            store((grad.astype(F32),), (sum_ref,), ((hidden,),))
            term = dot(grad, u_ref[...], 1, 1)
            total = term if total is None else total + term
        part_ref[...] = total.astype(BF)

    weight = whole((width, hidden))
    return pl.pallas_call(
        kernel,
        grid=(size // 512,),
        in_specs=[rows_of(width, 512)] + [weight] * 4 + [rows_of(hidden, 512)] * 2,
        out_specs=[rows_of(hidden, 512)] * 2 + [rows_of(width, 512)] + [whole((1, hidden))] * 2,
        out_shape=[jax.ShapeDtypeStruct((size, hidden), BF)] * 2
        + [jax.ShapeDtypeStruct((size, width), BF)]
        + [jax.ShapeDtypeStruct((1, hidden), F32)] * 2,
        compiler_params=params(60),
        cost_estimate=FREE,
        name="feed_back",
    )(grad_rows, *down, *up, *slopes)


def second_norm_back(part, other, middle, grad_rows, vectors, outs):
    size, width = part.shape
    inner = outs[0].shape[1]

    def kernel(p_ref, o_ref, m_ref, g_ref, v_ref, wa_ref, wb_ref, branch_ref, da_ref, db_ref, *sums):
        _, grad_middle, *terms = second_back_step(p_ref[...], o_ref[...], m_ref[...], g_ref[...], v_ref[...])
        branch = grad_middle.astype(BF)
        branch_ref[...] = branch
        for w_ref, d_ref in ((wa_ref, da_ref), (wb_ref, db_ref)):
            d_ref[...] = dot(w_ref[...], branch, 0, 1).astype(BF)
        store(terms, sums, ((width,),) * 4)

    return pl.pallas_call(
        kernel,
        grid=(size // BLOCK,),
        in_specs=[rows_of(width)] * 4 + [whole(vectors.shape)] + [whole((width, inner))] * 2,
        out_specs=[rows_of(width)] + [columns_of(inner)] * 2 + [whole((1, width))] * 4,
        out_shape=[jax.ShapeDtypeStruct((size, width), BF)]
        + [jax.ShapeDtypeStruct((inner, size), BF)] * 2
        + [jax.ShapeDtypeStruct((1, width), F32)] * 4,
        compiler_params=params(),
        cost_estimate=FREE,
        name="norm_two_back",
    )(part, other, middle, grad_rows, vectors, *outs)


def first_grads(a_one, grad_branch, grad_mixed, mixed, inner):
    rows, width = a_one.shape

    def kernel(a_ref, g_ref, m_ref, o_ref, out_ref):
        for slot in range(2):
            at = slot * inner
            out_ref[:, at : at + 480] = dot(a_ref[...], m_ref[slot * 480 : (slot + 1) * 480], 0, 1).astype(BF)
            out_ref[:, at + 480 : at + 640] = dot(g_ref[...], o_ref[slot * 160 : (slot + 1) * 160], 0, 1).astype(BF)

    return pl.pallas_call(
        kernel,
        grid=(width // BLOCK,),
        in_specs=[columns_of(rows), columns_of(rows), whole(grad_mixed.shape), whole(mixed.shape)],
        out_specs=rows_of(2 * inner),
        out_shape=jax.ShapeDtypeStruct((width, 2 * inner), BF),
        compiler_params=params(),
        cost_estimate=FREE,
        name="first_grads",
    )(a_one, grad_branch, grad_mixed, mixed)


def pack(core, qkv, out, up, down, inner):
    rows = out.shape[0]

    def kernel(core_ref, qkv_ref, out_ref, up_ref, down_ref, keep_ref, give_ref):
        for ref, mine in ((keep_ref, core_ref[0]), (give_ref, 1 - core_ref[0])):
            low = mine == 0
            for i in range(3):
                value = qkv_ref[i]
                ref[:, i * 160 : (i + 1) * 160] = jnp.where(low, value[:, :160], value[:, 160:]).astype(BF)
            value = out_ref[...]
            ref[:, 480:640] = jnp.where(low, value[:, :160], value[:, 160:]).astype(BF)
            for j in range(2):
                ref[:, inner + j * 320 : inner + (j + 1) * 320] = jnp.where(
                    low, up_ref[:, j], up_ref[:, j + 2]
                ).astype(BF)
                ref[:, 2 * inner + j * 320 : 2 * inner + (j + 1) * 320] = jnp.where(
                    low, down_ref[j], down_ref[j + 2]
                ).astype(BF)

    return pl.pallas_call(
        kernel,
        in_specs=[pl.BlockSpec(memory_space=pltpu.SMEM)] + [pl.BlockSpec(memory_space=pltpu.VMEM)] * 4,
        out_specs=[pl.BlockSpec(memory_space=pltpu.VMEM)] * 2,
        out_shape=[jax.ShapeDtypeStruct((rows, 3 * inner), BF)] * 2,
        compiler_params=pltpu.CompilerParams(vmem_limit_bytes=40 * 2**20),
        cost_estimate=FREE,
        name="pack",
    )(core, qkv, out, up, down)


def body(
    tokens_in,
    cotangent,
    picture_ids,
    patch_positions,
    qkv_weight,
    out_weight,
    up_projection_weight,
    down_weight,
    projection_bias_rows,
    norm_vectors,
    qkv_first,
    out_first,
    up_first,
    down_first,
    bias_first,
    vector_first,
    qkv_second,
    out_second,
    up_second,
    down_second,
    bias_second,
    vector_second,
):
    count = lax.axis_size("g")
    bits = count.bit_length() - 1
    g, c, z = lax.axis_index("g"), lax.axis_index("c"), lax.axis_index("z")
    low_core = c == 0
    d_local = qkv_weight.shape[0]
    width = tokens_in.shape[2]
    part_rows = tokens_in.shape[1]
    inner = 640
    forth, back = tuple(range(bits)), tuple(reversed(range(bits)))

    with jax.named_scope("small"):
        bias_half = jnp.where(
            low_core,
            jnp.concatenate([projection_bias_rows[0:3, :160].reshape(480), projection_bias_rows[3:5].reshape(640)]),
            jnp.concatenate([projection_bias_rows[0:3, 160:].reshape(480), projection_bias_rows[5:7].reshape(640)]),
        )
        counted = jnp.concatenate([picture_ids[None], patch_positions], axis=0).astype(F32)
        small = jnp.concatenate([bias_half, counted.reshape(3 * 2 * part_rows)])[None]
        smalls = [lax.ppermute(small, "z", [(i, i ^ d) for i in range(4)]) for d in (1, 2, 3)]
        relative = jnp.concatenate([small] + smalls, axis=0)
        biases = relative[:, :1120]
        bias_near = biases[:2]
        bias_far = biases[2:]
        counted = relative[:, 1120:].reshape(4, 3, 2, part_rows)
        counted = jnp.where((z & 1) == 0, counted[:, :, 0], counted[:, :, 1])
        counted = jnp.concatenate([lax.dynamic_slice_in_dim(counted, k ^ z, 1, 0) for k in range(4)], axis=0)
        counted = jnp.where((z >> 1) == c, counted, swap_core(counted))
        counted = jnp.moveaxis(counted, 1, 0).reshape(3, 4 * part_rows)

    rows_x, rows_g = RowsIn(tokens_in, c, z), RowsIn(cotangent, c, z)
    with jax.named_scope("rows_x"):
        r0, r1 = rows_x.send(), rows_x.send()

    with jax.named_scope("pack"):
        keep, give_away = pack(
            after(c[None].astype(jnp.int32), rows_x.sent),
            jnp.transpose(qkv_weight, (1, 0, 2)),
            out_weight.T,
            up_projection_weight,
            jnp.transpose(down_weight, (0, 2, 1)),
            inner,
        )
        other = swap_core(give_away)
        shard = jnp.concatenate([jnp.where(low_core, keep, other), jnp.where(low_core, other, keep)], axis=0)
        shard_q, shard_u, shard_d = [shard[:, i * inner : (i + 1) * inner] for i in range(3)]

    def pair(first, second):
        return jnp.concatenate([first, second], axis=-1)

    def along(value, distance, *earlier):
        return move(value, "z", [(i, i ^ distance) for i in range(4)], *earlier)

    def gather(block, order):
        return Gather(block, order, g, count)

    def far_of(two, three):
        return jnp.where(is_mid, pair(three, two), pair(two, three))

    start = jnp.sum((counted[0] == 1).astype(jnp.int32))

    def halves_of(rows_half, *earlier):
        own = rows_half.half(*earlier)
        other = swap_core(own)
        return jnp.where(low_core, own, other), jnp.where(low_core, other, own)

    with jax.named_scope("near"):
        near_q = pair(shard_q, along(shard_q, 1))
        near_u = pair(shard_u, along(shard_u, 1))
        near_d = pair(shard_d, along(shard_d, 1, near_q))
    with jax.named_scope("far"):
        far_q = along(near_q, 2)
        far_u = along(near_u, 2)
    qa, ua, da = gather(near_q, forth), gather(near_u, back), gather(near_d, forth)
    with jax.named_scope("gx"):
        qax = qa.step()
        dax = da.step(qax)
    with jax.named_scope("gy"):
        uay = ua.step()
        qay = qa.finish(uay)
    with jax.named_scope("gx"):
        uax = ua.finish(dax)
    with jax.named_scope("rows_x"):
        source, a_one = turn_rows(start, *halves_of(rows_x, near_d), norm_vectors)
    qa.take(a_one)
    qb = gather(after(far_q, a_one), back)
    with jax.named_scope("gy"):
        qby = qb.step(qay)
    with jax.named_scope("far"):
        far_d = along(near_d, 2, qay, uax)
    with jax.named_scope("gx"):
        qbx = qb.finish(uax)
    with jax.named_scope("gy"):
        day = da.finish(qby)

    first_wa = qa.whole()
    counted = jnp.roll(counted, -start, axis=1)
    ids = counted[0, MIDDLE:]
    mask = jnp.where(ids[:, None] == ids[None, :], 0.0, -1e30).astype(F32)
    powers = jnp.arange(HEAD // 4, dtype=F32) * (2.0 / (HEAD // 2))
    inverse = jnp.power(10000.0, -powers)
    angles = jnp.concatenate([inverse[:, None] * counted[1][None], inverse[:, None] * counted[2][None]], axis=0)
    cosine, sine = jnp.cos(angles), jnp.sin(angles)
    rows = source.shape[0]

    def qkv_bias(pair):
        zero = jnp.zeros((160,), F32)
        return jnp.concatenate([pair[0, :480], zero, pair[1, :480], zero])

    mixed = dot(after(first_wa, qby), a_one, 0, 1) + qkv_bias(bias_near)[:, None]
    saved = [attend(mixed, cosine, sine, mask)]
    done = saved[0][3]
    qb.take(done)
    ub = gather(after(far_u, done), forth)
    with jax.named_scope("rows_g"):
        rows_g.send(far_u, done)
        rows_g.send(far_u, done)
    with jax.named_scope("gx"):
        ubx = ub.step(qbx)
    db = gather(after(far_d, done, qbx), back)
    with jax.named_scope("gy"):
        dby = db.step(day)
    first_wb = qb.whole()
    mixed = dot(after(first_wb, day, far_d), a_one, 0, 1) + qkv_bias(bias_far)[:, None]
    saved.append(attend(mixed, cosine, sine, mask))
    done = saved[1][3]
    ub.take(done)
    db.take(done)
    with jax.named_scope("gy"):
        uby = ub.finish(dby)
    with jax.named_scope("gx"):
        dbx = db.finish(ubx)
    with jax.named_scope("rows_g"):
        (grad_rows,) = turn_rows(start, *halves_of(rows_g, ubx, dby, done))

    def out_part(weight):
        return jnp.concatenate([weight[:, 480:640], weight[:, 1120:1280]], axis=1)

    def qkv_part(weight):
        return jnp.concatenate([weight[:, :480], weight[:, 640:1120]], axis=1)

    out_wa, out_wb = out_part(first_wa), out_part(first_wb)
    qkv_wa, qkv_wb = qkv_part(first_wa), qkv_part(first_wb)
    same = lambda total: (total,)
    (branch,) = product(
        "out_product",
        [(saved[0][3], 0, out_wa, 1), (after(saved[1][3], ubx, dby), 0, out_wb, 1)],
        [(width, BF)],
        same,
    )
    middle, a_two = by_rows(
        "norm_two",
        [source, branch, swap_core(branch), norm_vectors],
        [(width, BF), (width, BF)],
        second_norm_step,
    )

    def feed_forward(weight, bias):
        return product(
            "up_product",
            [(a_two, 1, weight, 0)],
            [(2 * inner, BF), (2 * inner, BF)],
            hidden_step,
            [bias[:, 480:].reshape(1, 2 * inner)],
        )

    def down_grads(value):
        return product("down_grads", [(grad_rows, 0, value, 0)], [(2 * inner, BF)], same)[0]

    up_wa, down_wa = ua.whole(), da.whole()
    active_a, slope_a = feed_forward(up_wa, bias_near)
    grads_d_near = down_grads(active_a)
    ub.take(grads_d_near, qkv_wa, qkv_wb)
    db.take(grads_d_near)
    up_wb, down_wb = ub.whole(), db.whole()
    active_b, slope_b = feed_forward(up_wb, bias_far)
    grads_d_far = down_grads(active_b)
    active, slopes = (active_a, active_b), (slope_a, slope_b)

    def both_halves(own):
        upper, lower = own[:d_local], own[d_local:]
        keep = jnp.where(low_core, upper, lower)
        other = swap_core(jnp.where(low_core, lower, upper).astype(BF)).astype(F32)
        return jnp.stack([jnp.where(low_core, keep, other), jnp.where(low_core, other, keep)], axis=1)

    class SumZ:
        def __init__(self, near, far, *earlier):
            self.near = pair(near[:, :inner], far[:, :inner])
            self.moved = along(pair(near[:, inner:], far[:, inner:]).astype(BF), 1, *earlier)

        def step(self, *earlier):
            self.near = self.near + (after(self.moved, *earlier) if earlier else self.moved).astype(F32)
            self.moved = along(self.near[:, inner:].astype(BF), 2)
            return self.moved

        def whole(self, *earlier):
            moved = after(self.moved, *earlier) if earlier else self.moved
            return both_halves(self.near[:, :inner] + moved.astype(F32))

    grads_d = [grads_d_near, grads_d_far]
    with jax.named_scope("sd"):
        near_d, far_d = Scatter(grads_d[0], back, g, count), Scatter(grads_d[1], forth, g, count)
        one_d = [far_d.send(day, dbx), near_d.send(day, dbx)]
    *grad_hidden, part_u, sum_a, sum_b = feed_back(
        after(grad_rows, *grads_d), (down_wa, down_wb), (up_wa, up_wb), slopes
    )
    bias_up = [sum_a, sum_b]

    def up_grads(value, *earlier):
        return product("up_grads", [(after(a_two, *earlier), 0, value, 0)], [(2 * inner, BF)], same)[0]

    part_u_other = swap_core(part_u, *one_d)
    with jax.named_scope("sd"):
        far_d.add(part_u)
        near_d.add(part_u)
        sent_d = [far_d.send(*one_d), near_d.send(*one_d)]
    grads_u_far = up_grads(grad_hidden[1], far_d.sent, near_d.sent)
    grads_u_near = up_grads(grad_hidden[0], grads_u_far)
    with jax.named_scope("sd"):
        far_d.add(grads_u_near)
        near_d.add(grads_u_near)
        line_d = SumZ(near_d.whole(), far_d.whole())
        line_d_moved = line_d.moved
    with jax.named_scope("su"):
        near_u, far_u = Scatter(grads_u_near, back, g, count), Scatter(grads_u_far, forth, g, count)
        one_u = [far_u.send(*sent_d), near_u.send(*sent_d)]
    grad_branch, *grad_atts, sums_0, sums_1, sums_2, sums_3 = second_norm_back(
        part_u,
        part_u_other,
        after(middle, grads_u_near, *sent_d),
        grad_rows,
        norm_vectors,
        (out_wa, out_wb),
    )
    sums_two = [sums_0, sums_1, sums_2, sums_3]
    (feed,) = product(
        "down_product",
        [(active[0], 1, down_wa, 1), (after(active[1], grad_branch), 1, down_wb, 1)],
        [(width, BF)],
        same,
    )
    feed_other = jnp.concatenate(
        [swap_core(feed[i * rows // 3 : (i + 1) * rows // 3], line_d_moved) for i in range(3)], axis=0
    )

    def attention_back(i, *earlier):
        dq, dk, dv = attend_back(saved[i], after(grad_atts[i], *earlier), cosine, sine, mask)
        return jnp.stack([v.reshape(2, 160, rows) for v in (dq, dk, dv)], axis=1).reshape(960, rows)

    mixed_far = attention_back(1, feed)
    with jax.named_scope("su"):
        far_u.add(mixed_far)
        near_u.add(mixed_far)
        sent_u = [far_u.send(), near_u.send()]
    (result,) = by_rows(
        "result", [after(middle, mixed_far), feed, feed_other, norm_vectors], [(width, BF)], result_step
    )
    with jax.named_scope("rows_out"):
        block_out, out_pieces, out_sents = rows_out(result, start, c, z)
    grads_far = first_grads(a_one, after(grad_branch, *out_sents, *one_u), mixed_far, saved[1][3], inner)
    mixed_near = attention_back(0, grads_far)
    with jax.named_scope("su"):
        far_u.add(grads_far)
        near_u.add(grads_far)
        line_u = SumZ(near_u.whole(), far_u.whole())
        line_u_moved = line_u.moved
    with jax.named_scope("sd"):
        line_d.step(mixed_near)
    (part,) = product(
        "qkv_back",
        [(after(mixed_near, *sent_u), 0, qkv_wa, 1), (mixed_far, 0, qkv_wb, 1)],
        [(width, BF)],
        same,
    )
    part_other = jnp.concatenate(
        [swap_core(part[i * rows // 3 : (i + 1) * rows // 3], *out_pieces, line_u_moved) for i in range(3)], axis=0
    )
    grads_near = first_grads(a_one, after(grad_branch, part), mixed_near, saved[0][3], inner)
    with jax.named_scope("sq"):
        near_q, far_q = Scatter(grads_near, back, g, count), Scatter(grads_far, forth, g, count)
        one_q = [far_q.send(grads_near), near_q.send(grads_near)]
    bias_qkv = [jnp.sum(v, axis=1, dtype=F32) for v in (mixed_near, mixed_far)]
    grad_source, *sums_one = by_rows(
        "norm_back",
        [part, part_other, after(source, grads_near), grad_branch, norm_vectors],
        [(width, BF), (width,), (width,)],
        first_back_step,
    )
    with jax.named_scope("su"):
        line_u.step(grad_source)
    with jax.named_scope("rows_dx"):
        input_grad, dx_pieces, _ = rows_out(after(grad_source, line_u_moved), start, c, z, True)
        input_grad = input_grad.astype(F32)
    with jax.named_scope("sq"):
        far_q.add(grad_source)
        near_q.add(grad_source)
        sent_q = [far_q.send(), near_q.send()]
        far_q.add(dx_pieces[0])
        near_q.add(dx_pieces[0])
        line_q = SumZ(near_q.whole(), far_q.whole())
        moved_q = [line_q.moved, line_q.step()]
        grad_first = line_q.whole()
    with jax.named_scope("sd"):
        grad_down = after(line_d.whole(grad_source), *one_q)
    with jax.named_scope("su"):
        grad_up = after(line_u.whole(dx_pieces[0]), *one_q)

    vector_grad = 0.5 * jnp.concatenate(sums_one + sums_two, axis=0)
    bias_up = [after(v, *sent_q) for v in bias_up]
    placed = jnp.zeros((7, 4, 320), F32)
    for index, place in enumerate((z, z ^ 1, z ^ 2, z ^ 3)):
        qkv_sum = bias_qkv[index // 2].reshape(2, 3, 1, 160)[index % 2]
        up_sum = bias_up[index // 2].reshape(2, 2, 1, 320)[index % 2]
        placed = lax.dynamic_update_slice(placed, qkv_sum, (0, place, c * 160))
        placed = lax.dynamic_update_slice(placed, up_sum, (3 + 2 * c, place, 0))
    with jax.named_scope("vectors"):
        summed = add_up(
            jnp.concatenate([placed.reshape(7, 4 * 320), vector_grad], axis=0), count, moved_q[:1], moved_q + dx_pieces[1:]
        )
    grad_bias = lax.dynamic_slice(summed, (0, z * 320), (7, 320))
    grad_vector = summed[7:]

    first_split = grad_first.reshape(d_local, 2, 4, 160)
    grad_qkv = jnp.moveaxis(first_split[:, :, :3], 1, 2).reshape(d_local, 3, 320)
    grad_o = first_split[:, :, 3].reshape(d_local, 320).T
    grad_up = grad_up.reshape(d_local, 4, 320)
    grad_down = jnp.transpose(grad_down.reshape(d_local, 4, 320), (1, 2, 0))
    outputs = [block_out, input_grad]
    for weight, grad, first, second, rate, decay in (
        (qkv_weight, grad_qkv, qkv_first, qkv_second, MATRIX_RATE, MATRIX_DECAY),
        (out_weight, grad_o, out_first, out_second, MATRIX_RATE, MATRIX_DECAY),
        (up_projection_weight, grad_up, up_first, up_second, MATRIX_RATE, MATRIX_DECAY),
        (down_weight, grad_down, down_first, down_second, MATRIX_RATE, MATRIX_DECAY),
        (projection_bias_rows, grad_bias, bias_first, bias_second, VECTOR_RATE, 0.0),
        (norm_vectors, grad_vector, vector_first, vector_second, VECTOR_RATE, 0.0),
    ):
        outputs.extend(adam_step(weight, grad, first, second, rate, decay))
    return tuple(outputs)


def solution(mesh):
    devices = mesh.devices.reshape(mesh.shape["dp"] // 2, 2, mesh.shape["tensor"])
    own_mesh = Mesh(devices, ("g", "c", "z"))
    rows = P(("g", "c"), "z", None)
    in_weights = (P(("g", "c"), None, "z"), P("z", ("g", "c")), P(("g", "c"), None, "z"), P(None, "z", ("g", "c")))
    vectors = (P(None, "z"), P())
    params = in_weights + vectors
    out_specs = [rows, rows]
    for spec in params:
        out_specs.extend([spec] * 3)
    return jax.shard_map(
        body,
        mesh=own_mesh,
        in_specs=(rows, rows, P(("g", "c"), "z"), P(None, ("g", "c"), "z")) + params * 3,
        out_specs=tuple(out_specs),
        check_vma=False,
    )
```

```python
import functools

import jax
import jax.numpy as jnp
from jax import lax
from jax.experimental import pallas as pl
from jax.experimental.pallas import tpu as pltpu
from jax.sharding import Mesh, PartitionSpec as P

HEAD = 80
HALF = HEAD // 2
STEP = 10
MIDDLE = 1024

NORM_EPS = 1e-06
BETA_ONE = 0.9
BETA_TWO = 0.95
ADAM_EPS = 1e-08
MATRIX_RATE = 0.03
VECTOR_RATE = 0.2
MATRIX_DECAY = 0.1
GELU_SLOPE = 1.702
LOG2E = 1.4426950408889634
LN2 = 0.6931471805599453

BF = jnp.bfloat16
F32 = jnp.float32


def dot(left, right, left_dim, right_dim):
    return lax.dot_general(
        left, right, (((left_dim,), (right_dim,)), ((), ())), preferred_element_type=F32
    )


def normalise(source):
    centre = source - jnp.mean(source, axis=-1, keepdims=True)
    spread = lax.rsqrt(jnp.mean(centre * centre, axis=-1, keepdims=True) + NORM_EPS)
    return centre * spread, spread


def norm_back(gradient, gain_vec, normed, spread):
    scaled = gradient * gain_vec
    return spread * (
        scaled
        - jnp.mean(scaled, axis=-1, keepdims=True)
        - normed * jnp.mean(scaled * normed, axis=-1, keepdims=True)
    )


def adam_step(weight, gradient, first, second, rate, decay):
    first_new = BETA_ONE * first + (1.0 - BETA_ONE) * gradient
    second_new = BETA_TWO * second + (1.0 - BETA_TWO) * gradient * gradient
    fix_one = 1.0 - BETA_ONE**STEP
    fix_two = 1.0 - BETA_TWO**STEP
    ratio = first_new / fix_one / (jnp.sqrt(second_new / fix_two) + ADAM_EPS)
    return (weight - rate * (ratio + decay * weight), first_new, second_new)


def after(value, *earlier):
    return lax.optimization_barrier((value, *earlier))[0]


def move(value, axis, pairs, *earlier):
    return lax.ppermute(after(value, *earlier) if earlier else value, axis, pairs)


def swap_core(value, *earlier):
    return move(value, "c", [(0, 1), (1, 0)], *earlier)


def swap_bit(value, bit, count, *earlier):
    return move(value, "g", [(i, i ^ (1 << bit)) for i in range(count)], *earlier)


class Gather:
    def __init__(self, block, order, g, count):
        self.rows, self.columns = block.shape
        self.order, self.g, self.count = list(order), g, count
        self.bits = len(self.order)
        self.current = block.reshape((1,) * self.bits + block.shape)
        self.other = None

    def take(self, *earlier):
        if self.other is None:
            return
        other = after(self.other, *earlier) if earlier else self.other
        upper = ((self.g >> self.bit) & 1) == 1
        mine = self.current
        self.current = jnp.concatenate(
            [jnp.where(upper, other, mine), jnp.where(upper, mine, other)], axis=self.bits - 1 - self.bit
        )
        self.other = None

    def step(self, *earlier):
        self.take()
        if self.order:
            self.bit = self.order.pop(0)
            self.other = swap_bit(self.current, self.bit, self.count, *earlier)
            return self.other
        return self.current

    def finish(self, *earlier):
        last = self.step(*earlier)
        while self.order:
            last = self.step()
        return last

    def whole(self):
        self.take()
        return self.current.reshape(self.count * self.rows, self.columns)


class Scatter:
    def __init__(self, full, order, g, count):
        self.rows, self.columns = full.shape[0] // count, full.shape[1]
        self.order, self.g, self.count = list(order), g, count
        self.bits = len(self.order)
        self.terms = [full.reshape((2,) * self.bits + (self.rows, self.columns))]

    def sliced(self, place, axis):
        return [lax.dynamic_slice_in_dim(v, place, 1, axis) for v in self.terms]

    def total(self, terms):
        out = terms[0].astype(F32)
        for term in terms[1:]:
            out = out + term.astype(F32)
        return out

    def send(self, *earlier):
        bit = self.order.pop(0)
        axis = self.bits - 1 - bit
        mine = (self.g >> bit) & 1
        sent = self.total(self.sliced(1 - mine, axis)).astype(BF)
        self.kept = self.sliced(mine, axis)
        self.sent = sent
        self.got = swap_bit(sent, bit, self.count, *earlier)
        return self.got

    def add(self, *earlier):
        self.terms = self.kept + [after(self.got, *earlier) if earlier else self.got]
        while len(self.order) > 1:
            self.send()
            self.terms = self.kept + [self.got]

    def whole(self):
        return self.total(self.terms).reshape(self.rows, self.columns)


def row_moves(step):
    moves = []
    for c in range(2):
        for z in range(4):
            moves.append((c * 4 + z, (z >> 1) * 4 + 2 * c + ((z & 1) ^ step)))
    return [(a, b) for a, b in moves if a != b]


class RowsIn:
    def __init__(self, local, c, z):
        self.local, self.odd, self.stays = local, (z & 1) == 1, (z >> 1) == c
        self.pieces = []

    def send(self, *earlier):
        step = len(self.pieces)
        sent = jnp.where(self.odd, self.local[1 - step], self.local[step])
        self.sent = sent
        self.first = sent if step == 0 else self.first
        self.pieces.append(move(sent, ("c", "z"), row_moves(step), *earlier))
        return self.pieces[-1]

    def half(self, *earlier):
        first, second = [after(v, *earlier) if earlier else v for v in self.pieces]
        first = jnp.where(self.stays, self.first, first)
        return jnp.concatenate(
            [jnp.where(self.odd, second, first), jnp.where(self.odd, first, second)], axis=0
        )


def rows_out(turned, start, c, z, chained=False):
    rows, width = turned.shape
    part = rows // 4
    odd = z & 1
    longer = jnp.concatenate([turned, turned[:part]], axis=0)
    pieces, sents = [], []
    for step in range(2):
        first = lax.rem((2 * c + (odd ^ step)) * part - start + rows, rows)
        sent = lax.dynamic_slice(longer, (first, 0), (part, width))
        sents.append(sent)
        back = [(b, a) for a, b in row_moves(step)]
        pieces.append(move(sent, ("c", "z"), back, *(pieces if chained else [])))
    first, second = jnp.where((z >> 1) == c, sents[0], pieces[0]), pieces[1]
    return jnp.stack([jnp.where(odd == 1, second, first), jnp.where(odd == 1, first, second)]), pieces, sents


def turn_rows(start, upper, lower, vectors=None):
    half, width = upper.shape
    rows = 2 * half
    block = 256
    more = block + 16

    def kernel(start_ref, up_ref, low_ref, *refs):
        wide = refs[-1]
        for at in range(0, half, block):
            wide[at : at + block] = up_ref[at : at + block].astype(F32)
            wide[half + at : half + at + block] = low_ref[at : at + block].astype(F32)
        wide[rows : rows + more] = up_ref[:more].astype(F32)

        @pl.loop(0, rows // block)
        def _(i):
            at = i * block
            first = lax.rem(at + start_ref[0], rows)
            low = lax.rem(first, 8)
            value = wide[pl.ds(pl.multiple_of(first - low, 8), more)]
            value = pltpu.roll(value, lax.rem(more - low, more), 0)[:block]
            into = pl.ds(pl.multiple_of(at, block), block)
            if vectors is None:
                refs[0][into] = value.astype(BF)
            else:
                refs[1][into] = value.astype(BF)
                refs[2][into] = first_norm_step(value, refs[0][...])[0].astype(BF)

    outs = 1 if vectors is None else 2
    extra = [] if vectors is None else [vectors]
    return pl.pallas_call(
        kernel,
        in_specs=[pl.BlockSpec(memory_space=pltpu.SMEM)]
        + [pl.BlockSpec(memory_space=pltpu.VMEM)] * (2 + len(extra)),
        out_specs=[pl.BlockSpec(memory_space=pltpu.VMEM)] * outs,
        out_shape=[jax.ShapeDtypeStruct((rows, width), BF)] * outs,
        scratch_shapes=[pltpu.VMEM((rows + more, width), F32)],
        compiler_params=pltpu.CompilerParams(vmem_limit_bytes=40 * 2**20),
        cost_estimate=FREE,
        name="turn_rows",
    )(start[None], upper, lower, *extra)


def add_up(value, count, first, then):
    value = value + swap_core(value, *first)
    for bit in range(count.bit_length() - 1):
        value = value + swap_bit(value, bit, count)
    value = after(value, *then)
    for distance in (1, 2):
        value = value + lax.ppermute(value, "z", [(i, i ^ distance) for i in range(4)])
    return value


SEGMENTS = ((0, MIDDLE, False), (MIDDLE, None, True))


def attend_kernel(q_ref, k_ref, v_ref, cos_ref, sin_ref, mask_ref, qt_ref, kt_ref, vt_ref, ot_ref, lse_ref, *, block):
    cosine, sine = cos_ref[...], sin_ref[...]

    def turn(source, factor):
        first, second = source[:HALF], source[HALF:]
        return (
            jnp.concatenate([first * cosine - second * sine, second * cosine + first * sine], axis=0) * factor
        ).astype(BF)

    rows = q_ref.shape[1]
    qt = turn(q_ref[...], LOG2E * HEAD ** (-0.5))
    kt = turn(k_ref[...], 1.0)
    vt = v_ref[...].astype(BF)
    qt_ref[0] = qt
    kt_ref[0] = kt
    vt_ref[0] = vt
    for first, last, masked in ((0, MIDDLE, False), (MIDDLE, rows, True)):
        keys = kt[:, first:last]
        values = vt[:, first:last]
        for at in range(first, last, block):
            scores = dot(keys, qt[:, at : at + block], 0, 0)
            if masked:
                scores = scores + mask_ref[:, at - first : at - first + block]
            largest = jnp.max(scores, axis=0, keepdims=True)
            raised = jnp.exp2(scores - largest)
            total = jnp.sum(raised, axis=0, keepdims=True)
            mixed = dot(values, raised.astype(BF), 1, 0)
            ot_ref[:, at : at + block] = (mixed / total).astype(BF)
            lse_ref[0, :, at : at + block] = largest + jnp.log2(total)


def attend_back_kernel(qt_ref, kt_ref, vt_ref, ot_ref, dot_ref, lse_ref, cos_ref, sin_ref, mask_ref, dq_ref, dk_ref, dv_ref, *, block):
    cosine, sine = cos_ref[...], sin_ref[...]

    def turn_back(grad, factor):
        first, second = grad[:HALF] * factor, grad[HALF:] * factor
        return jnp.concatenate([first * cosine + second * sine, second * cosine - first * sine], axis=0).astype(BF)

    rows = cos_ref.shape[1]
    qt, kt, vt, dot_ = qt_ref[0], kt_ref[0], vt_ref[0], dot_ref[...]
    delta = jnp.sum(dot_.astype(F32) * ot_ref[...].astype(F32), axis=0, keepdims=True)
    lse = lse_ref[0]
    queries = qt.astype(F32).T.astype(BF)
    grads = dot_.astype(F32).T.astype(BF)
    dq_parts, dk_parts, dv_parts = [], [], []
    for first, last, masked in ((0, MIDDLE, False), (MIDDLE, rows, True)):
        keys = kt[:, first:last]
        values = vt[:, first:last]
        dk = dv = None
        for at in range(first, last, block):
            sl = slice(at, at + block)
            scores = dot(keys, qt[:, sl], 0, 0)
            if masked:
                scores = scores + mask_ref[:, at - first : at - first + block]
            chances = jnp.exp2(scores - lse[:, sl])
            grad_chances = dot(values, dot_[:, sl], 0, 0)
            grad_scores = (chances * (grad_chances - delta[:, sl])).astype(BF)
            dv_part = dot(chances.astype(BF), grads[sl], 1, 0)
            dk_part = dot(grad_scores, queries[sl], 1, 0)
            dv = dv_part if dv is None else dv + dv_part
            dk = dk_part if dk is None else dk + dk_part
            dq_parts.append(dot(keys, grad_scores, 1, 0))
        dk_parts.append(dk.T)
        dv_parts.append(dv.T)
    dq_ref[0] = turn_back(jnp.concatenate(dq_parts, axis=1), HEAD ** (-0.5))
    dk_ref[0] = turn_back(jnp.concatenate(dk_parts, axis=1), LN2)
    dv_ref[0] = jnp.concatenate(dv_parts, axis=1).astype(BF)


def attend(mixed, cosine, sine, mask):
    rows = mixed.shape[1]
    heads = 4
    once = lambda shape: pl.BlockSpec(shape, lambda h: (0, 0))
    part = lambda which: pl.BlockSpec((HEAD, rows), lambda h: ((h // 2) * 8 + 2 * which + h % 2, 0))
    each = pl.BlockSpec((1, HEAD, rows), lambda h: (h, 0, 0))
    return pl.pallas_call(
        functools.partial(attend_kernel, block=256),
        grid=(heads,),
        in_specs=[part(0), part(1), part(2), once(cosine.shape), once(sine.shape), once(mask.shape)],
        out_specs=[
            each,
            each,
            each,
            pl.BlockSpec((HEAD, rows), lambda h: (h, 0)),
            pl.BlockSpec((1, 1, rows), lambda h: (h, 0, 0)),
        ],
        out_shape=[jax.ShapeDtypeStruct((heads, HEAD, rows), BF)] * 3
        + [
            jax.ShapeDtypeStruct((heads * HEAD, rows), BF),
            jax.ShapeDtypeStruct((heads, 1, rows), F32),
        ],
        compiler_params=pltpu.CompilerParams(vmem_limit_bytes=40 * 2**20),
        cost_estimate=FREE,
        name="attend",
    )(mixed, mixed, mixed, cosine, sine, mask)


def attend_back(saved, grad_mixed, cosine, sine, mask):
    qt, kt, vt, mixed, lse = saved
    heads, _, rows = qt.shape
    once = lambda shape: pl.BlockSpec(shape, lambda h: (0, 0))
    each = pl.BlockSpec((1, HEAD, rows), lambda h: (h, 0, 0))
    flat = pl.BlockSpec((HEAD, rows), lambda h: (h, 0))
    return pl.pallas_call(
        functools.partial(attend_back_kernel, block=256),
        grid=(heads,),
        in_specs=[
            each,
            each,
            each,
            flat,
            flat,
            pl.BlockSpec((1, 1, rows), lambda h: (h, 0, 0)),
            once(cosine.shape),
            once(sine.shape),
            once(mask.shape),
        ],
        out_specs=[each, each, each],
        out_shape=[jax.ShapeDtypeStruct((heads, HEAD, rows), BF)] * 3,
        compiler_params=pltpu.CompilerParams(vmem_limit_bytes=50 * 2**20),
        cost_estimate=FREE,
        name="attend_back",
    )(qt, kt, vt, mixed, grad_mixed, lse, cosine, sine, mask)


FREE = pl.CostEstimate(flops=0, bytes_accessed=0, transcendentals=0)
BLOCK = 256


def params(mib=48):
    return pltpu.CompilerParams(vmem_limit_bytes=mib * 2**20, dimension_semantics=("arbitrary",))


def whole(shape):
    return pl.BlockSpec(shape, lambda i: (0,) * len(shape))


def rows_of(width, block=BLOCK):
    return pl.BlockSpec((block, width), lambda i: (i, 0))


def columns_of(height, block=BLOCK):
    return pl.BlockSpec((height, block), lambda i: (0, i))


def product(name, pairs, outs, finish, extras=(), block=None):
    size = pairs[0][0].shape[1 - pairs[0][1]]
    block = block or (640 if size % 640 == 0 else 512 if size % 512 == 0 else BLOCK)
    in_specs, operands = [], []
    for left, left_dim, right, _ in pairs:
        in_specs.append(rows_of(left.shape[1], block) if left_dim == 1 else columns_of(left.shape[0], block))
        in_specs.append(whole(right.shape))
        operands.extend([left, right])
    for value in extras:
        in_specs.append(rows_of(value.shape[1], block) if value.shape[0] == size else whole(value.shape))
        operands.append(value)
    out_specs, out_shape = [], []
    for out in outs:
        if len(out) == 2:
            out_specs.append(rows_of(out[0], block))
            out_shape.append(jax.ShapeDtypeStruct((size, out[0]), out[1]))
        else:
            out_specs.append(whole((1, out[0])))
            out_shape.append(jax.ShapeDtypeStruct((1, out[0]), F32))

    def kernel(*refs):
        total = None
        for i, (_, left_dim, _, right_dim) in enumerate(pairs):
            term = dot(refs[2 * i][...], refs[2 * i + 1][...], left_dim, right_dim)
            total = term if total is None else total + term
        at = 2 * len(pairs)
        values = finish(total, *[r[...] for r in refs[at : at + len(extras)]])
        store(values, refs[at + len(extras) :], outs)

    return pl.pallas_call(
        kernel,
        grid=(size // block,),
        in_specs=in_specs,
        out_specs=out_specs,
        out_shape=out_shape,
        compiler_params=params(),
        cost_estimate=FREE,
        name=name,
    )(*operands)


def product_in_thirds(name, pairs):
    size = pairs[0][0].shape[1 - pairs[0][1]]
    width = pairs[0][2].shape[1 - pairs[0][3]]
    block = size // 3
    in_specs, operands = [], []
    for left, left_dim, right, _ in pairs:
        in_specs.append(rows_of(left.shape[1], block) if left_dim == 1 else columns_of(left.shape[0], block))
        in_specs.append(whole(right.shape))
        operands.extend([left, right])

    def kernel(*refs):
        total = None
        for i, (_, left_dim, _, right_dim) in enumerate(pairs):
            term = dot(refs[2 * i][...], refs[2 * i + 1][...], left_dim, right_dim)
            total = term if total is None else total + term
        value = total.astype(BF)
        for k, ref in enumerate(refs[2 * len(pairs) :]):

            @pl.when(pl.program_id(0) == k)
            def _(ref=ref):
                ref[...] = value

    return pl.pallas_call(
        kernel,
        grid=(3,),
        in_specs=in_specs,
        out_specs=[whole((block, width))] * 3,
        out_shape=[jax.ShapeDtypeStruct((block, width), BF)] * 3,
        compiler_params=params(),
        cost_estimate=FREE,
        name=name,
    )(*operands)


def store(values, refs, outs):
    for value, ref, out in zip(values, refs, outs):
        if len(out) == 2:
            ref[...] = value.astype(out[1])
        else:
            summed = jnp.sum(value, axis=0, keepdims=True)

            @pl.when(pl.program_id(0) == 0)
            def _():
                ref[...] = summed

            @pl.when(pl.program_id(0) > 0)
            def _():
                ref[...] += summed


def by_rows(name, inputs, outs, step, block=256):
    size = inputs[0].shape[0] if not isinstance(inputs[0], (list, tuple)) else 3 * inputs[0][0].shape[0]
    count = size // block
    each = count // 3
    in_specs, operands = [], []
    for value in inputs:
        if isinstance(value, (list, tuple)):
            for k, third in enumerate(value):
                operands.append(third)
                in_specs.append(
                    pl.BlockSpec(
                        (block, third.shape[1]), lambda i, k=k: (jnp.clip(i - each * k, 0, each - 1), 0)
                    )
                )
        else:
            operands.append(value)
            in_specs.append(rows_of(value.shape[1], block) if value.shape[0] == size else whole(value.shape))
    out_specs, out_shape = [], []
    for out in outs:
        if len(out) == 2:
            out_specs.append(rows_of(out[0], block))
            out_shape.append(jax.ShapeDtypeStruct((size, out[0]), out[1]))
        else:
            out_specs.append(whole((1, out[0])))
            out_shape.append(jax.ShapeDtypeStruct((1, out[0]), F32))

    def kernel(*refs):
        place = pl.program_id(0)
        values, at = [], 0
        for value in inputs:
            if isinstance(value, (list, tuple)):
                one, two, three = [r[...] for r in refs[at : at + 3]]
                values.append(jnp.where(place < each, one, jnp.where(place < 2 * each, two, three)))
                at += 3
            else:
                values.append(refs[at][...])
                at += 1
        store(step(*values), refs[at:], outs)

    return pl.pallas_call(
        kernel,
        grid=(count,),
        in_specs=in_specs,
        out_specs=out_specs,
        out_shape=out_shape,
        compiler_params=params(),
        cost_estimate=FREE,
        name=name,
    )(*operands)


def first_norm_step(source, vectors):
    hat, _ = normalise(source.astype(F32))
    return (hat * vectors[0:1] + vectors[1:2],)


def second_norm_step(source, part, other, vectors):
    middle = source.astype(F32) + (part.astype(F32) + other.astype(F32)) + vectors[4:5]
    hat, _ = normalise(middle)
    return middle, hat * vectors[2:3] + vectors[3:4]


def second_back_step(part, other, middle, grad_out, vectors):
    grad = part.astype(F32) + other.astype(F32)
    hat, scale = normalise(middle.astype(F32))
    out = grad_out.astype(F32)
    grad_middle = out + norm_back(grad, vectors[2:3], hat, scale)
    return grad_middle, grad_middle, grad * hat, grad, grad_middle, out


def first_back_step(part, other, source, grad_middle, vectors):
    grad = part.astype(F32) + other.astype(F32)
    hat, scale = normalise(source.astype(F32))
    return grad_middle.astype(F32) + norm_back(grad, vectors[0:1], hat, scale), grad * hat, grad


def result_step(middle, part, other, vectors):
    return (middle.astype(F32) + (part.astype(F32) + other.astype(F32)) + vectors[5:6],)


def hidden_step(total, bias):
    hidden = total + bias
    gate = 1.0 / (1.0 + jnp.exp(-GELU_SLOPE * hidden))
    return hidden * gate, gate + GELU_SLOPE * hidden * gate * (1.0 - gate)


def hidden_back_step(total, slope):
    grad = (total * slope.astype(F32)).astype(BF)
    return grad, grad.astype(F32)


def feed_back(grad_rows, down, up, slopes):
    size, width = grad_rows.shape
    hidden = slopes[0].shape[1]

    def kernel(g_ref, da_ref, db_ref, ua_ref, ub_ref, sa_ref, sb_ref, ha_ref, hb_ref, part_ref, suma_ref, sumb_ref):
        total = None
        for d_ref, u_ref, s_ref, h_ref, sum_ref in (
            (da_ref, ua_ref, sa_ref, ha_ref, suma_ref),
            (db_ref, ub_ref, sb_ref, hb_ref, sumb_ref),
        ):
            grad = (dot(g_ref[...], d_ref[...], 1, 0) * s_ref[...].astype(F32)).astype(BF)
            h_ref[...] = grad
            store((grad.astype(F32),), (sum_ref,), ((hidden,),))
            term = dot(grad, u_ref[...], 1, 1)
            total = term if total is None else total + term
        part_ref[...] = total.astype(BF)

    weight = whole((width, hidden))
    return pl.pallas_call(
        kernel,
        grid=(size // 512,),
        in_specs=[rows_of(width, 512)] + [weight] * 4 + [rows_of(hidden, 512)] * 2,
        out_specs=[rows_of(hidden, 512)] * 2 + [rows_of(width, 512)] + [whole((1, hidden))] * 2,
        out_shape=[jax.ShapeDtypeStruct((size, hidden), BF)] * 2
        + [jax.ShapeDtypeStruct((size, width), BF)]
        + [jax.ShapeDtypeStruct((1, hidden), F32)] * 2,
        compiler_params=params(60),
        cost_estimate=FREE,
        name="feed_back",
    )(grad_rows, *down, *up, *slopes)


def second_norm_back(part, other, middle, grad_rows, vectors, outs):
    size, width = part.shape
    inner = outs[0].shape[1]

    def kernel(p_ref, o_ref, m_ref, g_ref, v_ref, wa_ref, wb_ref, branch_ref, da_ref, db_ref, *sums):
        _, grad_middle, *terms = second_back_step(p_ref[...], o_ref[...], m_ref[...], g_ref[...], v_ref[...])
        branch = grad_middle.astype(BF)
        branch_ref[...] = branch
        for w_ref, d_ref in ((wa_ref, da_ref), (wb_ref, db_ref)):
            d_ref[...] = dot(w_ref[...], branch, 0, 1).astype(BF)
        store(terms, sums, ((width,),) * 4)

    return pl.pallas_call(
        kernel,
        grid=(size // BLOCK,),
        in_specs=[rows_of(width)] * 4 + [whole(vectors.shape)] + [whole((width, inner))] * 2,
        out_specs=[rows_of(width)] + [columns_of(inner)] * 2 + [whole((1, width))] * 4,
        out_shape=[jax.ShapeDtypeStruct((size, width), BF)]
        + [jax.ShapeDtypeStruct((inner, size), BF)] * 2
        + [jax.ShapeDtypeStruct((1, width), F32)] * 4,
        compiler_params=params(),
        cost_estimate=FREE,
        name="norm_two_back",
    )(part, other, middle, grad_rows, vectors, *outs)


def first_grads(a_one, grad_branch, grad_mixed, mixed, inner):
    rows, width = a_one.shape

    def kernel(a_ref, g_ref, m_ref, o_ref, out_ref):
        for slot in range(2):
            at = slot * inner
            out_ref[:, at : at + 480] = dot(a_ref[...], m_ref[slot * 480 : (slot + 1) * 480], 0, 1).astype(BF)
            out_ref[:, at + 480 : at + 640] = dot(g_ref[...], o_ref[slot * 160 : (slot + 1) * 160], 0, 1).astype(BF)

    return pl.pallas_call(
        kernel,
        grid=(width // BLOCK,),
        in_specs=[columns_of(rows), columns_of(rows), whole(grad_mixed.shape), whole(mixed.shape)],
        out_specs=rows_of(2 * inner),
        out_shape=jax.ShapeDtypeStruct((width, 2 * inner), BF),
        compiler_params=params(),
        cost_estimate=FREE,
        name="first_grads",
    )(a_one, grad_branch, grad_mixed, mixed)


def pack(core, qkv, out, up, down, inner):
    rows = out.shape[0]

    def kernel(core_ref, qkv_ref, out_ref, up_ref, down_ref, keep_ref, give_ref):
        for ref, mine in ((keep_ref, core_ref[0]), (give_ref, 1 - core_ref[0])):
            low = mine == 0
            for i in range(3):
                value = qkv_ref[i]
                ref[:, i * 160 : (i + 1) * 160] = jnp.where(low, value[:, :160], value[:, 160:]).astype(BF)
            value = out_ref[...]
            ref[:, 480:640] = jnp.where(low, value[:, :160], value[:, 160:]).astype(BF)
            for j in range(2):
                ref[:, inner + j * 320 : inner + (j + 1) * 320] = jnp.where(
                    low, up_ref[:, j], up_ref[:, j + 2]
                ).astype(BF)
                ref[:, 2 * inner + j * 320 : 2 * inner + (j + 1) * 320] = jnp.where(
                    low, down_ref[j], down_ref[j + 2]
                ).astype(BF)

    return pl.pallas_call(
        kernel,
        in_specs=[pl.BlockSpec(memory_space=pltpu.SMEM)] + [pl.BlockSpec(memory_space=pltpu.VMEM)] * 4,
        out_specs=[pl.BlockSpec(memory_space=pltpu.VMEM)] * 2,
        out_shape=[jax.ShapeDtypeStruct((rows, 3 * inner), BF)] * 2,
        compiler_params=pltpu.CompilerParams(vmem_limit_bytes=40 * 2**20),
        cost_estimate=FREE,
        name="pack",
    )(core, qkv, out, up, down)


def body(
    tokens_in,
    cotangent,
    picture_ids,
    patch_positions,
    qkv_weight,
    out_weight,
    up_projection_weight,
    down_weight,
    projection_bias_rows,
    norm_vectors,
    qkv_first,
    out_first,
    up_first,
    down_first,
    bias_first,
    vector_first,
    qkv_second,
    out_second,
    up_second,
    down_second,
    bias_second,
    vector_second,
):
    count = lax.axis_size("g")
    bits = count.bit_length() - 1
    g, c, z = lax.axis_index("g"), lax.axis_index("c"), lax.axis_index("z")
    low_core = c == 0
    d_local = qkv_weight.shape[0]
    width = tokens_in.shape[2]
    part_rows = tokens_in.shape[1]
    inner = 640
    forth, back = tuple(range(bits)), tuple(reversed(range(bits)))

    with jax.named_scope("small"):
        bias_half = jnp.where(
            low_core,
            jnp.concatenate([projection_bias_rows[0:3, :160].reshape(480), projection_bias_rows[3:5].reshape(640)]),
            jnp.concatenate([projection_bias_rows[0:3, 160:].reshape(480), projection_bias_rows[5:7].reshape(640)]),
        )
        counted = jnp.concatenate([picture_ids[None], patch_positions], axis=0).astype(F32)
        small = jnp.concatenate([bias_half, counted.reshape(3 * 2 * part_rows)])[None]
        smalls = [lax.ppermute(small, "z", [(i, i ^ d) for i in range(4)]) for d in (1, 2, 3)]
        relative = jnp.concatenate([small] + smalls, axis=0)
        biases = relative[:, :1120]
        bias_near = biases[:2]
        bias_far = biases[2:]
        counted = relative[:, 1120:].reshape(4, 3, 2, part_rows)
        counted = jnp.where((z & 1) == 0, counted[:, :, 0], counted[:, :, 1])
        counted = jnp.concatenate([lax.dynamic_slice_in_dim(counted, k ^ z, 1, 0) for k in range(4)], axis=0)
        counted = jnp.where((z >> 1) == c, counted, swap_core(counted))
        counted = jnp.moveaxis(counted, 1, 0).reshape(3, 4 * part_rows)

    rows_x, rows_g = RowsIn(tokens_in, c, z), RowsIn(cotangent, c, z)
    with jax.named_scope("rows_x"):
        r0, r1 = rows_x.send(), rows_x.send()

    with jax.named_scope("pack"):
        keep, give_away = pack(
            after(c[None].astype(jnp.int32), rows_x.sent),
            jnp.transpose(qkv_weight, (1, 0, 2)),
            out_weight.T,
            up_projection_weight,
            jnp.transpose(down_weight, (0, 2, 1)),
            inner,
        )
        other = swap_core(give_away)
        shard = jnp.concatenate([jnp.where(low_core, keep, other), jnp.where(low_core, other, keep)], axis=0)
        shard_q, shard_u, shard_d = [shard[:, i * inner : (i + 1) * inner] for i in range(3)]

    def pair(first, second):
        return jnp.concatenate([first, second], axis=-1)

    def along(value, distance, *earlier):
        return move(value, "z", [(i, i ^ distance) for i in range(4)], *earlier)

    def gather(block, order):
        return Gather(block, order, g, count)

    def far_of(two, three):
        return jnp.where(is_mid, pair(three, two), pair(two, three))

    start = jnp.sum((counted[0] == 1).astype(jnp.int32))

    def halves_of(rows_half, *earlier):
        own = rows_half.half(*earlier)
        other = swap_core(own)
        return jnp.where(low_core, own, other), jnp.where(low_core, other, own)

    with jax.named_scope("near"):
        near_q = pair(shard_q, along(shard_q, 1))
        near_u = pair(shard_u, along(shard_u, 1))
        near_d = pair(shard_d, along(shard_d, 1, near_q))
    with jax.named_scope("far"):
        far_q = along(near_q, 2)
        far_u = along(near_u, 2)
    qa, ua, da = gather(near_q, forth), gather(near_u, back), gather(near_d, forth)
    with jax.named_scope("gx"):
        qax = qa.step()
        dax = da.step(qax)
    with jax.named_scope("gy"):
        uay = ua.step()
        qay = qa.finish(uay)
    with jax.named_scope("gx"):
        uax = ua.finish(dax)
    with jax.named_scope("rows_x"):
        source, a_one = turn_rows(start, *halves_of(rows_x, near_d), norm_vectors)
    qa.take(a_one)
    qb = gather(after(far_q, a_one), back)
    with jax.named_scope("gy"):
        qby = qb.step(qay)
    with jax.named_scope("far"):
        far_d = along(near_d, 2, qay, uax)
    with jax.named_scope("gx"):
        qbx = qb.finish(uax)
    with jax.named_scope("gy"):
        day = da.finish(qby)

    first_wa = qa.whole()
    counted = jnp.roll(counted, -start, axis=1)
    ids = counted[0, MIDDLE:]
    mask = jnp.where(ids[:, None] == ids[None, :], 0.0, -1e30).astype(F32)
    powers = jnp.arange(HEAD // 4, dtype=F32) * (2.0 / (HEAD // 2))
    inverse = jnp.power(10000.0, -powers)
    angles = jnp.concatenate([inverse[:, None] * counted[1][None], inverse[:, None] * counted[2][None]], axis=0)
    cosine, sine = jnp.cos(angles), jnp.sin(angles)
    rows = source.shape[0]

    def qkv_bias(pair):
        zero = jnp.zeros((160,), F32)
        return jnp.concatenate([pair[0, :480], zero, pair[1, :480], zero])

    mixed = dot(after(first_wa, qby), a_one, 0, 1) + qkv_bias(bias_near)[:, None]
    saved = [attend(mixed, cosine, sine, mask)]
    done = saved[0][3]
    qb.take(done)
    ub = gather(after(far_u, done), forth)
    with jax.named_scope("rows_g"):
        rows_g.send(far_u, done)
        rows_g.send(far_u, done)
    with jax.named_scope("gx"):
        ubx = ub.step(qbx)
    db = gather(after(far_d, done, qbx), back)
    with jax.named_scope("gy"):
        dby = db.step(day)
    first_wb = qb.whole()
    mixed = dot(after(first_wb, day, far_d), a_one, 0, 1) + qkv_bias(bias_far)[:, None]
    saved.append(attend(mixed, cosine, sine, mask))
    done = saved[1][3]
    ub.take(done)
    db.take(done)
    with jax.named_scope("gy"):
        uby = ub.finish(dby)
    with jax.named_scope("gx"):
        dbx = db.finish(ubx)
    with jax.named_scope("rows_g"):
        (grad_rows,) = turn_rows(start, *halves_of(rows_g, ubx, dby, done))

    def out_part(weight):
        return jnp.concatenate([weight[:, 480:640], weight[:, 1120:1280]], axis=1)

    def qkv_part(weight):
        return jnp.concatenate([weight[:, :480], weight[:, 640:1120]], axis=1)

    out_wa, out_wb = out_part(first_wa), out_part(first_wb)
    qkv_wa, qkv_wb = qkv_part(first_wa), qkv_part(first_wb)
    same = lambda total: (total,)
    (branch,) = product(
        "out_product",
        [(saved[0][3], 0, out_wa, 1), (after(saved[1][3], ubx, dby), 0, out_wb, 1)],
        [(width, BF)],
        same,
    )
    middle, a_two = by_rows(
        "norm_two",
        [source, branch, swap_core(branch), norm_vectors],
        [(width, BF), (width, BF)],
        second_norm_step,
    )

    def feed_forward(weight, bias):
        return product(
            "up_product",
            [(a_two, 1, weight, 0)],
            [(2 * inner, BF), (2 * inner, BF)],
            hidden_step,
            [bias[:, 480:].reshape(1, 2 * inner)],
        )

    def down_grads(value):
        return product("down_grads", [(grad_rows, 0, value, 0)], [(2 * inner, BF)], same)[0]

    up_wa, down_wa = ua.whole(), da.whole()
    active_a, slope_a = feed_forward(up_wa, bias_near)
    grads_d_near = down_grads(active_a)
    ub.take(grads_d_near, qkv_wa, qkv_wb)
    db.take(grads_d_near)
    up_wb, down_wb = ub.whole(), db.whole()
    active_b, slope_b = feed_forward(up_wb, bias_far)
    grads_d_far = down_grads(active_b)
    active, slopes = (active_a, active_b), (slope_a, slope_b)

    def both_halves(own):
        upper, lower = own[:d_local], own[d_local:]
        keep = jnp.where(low_core, upper, lower)
        other = swap_core(jnp.where(low_core, lower, upper).astype(BF)).astype(F32)
        return jnp.stack([jnp.where(low_core, keep, other), jnp.where(low_core, other, keep)], axis=1)

    class SumZ:
        def __init__(self, near, far, *earlier):
            self.near = pair(near[:, :inner], far[:, :inner])
            self.moved = along(pair(near[:, inner:], far[:, inner:]).astype(BF), 1, *earlier)

        def step(self, *earlier):
            self.near = self.near + (after(self.moved, *earlier) if earlier else self.moved).astype(F32)
            self.moved = along(self.near[:, inner:].astype(BF), 2)
            return self.moved

        def whole(self, *earlier):
            moved = after(self.moved, *earlier) if earlier else self.moved
            return both_halves(self.near[:, :inner] + moved.astype(F32))

    grads_d = [grads_d_near, grads_d_far]
    with jax.named_scope("sd"):
        near_d, far_d = Scatter(grads_d[0], back, g, count), Scatter(grads_d[1], forth, g, count)
        one_d = [far_d.send(day, dbx), near_d.send(day, dbx)]
    *grad_hidden, part_u, sum_a, sum_b = feed_back(
        after(grad_rows, *grads_d), (down_wa, down_wb), (up_wa, up_wb), slopes
    )
    bias_up = [sum_a, sum_b]

    def up_grads(value, *earlier):
        return product("up_grads", [(after(a_two, *earlier), 0, value, 0)], [(2 * inner, BF)], same)[0]

    part_u_other = swap_core(part_u, *one_d)
    with jax.named_scope("sd"):
        far_d.add(part_u)
        near_d.add(part_u)
        sent_d = [far_d.send(*one_d), near_d.send(*one_d)]
    grads_u_far = up_grads(grad_hidden[1], far_d.sent, near_d.sent)
    grads_u_near = up_grads(grad_hidden[0], grads_u_far)
    with jax.named_scope("sd"):
        far_d.add(grads_u_near)
        near_d.add(grads_u_near)
        line_d = SumZ(near_d.whole(), far_d.whole())
        line_d_moved = line_d.moved
    with jax.named_scope("su"):
        near_u, far_u = Scatter(grads_u_near, back, g, count), Scatter(grads_u_far, forth, g, count)
        one_u = [far_u.send(*sent_d), near_u.send(*sent_d)]
    grad_branch, *grad_atts, sums_0, sums_1, sums_2, sums_3 = second_norm_back(
        part_u,
        part_u_other,
        after(middle, grads_u_near, *sent_d),
        grad_rows,
        norm_vectors,
        (out_wa, out_wb),
    )
    sums_two = [sums_0, sums_1, sums_2, sums_3]
    feed = product_in_thirds(
        "down_product", [(active[0], 1, down_wa, 1), (after(active[1], grad_branch), 1, down_wb, 1)]
    )
    feed_other = [swap_core(v, line_d_moved) for v in feed]

    def attention_back(i, *earlier):
        dq, dk, dv = attend_back(saved[i], after(grad_atts[i], *earlier), cosine, sine, mask)
        return jnp.stack([v.reshape(2, 160, rows) for v in (dq, dk, dv)], axis=1).reshape(960, rows)

    mixed_far = attention_back(1, *feed)
    with jax.named_scope("su"):
        far_u.add(mixed_far)
        near_u.add(mixed_far)
        sent_u = [far_u.send(), near_u.send()]
    (result,) = by_rows(
        "result", [after(middle, mixed_far), feed, feed_other, norm_vectors], [(width, BF)], result_step
    )
    with jax.named_scope("rows_out"):
        block_out, out_pieces, out_sents = rows_out(result, start, c, z)
    grads_far = first_grads(a_one, after(grad_branch, *out_sents, *one_u), mixed_far, saved[1][3], inner)
    mixed_near = attention_back(0, grads_far)
    with jax.named_scope("su"):
        far_u.add(grads_far)
        near_u.add(grads_far)
        line_u = SumZ(near_u.whole(), far_u.whole())
        line_u_moved = line_u.moved
    with jax.named_scope("sd"):
        line_d.step(mixed_near)
    part = product_in_thirds(
        "qkv_back", [(after(mixed_near, *sent_u), 0, qkv_wa, 1), (mixed_far, 0, qkv_wb, 1)]
    )
    part_other = [swap_core(v, *out_pieces, line_u_moved) for v in part]
    grads_near = first_grads(a_one, after(grad_branch, *part), mixed_near, saved[0][3], inner)
    with jax.named_scope("sq"):
        near_q, far_q = Scatter(grads_near, back, g, count), Scatter(grads_far, forth, g, count)
        one_q = [far_q.send(grads_near), near_q.send(grads_near)]
    bias_qkv = [jnp.sum(v, axis=1, dtype=F32) for v in (mixed_near, mixed_far)]
    grad_source, *sums_one = by_rows(
        "norm_back",
        [part, part_other, after(source, grads_near), grad_branch, norm_vectors],
        [(width, BF), (width,), (width,)],
        first_back_step,
    )
    with jax.named_scope("su"):
        line_u.step(grad_source)
    with jax.named_scope("rows_dx"):
        input_grad, dx_pieces, _ = rows_out(after(grad_source, line_u_moved), start, c, z, True)
        input_grad = input_grad.astype(F32)
    with jax.named_scope("sq"):
        far_q.add(grad_source)
        near_q.add(grad_source)
        sent_q = [far_q.send(), near_q.send()]
        far_q.add(dx_pieces[0])
        near_q.add(dx_pieces[0])
        line_q = SumZ(near_q.whole(), far_q.whole())
        moved_q = [line_q.moved, line_q.step()]
        grad_first = line_q.whole()
    with jax.named_scope("sd"):
        grad_down = after(line_d.whole(grad_source), *one_q)
    with jax.named_scope("su"):
        grad_up = after(line_u.whole(dx_pieces[0]), *one_q)

    vector_grad = 0.5 * jnp.concatenate(sums_one + sums_two, axis=0)
    bias_up = [after(v, *sent_q) for v in bias_up]
    placed = jnp.zeros((7, 4, 320), F32)
    for index, place in enumerate((z, z ^ 1, z ^ 2, z ^ 3)):
        qkv_sum = bias_qkv[index // 2].reshape(2, 3, 1, 160)[index % 2]
        up_sum = bias_up[index // 2].reshape(2, 2, 1, 320)[index % 2]
        placed = lax.dynamic_update_slice(placed, qkv_sum, (0, place, c * 160))
        placed = lax.dynamic_update_slice(placed, up_sum, (3 + 2 * c, place, 0))
    with jax.named_scope("vectors"):
        summed = add_up(
            jnp.concatenate([placed.reshape(7, 4 * 320), vector_grad], axis=0), count, moved_q[:1], moved_q + dx_pieces[1:]
        )
    grad_bias = lax.dynamic_slice(summed, (0, z * 320), (7, 320))
    grad_vector = summed[7:]

    first_split = grad_first.reshape(d_local, 2, 4, 160)
    grad_qkv = jnp.moveaxis(first_split[:, :, :3], 1, 2).reshape(d_local, 3, 320)
    grad_o = first_split[:, :, 3].reshape(d_local, 320).T
    grad_up = grad_up.reshape(d_local, 4, 320)
    grad_down = jnp.transpose(grad_down.reshape(d_local, 4, 320), (1, 2, 0))
    outputs = [block_out, input_grad]
    for weight, grad, first, second, rate, decay in (
        (qkv_weight, grad_qkv, qkv_first, qkv_second, MATRIX_RATE, MATRIX_DECAY),
        (out_weight, grad_o, out_first, out_second, MATRIX_RATE, MATRIX_DECAY),
        (up_projection_weight, grad_up, up_first, up_second, MATRIX_RATE, MATRIX_DECAY),
        (down_weight, grad_down, down_first, down_second, MATRIX_RATE, MATRIX_DECAY),
        (projection_bias_rows, grad_bias, bias_first, bias_second, VECTOR_RATE, 0.0),
        (norm_vectors, grad_vector, vector_first, vector_second, VECTOR_RATE, 0.0),
    ):
        outputs.extend(adam_step(weight, grad, first, second, rate, decay))
    return tuple(outputs)


def solution(mesh):
    devices = mesh.devices.reshape(mesh.shape["dp"] // 2, 2, mesh.shape["tensor"])
    own_mesh = Mesh(devices, ("g", "c", "z"))
    rows = P(("g", "c"), "z", None)
    in_weights = (P(("g", "c"), None, "z"), P("z", ("g", "c")), P(("g", "c"), None, "z"), P(None, "z", ("g", "c")))
    vectors = (P(None, "z"), P())
    params = in_weights + vectors
    out_specs = [rows, rows]
    for spec in params:
        out_specs.extend([spec] * 3)
    return jax.shard_map(
        body,
        mesh=own_mesh,
        in_specs=(rows, rows, P(("g", "c"), "z"), P(None, ("g", "c"), "z")) + params * 3,
        out_specs=tuple(out_specs),
        check_vma=False,
    )
```

```python
import functools

import jax
import jax.numpy as jnp
from jax import lax
from jax.experimental import pallas as pl
from jax.experimental.pallas import tpu as pltpu
from jax.sharding import Mesh, PartitionSpec as P

HEAD = 80
HALF = HEAD // 2
STEP = 10
MIDDLE = 1024

NORM_EPS = 1e-06
BETA_ONE = 0.9
BETA_TWO = 0.95
ADAM_EPS = 1e-08
MATRIX_RATE = 0.03
VECTOR_RATE = 0.2
MATRIX_DECAY = 0.1
GELU_SLOPE = 1.702
LOG2E = 1.4426950408889634
LN2 = 0.6931471805599453

BF = jnp.bfloat16
F32 = jnp.float32


def dot(left, right, left_dim, right_dim):
    return lax.dot_general(
        left, right, (((left_dim,), (right_dim,)), ((), ())), preferred_element_type=F32
    )


def normalise(source):
    centre = source - jnp.mean(source, axis=-1, keepdims=True)
    spread = lax.rsqrt(jnp.mean(centre * centre, axis=-1, keepdims=True) + NORM_EPS)
    return centre * spread, spread


def norm_back(gradient, gain_vec, normed, spread):
    scaled = gradient * gain_vec
    return spread * (
        scaled
        - jnp.mean(scaled, axis=-1, keepdims=True)
        - normed * jnp.mean(scaled * normed, axis=-1, keepdims=True)
    )


def adam_step(weight, gradient, first, second, rate, decay):
    first_new = BETA_ONE * first + (1.0 - BETA_ONE) * gradient
    second_new = BETA_TWO * second + (1.0 - BETA_TWO) * gradient * gradient
    fix_one = 1.0 - BETA_ONE**STEP
    fix_two = 1.0 - BETA_TWO**STEP
    ratio = first_new / fix_one / (jnp.sqrt(second_new / fix_two) + ADAM_EPS)
    return (weight - rate * (ratio + decay * weight), first_new, second_new)


def after(value, *earlier):
    return lax.optimization_barrier((value, *earlier))[0]


def move(value, axis, pairs, *earlier):
    return lax.ppermute(after(value, *earlier) if earlier else value, axis, pairs)


def swap_core(value, *earlier):
    return move(value, "c", [(0, 1), (1, 0)], *earlier)


def swap_bit(value, bit, count, *earlier):
    return move(value, "g", [(i, i ^ (1 << bit)) for i in range(count)], *earlier)


class Gather:
    def __init__(self, block, order, g, count):
        self.rows, self.columns = block.shape
        self.order, self.g, self.count = list(order), g, count
        self.bits = len(self.order)
        self.current = block.reshape((1,) * self.bits + block.shape)
        self.other = None

    def take(self, *earlier):
        if self.other is None:
            return
        other = after(self.other, *earlier) if earlier else self.other
        upper = ((self.g >> self.bit) & 1) == 1
        mine = self.current
        self.current = jnp.concatenate(
            [jnp.where(upper, other, mine), jnp.where(upper, mine, other)], axis=self.bits - 1 - self.bit
        )
        self.other = None

    def step(self, *earlier):
        self.take()
        if self.order:
            self.bit = self.order.pop(0)
            self.other = swap_bit(self.current, self.bit, self.count, *earlier)
            return self.other
        return self.current

    def finish(self, *earlier):
        last = self.step(*earlier)
        while self.order:
            last = self.step()
        return last

    def whole(self):
        self.take()
        return self.current.reshape(self.count * self.rows, self.columns)


class Scatter:
    def __init__(self, full, order, g, count):
        self.rows, self.columns = full.shape[0] // count, full.shape[1]
        self.order, self.g, self.count = list(order), g, count
        self.bits = len(self.order)
        self.terms = [full.reshape((2,) * self.bits + (self.rows, self.columns))]

    def sliced(self, place, axis):
        return [lax.dynamic_slice_in_dim(v, place, 1, axis) for v in self.terms]

    def total(self, terms):
        out = terms[0].astype(F32)
        for term in terms[1:]:
            out = out + term.astype(F32)
        return out

    def send(self, *earlier):
        bit = self.order.pop(0)
        axis = self.bits - 1 - bit
        mine = (self.g >> bit) & 1
        sent = self.total(self.sliced(1 - mine, axis)).astype(BF)
        self.kept = self.sliced(mine, axis)
        self.sent = sent
        self.got = swap_bit(sent, bit, self.count, *earlier)
        return self.got

    def add(self, *earlier):
        self.terms = self.kept + [after(self.got, *earlier) if earlier else self.got]
        while len(self.order) > 1:
            self.send()
            self.terms = self.kept + [self.got]

    def whole(self):
        return self.total(self.terms).reshape(self.rows, self.columns)


def row_moves(step):
    moves = []
    for c in range(2):
        for z in range(4):
            moves.append((c * 4 + z, (z >> 1) * 4 + 2 * c + ((z & 1) ^ step)))
    return [(a, b) for a, b in moves if a != b]


class RowsIn:
    def __init__(self, local, c, z):
        self.local, self.odd, self.stays = local, (z & 1) == 1, (z >> 1) == c
        self.pieces = []

    def send(self, *earlier):
        step = len(self.pieces)
        sent = jnp.where(self.odd, self.local[1 - step], self.local[step])
        self.sent = sent
        self.first = sent if step == 0 else self.first
        self.pieces.append(move(sent, ("c", "z"), row_moves(step), *earlier))
        return self.pieces[-1]

    def half(self, *earlier):
        first, second = [after(v, *earlier) if earlier else v for v in self.pieces]
        first = jnp.where(self.stays, self.first, first)
        return jnp.concatenate(
            [jnp.where(self.odd, second, first), jnp.where(self.odd, first, second)], axis=0
        )


def rows_out(turned, start, c, z, chained=False):
    rows, width = turned.shape
    part = rows // 4
    odd = z & 1
    longer = jnp.concatenate([turned, turned[:part]], axis=0)
    pieces, sents = [], []
    for step in range(2):
        first = lax.rem((2 * c + (odd ^ step)) * part - start + rows, rows)
        sent = lax.dynamic_slice(longer, (first, 0), (part, width))
        sents.append(sent)
        back = [(b, a) for a, b in row_moves(step)]
        pieces.append(move(sent, ("c", "z"), back, *(pieces if chained else [])))
    first, second = jnp.where((z >> 1) == c, sents[0], pieces[0]), pieces[1]
    return jnp.stack([jnp.where(odd == 1, second, first), jnp.where(odd == 1, first, second)]), pieces, sents


def turn_rows(start, upper, lower, vectors=None):
    half, width = upper.shape
    rows = 2 * half
    block = 256
    more = block + 16

    def kernel(start_ref, up_ref, low_ref, *refs):
        wide = refs[-1]
        for at in range(0, half, block):
            wide[at : at + block] = up_ref[at : at + block].astype(F32)
            wide[half + at : half + at + block] = low_ref[at : at + block].astype(F32)
        wide[rows : rows + more] = up_ref[:more].astype(F32)

        @pl.loop(0, rows // block)
        def _(i):
            at = i * block
            first = lax.rem(at + start_ref[0], rows)
            low = lax.rem(first, 8)
            value = wide[pl.ds(pl.multiple_of(first - low, 8), more)]
            value = pltpu.roll(value, lax.rem(more - low, more), 0)[:block]
            into = pl.ds(pl.multiple_of(at, block), block)
            if vectors is None:
                refs[0][into] = value.astype(BF)
            else:
                refs[1][into] = value.astype(BF)
                refs[2][into] = first_norm_step(value, refs[0][...])[0].astype(BF)

    outs = 1 if vectors is None else 2
    extra = [] if vectors is None else [vectors]
    return pl.pallas_call(
        kernel,
        in_specs=[pl.BlockSpec(memory_space=pltpu.SMEM)]
        + [pl.BlockSpec(memory_space=pltpu.VMEM)] * (2 + len(extra)),
        out_specs=[pl.BlockSpec(memory_space=pltpu.VMEM)] * outs,
        out_shape=[jax.ShapeDtypeStruct((rows, width), BF)] * outs,
        scratch_shapes=[pltpu.VMEM((rows + more, width), F32)],
        compiler_params=pltpu.CompilerParams(vmem_limit_bytes=40 * 2**20),
        cost_estimate=FREE,
        name="turn_rows",
    )(start[None], upper, lower, *extra)


def add_up(value, count, first, then):
    value = value + swap_core(value, *first)
    for bit in range(count.bit_length() - 1):
        value = value + swap_bit(value, bit, count)
    value = after(value, *then)
    for distance in (1, 2):
        value = value + lax.ppermute(value, "z", [(i, i ^ distance) for i in range(4)])
    return value


SEGMENTS = ((0, MIDDLE, False), (MIDDLE, None, True))


def attend_kernel(q_ref, k_ref, v_ref, cos_ref, sin_ref, mask_ref, qt_ref, kt_ref, vt_ref, ot_ref, lse_ref, *, block):
    cosine, sine = cos_ref[...], sin_ref[...]

    def turn(source, factor):
        first, second = source[:HALF], source[HALF:]
        return (
            jnp.concatenate([first * cosine - second * sine, second * cosine + first * sine], axis=0) * factor
        ).astype(BF)

    rows = q_ref.shape[1]
    qt = turn(q_ref[...], LOG2E * HEAD ** (-0.5))
    kt = turn(k_ref[...], 1.0)
    vt = v_ref[...].astype(BF)
    qt_ref[0] = qt
    kt_ref[0] = kt
    vt_ref[0] = vt
    for first, last, masked in ((0, MIDDLE, False), (MIDDLE, rows, True)):
        keys = kt[:, first:last]
        values = vt[:, first:last]
        for at in range(first, last, block):
            scores = dot(keys, qt[:, at : at + block], 0, 0)
            if masked:
                scores = scores + mask_ref[:, at - first : at - first + block]
            largest = jnp.max(scores, axis=0, keepdims=True)
            raised = jnp.exp2(scores - largest)
            total = jnp.sum(raised, axis=0, keepdims=True)
            mixed = dot(values, raised.astype(BF), 1, 0)
            ot_ref[:, at : at + block] = (mixed / total).astype(BF)
            lse_ref[0, :, at : at + block] = largest + jnp.log2(total)


def attend_back_kernel(qt_ref, kt_ref, vt_ref, ot_ref, dot_ref, lse_ref, cos_ref, sin_ref, mask_ref, dq_ref, dk_ref, dv_ref, *, block):
    cosine, sine = cos_ref[...], sin_ref[...]

    def turn_back(grad, factor):
        first, second = grad[:HALF] * factor, grad[HALF:] * factor
        return jnp.concatenate([first * cosine + second * sine, second * cosine - first * sine], axis=0).astype(BF)

    rows = cos_ref.shape[1]
    qt, kt, vt, dot_ = qt_ref[0], kt_ref[0], vt_ref[0], dot_ref[...]
    delta = jnp.sum(dot_.astype(F32) * ot_ref[...].astype(F32), axis=0, keepdims=True)
    lse = lse_ref[0]
    queries = qt.astype(F32).T.astype(BF)
    grads = dot_.astype(F32).T.astype(BF)
    dq_parts, dk_parts, dv_parts = [], [], []
    for first, last, masked in ((0, MIDDLE, False), (MIDDLE, rows, True)):
        keys = kt[:, first:last]
        values = vt[:, first:last]
        dk = dv = None
        for at in range(first, last, block):
            sl = slice(at, at + block)
            scores = dot(keys, qt[:, sl], 0, 0)
            if masked:
                scores = scores + mask_ref[:, at - first : at - first + block]
            chances = jnp.exp2(scores - lse[:, sl])
            grad_chances = dot(values, dot_[:, sl], 0, 0)
            grad_scores = (chances * (grad_chances - delta[:, sl])).astype(BF)
            dv_part = dot(chances.astype(BF), grads[sl], 1, 0)
            dk_part = dot(grad_scores, queries[sl], 1, 0)
            dv = dv_part if dv is None else dv + dv_part
            dk = dk_part if dk is None else dk + dk_part
            dq_parts.append(dot(keys, grad_scores, 1, 0))
        dk_parts.append(dk.T)
        dv_parts.append(dv.T)
    dq_ref[0] = turn_back(jnp.concatenate(dq_parts, axis=1), HEAD ** (-0.5))
    dk_ref[0] = turn_back(jnp.concatenate(dk_parts, axis=1), LN2)
    dv_ref[0] = jnp.concatenate(dv_parts, axis=1).astype(BF)


def attend(mixed, cosine, sine, mask):
    rows = mixed.shape[1]
    heads = 4
    once = lambda shape: pl.BlockSpec(shape, lambda h: (0, 0))
    part = lambda which: pl.BlockSpec((HEAD, rows), lambda h: ((h // 2) * 8 + 2 * which + h % 2, 0))
    each = pl.BlockSpec((1, HEAD, rows), lambda h: (h, 0, 0))
    return pl.pallas_call(
        functools.partial(attend_kernel, block=256),
        grid=(heads,),
        in_specs=[part(0), part(1), part(2), once(cosine.shape), once(sine.shape), once(mask.shape)],
        out_specs=[
            each,
            each,
            each,
            pl.BlockSpec((HEAD, rows), lambda h: (h, 0)),
            pl.BlockSpec((1, 1, rows), lambda h: (h, 0, 0)),
        ],
        out_shape=[jax.ShapeDtypeStruct((heads, HEAD, rows), BF)] * 3
        + [
            jax.ShapeDtypeStruct((heads * HEAD, rows), BF),
            jax.ShapeDtypeStruct((heads, 1, rows), F32),
        ],
        compiler_params=pltpu.CompilerParams(vmem_limit_bytes=40 * 2**20),
        cost_estimate=FREE,
        name="attend",
    )(mixed, mixed, mixed, cosine, sine, mask)


def attend_back(saved, grad_mixed, cosine, sine, mask):
    qt, kt, vt, mixed, lse = saved
    heads, _, rows = qt.shape
    once = lambda shape: pl.BlockSpec(shape, lambda h: (0, 0))
    each = pl.BlockSpec((1, HEAD, rows), lambda h: (h, 0, 0))
    flat = pl.BlockSpec((HEAD, rows), lambda h: (h, 0))
    return pl.pallas_call(
        functools.partial(attend_back_kernel, block=256),
        grid=(heads,),
        in_specs=[
            each,
            each,
            each,
            flat,
            flat,
            pl.BlockSpec((1, 1, rows), lambda h: (h, 0, 0)),
            once(cosine.shape),
            once(sine.shape),
            once(mask.shape),
        ],
        out_specs=[each, each, each],
        out_shape=[jax.ShapeDtypeStruct((heads, HEAD, rows), BF)] * 3,
        compiler_params=pltpu.CompilerParams(vmem_limit_bytes=50 * 2**20),
        cost_estimate=FREE,
        name="attend_back",
    )(qt, kt, vt, mixed, grad_mixed, lse, cosine, sine, mask)


FREE = pl.CostEstimate(flops=0, bytes_accessed=0, transcendentals=0)
BLOCK = 256


def params(mib=48):
    return pltpu.CompilerParams(vmem_limit_bytes=mib * 2**20, dimension_semantics=("arbitrary",))


def whole(shape):
    return pl.BlockSpec(shape, lambda i: (0,) * len(shape))


def rows_of(width, block=BLOCK):
    return pl.BlockSpec((block, width), lambda i: (i, 0))


def columns_of(height, block=BLOCK):
    return pl.BlockSpec((height, block), lambda i: (0, i))


def product(name, pairs, outs, finish, extras=(), block=None):
    size = pairs[0][0].shape[1 - pairs[0][1]]
    block = block or (640 if size % 640 == 0 else 512 if size % 512 == 0 else BLOCK)
    in_specs, operands = [], []
    for left, left_dim, right, _ in pairs:
        in_specs.append(rows_of(left.shape[1], block) if left_dim == 1 else columns_of(left.shape[0], block))
        in_specs.append(whole(right.shape))
        operands.extend([left, right])
    for value in extras:
        in_specs.append(rows_of(value.shape[1], block) if value.shape[0] == size else whole(value.shape))
        operands.append(value)
    out_specs, out_shape = [], []
    for out in outs:
        if len(out) == 2:
            out_specs.append(rows_of(out[0], block))
            out_shape.append(jax.ShapeDtypeStruct((size, out[0]), out[1]))
        else:
            out_specs.append(whole((1, out[0])))
            out_shape.append(jax.ShapeDtypeStruct((1, out[0]), F32))

    def kernel(*refs):
        total = None
        for i, (_, left_dim, _, right_dim) in enumerate(pairs):
            term = dot(refs[2 * i][...], refs[2 * i + 1][...], left_dim, right_dim)
            total = term if total is None else total + term
        at = 2 * len(pairs)
        values = finish(total, *[r[...] for r in refs[at : at + len(extras)]])
        store(values, refs[at + len(extras) :], outs)

    return pl.pallas_call(
        kernel,
        grid=(size // block,),
        in_specs=in_specs,
        out_specs=out_specs,
        out_shape=out_shape,
        compiler_params=params(),
        cost_estimate=FREE,
        name=name,
    )(*operands)


def product_in_thirds(name, pairs):
    size = pairs[0][0].shape[1 - pairs[0][1]]
    width = pairs[0][2].shape[1 - pairs[0][3]]
    block = size // 3
    in_specs, operands = [], []
    for left, left_dim, right, _ in pairs:
        in_specs.append(rows_of(left.shape[1], block) if left_dim == 1 else columns_of(left.shape[0], block))
        in_specs.append(whole(right.shape))
        operands.extend([left, right])

    def kernel(*refs):
        total = None
        for i, (_, left_dim, _, right_dim) in enumerate(pairs):
            term = dot(refs[2 * i][...], refs[2 * i + 1][...], left_dim, right_dim)
            total = term if total is None else total + term
        value = total.astype(BF)
        for k, ref in enumerate(refs[2 * len(pairs) :]):

            @pl.when(pl.program_id(0) == k)
            def _(ref=ref):
                ref[...] = value

    return pl.pallas_call(
        kernel,
        grid=(3,),
        in_specs=in_specs,
        out_specs=[whole((block, width))] * 3,
        out_shape=[jax.ShapeDtypeStruct((block, width), BF)] * 3,
        compiler_params=params(),
        cost_estimate=FREE,
        name=name,
    )(*operands)


def store(values, refs, outs):
    for value, ref, out in zip(values, refs, outs):
        if len(out) == 2:
            ref[...] = value.astype(out[1])
        else:
            summed = jnp.sum(value, axis=0, keepdims=True)

            @pl.when(pl.program_id(0) == 0)
            def _():
                ref[...] = summed

            @pl.when(pl.program_id(0) > 0)
            def _():
                ref[...] += summed


def by_rows(name, inputs, outs, step, block=256):
    size = inputs[0].shape[0] if not isinstance(inputs[0], (list, tuple)) else 3 * inputs[0][0].shape[0]
    count = size // block
    each = count // 3
    in_specs, operands = [], []
    for value in inputs:
        if isinstance(value, (list, tuple)):
            for k, third in enumerate(value):
                operands.append(third)
                in_specs.append(
                    pl.BlockSpec(
                        (block, third.shape[1]), lambda i, k=k: (jnp.clip(i - each * k, 0, each - 1), 0)
                    )
                )
        else:
            operands.append(value)
            in_specs.append(rows_of(value.shape[1], block) if value.shape[0] == size else whole(value.shape))
    out_specs, out_shape = [], []
    for out in outs:
        if len(out) == 2:
            out_specs.append(rows_of(out[0], block))
            out_shape.append(jax.ShapeDtypeStruct((size, out[0]), out[1]))
        else:
            out_specs.append(whole((1, out[0])))
            out_shape.append(jax.ShapeDtypeStruct((1, out[0]), F32))

    def kernel(*refs):
        place = pl.program_id(0)
        values, at = [], 0
        for value in inputs:
            if isinstance(value, (list, tuple)):
                one, two, three = [r[...] for r in refs[at : at + 3]]
                values.append(jnp.where(place < each, one, jnp.where(place < 2 * each, two, three)))
                at += 3
            else:
                values.append(refs[at][...])
                at += 1
        store(step(*values), refs[at:], outs)

    return pl.pallas_call(
        kernel,
        grid=(count,),
        in_specs=in_specs,
        out_specs=out_specs,
        out_shape=out_shape,
        compiler_params=params(),
        cost_estimate=FREE,
        name=name,
    )(*operands)


def first_norm_step(source, vectors):
    hat, _ = normalise(source.astype(F32))
    return (hat * vectors[0:1] + vectors[1:2],)


def second_norm_step(source, part, other, vectors):
    middle = source.astype(F32) + (part.astype(F32) + other.astype(F32)) + vectors[4:5]
    hat, _ = normalise(middle)
    return middle, hat * vectors[2:3] + vectors[3:4]


def second_back_step(part, other, middle, grad_out, vectors):
    grad = part.astype(F32) + other.astype(F32)
    hat, scale = normalise(middle.astype(F32))
    out = grad_out.astype(F32)
    grad_middle = out + norm_back(grad, vectors[2:3], hat, scale)
    return grad_middle, grad_middle, grad * hat, grad, grad_middle, out


def first_back_step(part, other, source, grad_middle, vectors):
    grad = part.astype(F32) + other.astype(F32)
    hat, scale = normalise(source.astype(F32))
    return grad_middle.astype(F32) + norm_back(grad, vectors[0:1], hat, scale), grad * hat, grad


def result_step(middle, part, other, vectors):
    return (middle.astype(F32) + (part.astype(F32) + other.astype(F32)) + vectors[5:6],)


def hidden_step(total, bias):
    hidden = total + bias
    gate = 0.5 + 0.5 * jnp.tanh((0.5 * GELU_SLOPE) * hidden)
    return hidden * gate, gate + GELU_SLOPE * hidden * gate * (1.0 - gate)


def hidden_back_step(total, slope):
    grad = (total * slope.astype(F32)).astype(BF)
    return grad, grad.astype(F32)


def feed_back(grad_rows, down, up, slopes):
    size, width = grad_rows.shape
    hidden = slopes[0].shape[1]

    def kernel(g_ref, da_ref, db_ref, ua_ref, ub_ref, sa_ref, sb_ref, ha_ref, hb_ref, part_ref, suma_ref, sumb_ref):
        total = None
        for d_ref, u_ref, s_ref, h_ref, sum_ref in (
            (da_ref, ua_ref, sa_ref, ha_ref, suma_ref),
            (db_ref, ub_ref, sb_ref, hb_ref, sumb_ref),
        ):
            grad = (dot(g_ref[...], d_ref[...], 1, 0) * s_ref[...].astype(F32)).astype(BF)
            h_ref[...] = grad
            store((grad.astype(F32),), (sum_ref,), ((hidden,),))
            term = dot(grad, u_ref[...], 1, 1)
            total = term if total is None else total + term
        part_ref[...] = total.astype(BF)

    weight = whole((width, hidden))
    return pl.pallas_call(
        kernel,
        grid=(size // 512,),
        in_specs=[rows_of(width, 512)] + [weight] * 4 + [rows_of(hidden, 512)] * 2,
        out_specs=[rows_of(hidden, 512)] * 2 + [rows_of(width, 512)] + [whole((1, hidden))] * 2,
        out_shape=[jax.ShapeDtypeStruct((size, hidden), BF)] * 2
        + [jax.ShapeDtypeStruct((size, width), BF)]
        + [jax.ShapeDtypeStruct((1, hidden), F32)] * 2,
        compiler_params=params(60),
        cost_estimate=FREE,
        name="feed_back",
    )(grad_rows, *down, *up, *slopes)


def second_norm_back(part, other, middle, grad_rows, vectors, outs):
    size, width = part.shape
    inner = outs[0].shape[1]

    def kernel(p_ref, o_ref, m_ref, g_ref, v_ref, wa_ref, wb_ref, branch_ref, da_ref, db_ref, *sums):
        _, grad_middle, *terms = second_back_step(p_ref[...], o_ref[...], m_ref[...], g_ref[...], v_ref[...])
        branch = grad_middle.astype(BF)
        branch_ref[...] = branch
        for w_ref, d_ref in ((wa_ref, da_ref), (wb_ref, db_ref)):
            d_ref[...] = dot(w_ref[...], branch, 0, 1).astype(BF)
        store(terms, sums, ((width,),) * 4)

    return pl.pallas_call(
        kernel,
        grid=(size // BLOCK,),
        in_specs=[rows_of(width)] * 4 + [whole(vectors.shape)] + [whole((width, inner))] * 2,
        out_specs=[rows_of(width)] + [columns_of(inner)] * 2 + [whole((1, width))] * 4,
        out_shape=[jax.ShapeDtypeStruct((size, width), BF)]
        + [jax.ShapeDtypeStruct((inner, size), BF)] * 2
        + [jax.ShapeDtypeStruct((1, width), F32)] * 4,
        compiler_params=params(),
        cost_estimate=FREE,
        name="norm_two_back",
    )(part, other, middle, grad_rows, vectors, *outs)


def first_grads(a_one, grad_branch, grad_mixed, mixed, inner):
    rows, width = a_one.shape

    def kernel(a_ref, g_ref, m_ref, o_ref, out_ref):
        for slot in range(2):
            at = slot * inner
            out_ref[:, at : at + 480] = dot(a_ref[...], m_ref[slot * 480 : (slot + 1) * 480], 0, 1).astype(BF)
            out_ref[:, at + 480 : at + 640] = dot(g_ref[...], o_ref[slot * 160 : (slot + 1) * 160], 0, 1).astype(BF)

    return pl.pallas_call(
        kernel,
        grid=(width // BLOCK,),
        in_specs=[columns_of(rows), columns_of(rows), whole(grad_mixed.shape), whole(mixed.shape)],
        out_specs=rows_of(2 * inner),
        out_shape=jax.ShapeDtypeStruct((width, 2 * inner), BF),
        compiler_params=params(),
        cost_estimate=FREE,
        name="first_grads",
    )(a_one, grad_branch, grad_mixed, mixed)


def pack(core, qkv, out, up, down, inner):
    rows = out.shape[0]

    def kernel(core_ref, qkv_ref, out_ref, up_ref, down_ref, keep_ref, give_ref):
        for ref, mine in ((keep_ref, core_ref[0]), (give_ref, 1 - core_ref[0])):
            low = mine == 0
            for i in range(3):
                value = qkv_ref[i]
                ref[:, i * 160 : (i + 1) * 160] = jnp.where(low, value[:, :160], value[:, 160:]).astype(BF)
            value = out_ref[...]
            ref[:, 480:640] = jnp.where(low, value[:, :160], value[:, 160:]).astype(BF)
            for j in range(2):
                ref[:, inner + j * 320 : inner + (j + 1) * 320] = jnp.where(
                    low, up_ref[:, j], up_ref[:, j + 2]
                ).astype(BF)
                ref[:, 2 * inner + j * 320 : 2 * inner + (j + 1) * 320] = jnp.where(
                    low, down_ref[j], down_ref[j + 2]
                ).astype(BF)

    return pl.pallas_call(
        kernel,
        in_specs=[pl.BlockSpec(memory_space=pltpu.SMEM)] + [pl.BlockSpec(memory_space=pltpu.VMEM)] * 4,
        out_specs=[pl.BlockSpec(memory_space=pltpu.VMEM)] * 2,
        out_shape=[jax.ShapeDtypeStruct((rows, 3 * inner), BF)] * 2,
        compiler_params=pltpu.CompilerParams(vmem_limit_bytes=40 * 2**20),
        cost_estimate=FREE,
        name="pack",
    )(core, qkv, out, up, down)


def body(
    tokens_in,
    cotangent,
    picture_ids,
    patch_positions,
    qkv_weight,
    out_weight,
    up_projection_weight,
    down_weight,
    projection_bias_rows,
    norm_vectors,
    qkv_first,
    out_first,
    up_first,
    down_first,
    bias_first,
    vector_first,
    qkv_second,
    out_second,
    up_second,
    down_second,
    bias_second,
    vector_second,
):
    count = lax.axis_size("g")
    bits = count.bit_length() - 1
    g, c, z = lax.axis_index("g"), lax.axis_index("c"), lax.axis_index("z")
    low_core = c == 0
    d_local = qkv_weight.shape[0]
    width = tokens_in.shape[2]
    part_rows = tokens_in.shape[1]
    inner = 640
    forth, back = tuple(range(bits)), tuple(reversed(range(bits)))

    with jax.named_scope("small"):
        bias_half = jnp.where(
            low_core,
            jnp.concatenate([projection_bias_rows[0:3, :160].reshape(480), projection_bias_rows[3:5].reshape(640)]),
            jnp.concatenate([projection_bias_rows[0:3, 160:].reshape(480), projection_bias_rows[5:7].reshape(640)]),
        )
        counted = jnp.concatenate([picture_ids[None], patch_positions], axis=0).astype(F32)
        small = jnp.concatenate([bias_half, counted.reshape(3 * 2 * part_rows)])[None]
        smalls = [lax.ppermute(small, "z", [(i, i ^ d) for i in range(4)]) for d in (1, 2, 3)]
        relative = jnp.concatenate([small] + smalls, axis=0)
        biases = relative[:, :1120]
        bias_near = biases[:2]
        bias_far = biases[2:]
        counted = relative[:, 1120:].reshape(4, 3, 2, part_rows)
        counted = jnp.where((z & 1) == 0, counted[:, :, 0], counted[:, :, 1])
        counted = jnp.concatenate([lax.dynamic_slice_in_dim(counted, k ^ z, 1, 0) for k in range(4)], axis=0)
        counted = jnp.where((z >> 1) == c, counted, swap_core(counted))
        counted = jnp.moveaxis(counted, 1, 0).reshape(3, 4 * part_rows)

    rows_x, rows_g = RowsIn(tokens_in, c, z), RowsIn(cotangent, c, z)
    with jax.named_scope("rows_x"):
        r0, r1 = rows_x.send(), rows_x.send()

    with jax.named_scope("pack"):
        keep, give_away = pack(
            after(c[None].astype(jnp.int32), rows_x.sent),
            jnp.transpose(qkv_weight, (1, 0, 2)),
            out_weight.T,
            up_projection_weight,
            jnp.transpose(down_weight, (0, 2, 1)),
            inner,
        )
        other = swap_core(give_away)
        shard = jnp.concatenate([jnp.where(low_core, keep, other), jnp.where(low_core, other, keep)], axis=0)
        shard_q, shard_u, shard_d = [shard[:, i * inner : (i + 1) * inner] for i in range(3)]

    def pair(first, second):
        return jnp.concatenate([first, second], axis=-1)

    def along(value, distance, *earlier):
        return move(value, "z", [(i, i ^ distance) for i in range(4)], *earlier)

    def gather(block, order):
        return Gather(block, order, g, count)

    def far_of(two, three):
        return jnp.where(is_mid, pair(three, two), pair(two, three))

    start = jnp.sum((counted[0] == 1).astype(jnp.int32))

    def halves_of(rows_half, *earlier):
        own = rows_half.half(*earlier)
        other = swap_core(own)
        return jnp.where(low_core, own, other), jnp.where(low_core, other, own)

    with jax.named_scope("near"):
        near_q = pair(shard_q, along(shard_q, 1))
        near_u = pair(shard_u, along(shard_u, 1))
        near_d = pair(shard_d, along(shard_d, 1, near_q))
    with jax.named_scope("far"):
        far_q = along(near_q, 2)
        far_u = along(near_u, 2)
    qa, ua, da = gather(near_q, forth), gather(near_u, back), gather(near_d, forth)
    with jax.named_scope("gx"):
        qax = qa.step()
        dax = da.step(qax)
    with jax.named_scope("gy"):
        uay = ua.step()
        qay = qa.finish(uay)
    with jax.named_scope("gx"):
        uax = ua.finish(dax)
    with jax.named_scope("rows_x"):
        source, a_one = turn_rows(start, *halves_of(rows_x, near_d), norm_vectors)
    qa.take(a_one)
    qb = gather(after(far_q, a_one), back)
    with jax.named_scope("gy"):
        qby = qb.step(qay)
    with jax.named_scope("far"):
        far_d = along(near_d, 2, qay, uax)
    with jax.named_scope("gx"):
        qbx = qb.finish(uax)
    with jax.named_scope("gy"):
        day = da.finish(qby)

    first_wa = qa.whole()
    counted = jnp.roll(counted, -start, axis=1)
    ids = counted[0, MIDDLE:]
    mask = jnp.where(ids[:, None] == ids[None, :], 0.0, -1e30).astype(F32)
    powers = jnp.arange(HEAD // 4, dtype=F32) * (2.0 / (HEAD // 2))
    inverse = jnp.power(10000.0, -powers)
    angles = jnp.concatenate([inverse[:, None] * counted[1][None], inverse[:, None] * counted[2][None]], axis=0)
    cosine, sine = jnp.cos(angles), jnp.sin(angles)
    rows = source.shape[0]

    def qkv_bias(pair):
        zero = jnp.zeros((160,), F32)
        return jnp.concatenate([pair[0, :480], zero, pair[1, :480], zero])

    mixed = dot(after(first_wa, qby), a_one, 0, 1) + qkv_bias(bias_near)[:, None]
    saved = [attend(mixed, cosine, sine, mask)]
    done = saved[0][3]
    qb.take(done)
    ub = gather(after(far_u, done), forth)
    with jax.named_scope("rows_g"):
        rows_g.send(far_u, done)
        rows_g.send(far_u, done)
    with jax.named_scope("gx"):
        ubx = ub.step(qbx)
    db = gather(after(far_d, done, qbx), back)
    with jax.named_scope("gy"):
        dby = db.step(day)
    first_wb = qb.whole()
    mixed = dot(after(first_wb, day, far_d), a_one, 0, 1) + qkv_bias(bias_far)[:, None]
    saved.append(attend(mixed, cosine, sine, mask))
    done = saved[1][3]
    ub.take(done)
    db.take(done)
    with jax.named_scope("gy"):
        uby = ub.finish(dby)
    with jax.named_scope("gx"):
        dbx = db.finish(ubx)
    with jax.named_scope("rows_g"):
        (grad_rows,) = turn_rows(start, *halves_of(rows_g, ubx, dby, done))

    def out_part(weight):
        return jnp.concatenate([weight[:, 480:640], weight[:, 1120:1280]], axis=1)

    def qkv_part(weight):
        return jnp.concatenate([weight[:, :480], weight[:, 640:1120]], axis=1)

    out_wa, out_wb = out_part(first_wa), out_part(first_wb)
    qkv_wa, qkv_wb = qkv_part(first_wa), qkv_part(first_wb)
    same = lambda total: (total,)
    (branch,) = product(
        "out_product",
        [(saved[0][3], 0, out_wa, 1), (after(saved[1][3], ubx, dby), 0, out_wb, 1)],
        [(width, BF)],
        same,
    )
    middle, a_two = by_rows(
        "norm_two",
        [source, branch, swap_core(branch), norm_vectors],
        [(width, BF), (width, BF)],
        second_norm_step,
    )

    def feed_forward(weight, bias):
        return product(
            "up_product",
            [(a_two, 1, weight, 0)],
            [(2 * inner, BF), (2 * inner, BF)],
            hidden_step,
            [bias[:, 480:].reshape(1, 2 * inner)],
        )

    def down_grads(value):
        return product("down_grads", [(grad_rows, 0, value, 0)], [(2 * inner, BF)], same)[0]

    up_wa, down_wa = ua.whole(), da.whole()
    active_a, slope_a = feed_forward(up_wa, bias_near)
    grads_d_near = down_grads(active_a)
    ub.take(grads_d_near, qkv_wa, qkv_wb)
    db.take(grads_d_near)
    up_wb, down_wb = ub.whole(), db.whole()
    active_b, slope_b = feed_forward(up_wb, bias_far)
    grads_d_far = down_grads(active_b)
    active, slopes = (active_a, active_b), (slope_a, slope_b)

    def both_halves(own):
        upper, lower = own[:d_local], own[d_local:]
        keep = jnp.where(low_core, upper, lower)
        other = swap_core(jnp.where(low_core, lower, upper).astype(BF)).astype(F32)
        return jnp.stack([jnp.where(low_core, keep, other), jnp.where(low_core, other, keep)], axis=1)

    class SumZ:
        def __init__(self, near, far, *earlier):
            self.near = pair(near[:, :inner], far[:, :inner])
            self.moved = along(pair(near[:, inner:], far[:, inner:]).astype(BF), 1, *earlier)

        def step(self, *earlier):
            self.near = self.near + (after(self.moved, *earlier) if earlier else self.moved).astype(F32)
            self.moved = along(self.near[:, inner:].astype(BF), 2)
            return self.moved

        def whole(self, *earlier):
            moved = after(self.moved, *earlier) if earlier else self.moved
            return both_halves(self.near[:, :inner] + moved.astype(F32))

    grads_d = [grads_d_near, grads_d_far]
    with jax.named_scope("sd"):
        near_d, far_d = Scatter(grads_d[0], back, g, count), Scatter(grads_d[1], forth, g, count)
        one_d = [far_d.send(day, dbx), near_d.send(day, dbx)]
    *grad_hidden, part_u, sum_a, sum_b = feed_back(
        after(grad_rows, *grads_d), (down_wa, down_wb), (up_wa, up_wb), slopes
    )
    bias_up = [sum_a, sum_b]

    def up_grads(value, *earlier):
        return product("up_grads", [(after(a_two, *earlier), 0, value, 0)], [(2 * inner, BF)], same)[0]

    part_u_other = swap_core(part_u, *one_d)
    with jax.named_scope("sd"):
        far_d.add(part_u)
        near_d.add(part_u)
        sent_d = [far_d.send(*one_d), near_d.send(*one_d)]
    grads_u_far = up_grads(grad_hidden[1], far_d.sent, near_d.sent)
    grads_u_near = up_grads(grad_hidden[0], grads_u_far)
    with jax.named_scope("sd"):
        far_d.add(grads_u_near)
        near_d.add(grads_u_near)
        line_d = SumZ(near_d.whole(), far_d.whole())
        line_d_moved = line_d.moved
    with jax.named_scope("su"):
        near_u, far_u = Scatter(grads_u_near, back, g, count), Scatter(grads_u_far, forth, g, count)
        one_u = [far_u.send(*sent_d), near_u.send(*sent_d)]
    grad_branch, *grad_atts, sums_0, sums_1, sums_2, sums_3 = second_norm_back(
        part_u,
        part_u_other,
        after(middle, grads_u_near, *sent_d),
        grad_rows,
        norm_vectors,
        (out_wa, out_wb),
    )
    sums_two = [sums_0, sums_1, sums_2, sums_3]
    feed = product_in_thirds(
        "down_product", [(active[0], 1, down_wa, 1), (after(active[1], grad_branch), 1, down_wb, 1)]
    )
    feed_other = [swap_core(v, line_d_moved) for v in feed]

    def attention_back(i, *earlier):
        dq, dk, dv = attend_back(saved[i], after(grad_atts[i], *earlier), cosine, sine, mask)
        return jnp.stack([v.reshape(2, 160, rows) for v in (dq, dk, dv)], axis=1).reshape(960, rows)

    mixed_far = attention_back(1, *feed)
    with jax.named_scope("su"):
        far_u.add(mixed_far)
        near_u.add(mixed_far)
        sent_u = [far_u.send(), near_u.send()]
    (result,) = by_rows(
        "result", [after(middle, mixed_far), feed, feed_other, norm_vectors], [(width, BF)], result_step
    )
    with jax.named_scope("rows_out"):
        block_out, out_pieces, out_sents = rows_out(result, start, c, z)
    grads_far = first_grads(a_one, after(grad_branch, *out_sents, *one_u), mixed_far, saved[1][3], inner)
    mixed_near = attention_back(0, grads_far)
    with jax.named_scope("su"):
        far_u.add(grads_far)
        near_u.add(grads_far)
        line_u = SumZ(near_u.whole(), far_u.whole())
        line_u_moved = line_u.moved
    with jax.named_scope("sd"):
        line_d.step(mixed_near)
    part = product_in_thirds(
        "qkv_back", [(after(mixed_near, *sent_u), 0, qkv_wa, 1), (mixed_far, 0, qkv_wb, 1)]
    )
    part_other = [swap_core(v, *out_pieces, line_u_moved) for v in part]
    grads_near = first_grads(a_one, after(grad_branch, *part), mixed_near, saved[0][3], inner)
    with jax.named_scope("sq"):
        near_q, far_q = Scatter(grads_near, back, g, count), Scatter(grads_far, forth, g, count)
        one_q = [far_q.send(grads_near), near_q.send(grads_near)]
    bias_qkv = [jnp.sum(v, axis=1, dtype=F32) for v in (mixed_near, mixed_far)]
    grad_source, *sums_one = by_rows(
        "norm_back",
        [part, part_other, after(source, grads_near), grad_branch, norm_vectors],
        [(width, BF), (width,), (width,)],
        first_back_step,
    )
    with jax.named_scope("su"):
        line_u.step(grad_source)
    with jax.named_scope("rows_dx"):
        input_grad, dx_pieces, _ = rows_out(after(grad_source, line_u_moved), start, c, z, True)
        input_grad = input_grad.astype(F32)
    with jax.named_scope("sq"):
        far_q.add(grad_source)
        near_q.add(grad_source)
        sent_q = [far_q.send(), near_q.send()]
        far_q.add(dx_pieces[0])
        near_q.add(dx_pieces[0])
        line_q = SumZ(near_q.whole(), far_q.whole())
        moved_q = [line_q.moved, line_q.step()]
        grad_first = line_q.whole()
    with jax.named_scope("sd"):
        grad_down = after(line_d.whole(grad_source), *one_q)
    with jax.named_scope("su"):
        grad_up = after(line_u.whole(dx_pieces[0]), *one_q)

    vector_grad = 0.5 * jnp.concatenate(sums_one + sums_two, axis=0)
    bias_up = [after(v, *sent_q) for v in bias_up]
    placed = jnp.zeros((7, 4, 320), F32)
    for index, place in enumerate((z, z ^ 1, z ^ 2, z ^ 3)):
        qkv_sum = bias_qkv[index // 2].reshape(2, 3, 1, 160)[index % 2]
        up_sum = bias_up[index // 2].reshape(2, 2, 1, 320)[index % 2]
        placed = lax.dynamic_update_slice(placed, qkv_sum, (0, place, c * 160))
        placed = lax.dynamic_update_slice(placed, up_sum, (3 + 2 * c, place, 0))
    with jax.named_scope("vectors"):
        summed = add_up(
            jnp.concatenate([placed.reshape(7, 4 * 320), vector_grad], axis=0), count, moved_q[:1], moved_q + dx_pieces[1:]
        )
    grad_bias = lax.dynamic_slice(summed, (0, z * 320), (7, 320))
    grad_vector = summed[7:]

    first_split = grad_first.reshape(d_local, 2, 4, 160)
    grad_qkv = jnp.moveaxis(first_split[:, :, :3], 1, 2).reshape(d_local, 3, 320)
    grad_o = first_split[:, :, 3].reshape(d_local, 320).T
    grad_up = grad_up.reshape(d_local, 4, 320)
    grad_down = jnp.transpose(grad_down.reshape(d_local, 4, 320), (1, 2, 0))
    outputs = [block_out, input_grad]
    for weight, grad, first, second, rate, decay in (
        (qkv_weight, grad_qkv, qkv_first, qkv_second, MATRIX_RATE, MATRIX_DECAY),
        (out_weight, grad_o, out_first, out_second, MATRIX_RATE, MATRIX_DECAY),
        (up_projection_weight, grad_up, up_first, up_second, MATRIX_RATE, MATRIX_DECAY),
        (down_weight, grad_down, down_first, down_second, MATRIX_RATE, MATRIX_DECAY),
        (projection_bias_rows, grad_bias, bias_first, bias_second, VECTOR_RATE, 0.0),
        (norm_vectors, grad_vector, vector_first, vector_second, VECTOR_RATE, 0.0),
    ):
        outputs.extend(adam_step(weight, grad, first, second, rate, decay))
    return tuple(outputs)


def solution(mesh):
    devices = mesh.devices.reshape(mesh.shape["dp"] // 2, 2, mesh.shape["tensor"])
    own_mesh = Mesh(devices, ("g", "c", "z"))
    rows = P(("g", "c"), "z", None)
    in_weights = (P(("g", "c"), None, "z"), P("z", ("g", "c")), P(("g", "c"), None, "z"), P(None, "z", ("g", "c")))
    vectors = (P(None, "z"), P())
    params = in_weights + vectors
    out_specs = [rows, rows]
    for spec in params:
        out_specs.extend([spec] * 3)
    return jax.shard_map(
        body,
        mesh=own_mesh,
        in_specs=(rows, rows, P(("g", "c"), "z"), P(None, ("g", "c"), "z")) + params * 3,
        out_specs=tuple(out_specs),
        check_vma=False,
    )
```
